32 devices in a mesh: grp: 2 (over x), req: 16 (over z, y, core).
Axes of the slice: x: 2, y: 2, z: 4, core: 2. Of those that a mesh axis runs over, the one named last changes fastest.
Arguments:
- xbc: bfloat16 [4096, 9216], P(('grp', 'req')), parts along dimension 0, may hold values from -6 to 6
- dt_raw: float32 [4096, 128], P(('grp', 'req')), parts along dimension 0, may hold values from -6 to 6
- conv_weight: float32 [4, 9216], replicated, may hold values from -3 to 3
- conv_bias: float32 [9216], replicated, may hold values from -3 to 3
- dt_bias: float32 [128], replicated, may hold values from -1 to 1
- a_log: float32 [128], replicated, may hold values from -6 to -2.5
- d_skip: float32 [128], replicated, may hold values from 0.5 to 1.5
- cache_states: bfloat16 [96, 128, 8192], P(('grp', 'req')), parts along dimension 0, may hold values from -24 to 24
- cache_tails: bfloat16 [96, 3, 9216], P(('grp', 'req')), parts along dimension 0, may hold values from -6 to 6
- hit_owner: int32 [32], P('grp'), parts along dimension 0, may hold values from 0 to 15, as said below
- hit_slot: int32 [32], P('grp'), parts along dimension 0, may hold values from 0 to 2, as said below
- hit_spans: int32 [32], P('grp'), parts along dimension 0, may hold values from 0 to 4
- request_of: int32 [32], P(('grp', 'req')), parts along dimension 0, may hold values from 0 to 15, each once
Outputs:
- y_out: bfloat16 [4096, 8192], P(('grp', 'req')), parts along dimension 0
- final_state: bfloat16 [32, 128, 8192], P(('grp', 'req')), parts along dimension 0
The draws below stay inside these ranges and needn't reach their ends.
There are 2 independent parts, one for each index of `grp`. The reference program is written for one: setup_inputs(seed, part) draws one part's arguments, and reference() takes and returns one part's arrays. A program takes and returns all parts, laid end to end along the dimension named above; an argument that names none is the same for every part. Nothing has to cross between parts.
Inputs may be any that keep to these rules, and one draw needn't show every extreme that they name: `hit_owner`: owners are skewed: some devices hold the prefixes of several requests, others of none. `hit_slot`: all requests that name the same owner device name the same slot of it. `request_of`: each request stands on exactly one device.
All inputs are finite; a program needn't handle non-finite values.
Results may differ from the reference program's by a relative error of at most 0.0039.
Values may be sent and summed in bfloat16 or wider, within the bound.
A program may use at most 128 MiB of HBM per device.

```python
import jax
import jax.numpy as jnp
from jax import lax

HEADS = 128
HEAD_DIM = 64
GROUPS = 4
NST = 128
CONV_WIDTH = 4
SPAN = 128
SLOTS = 3
INNER = 8192
CONV_CH = 9216
REQUESTS = 16
ROWS = 2048
SLOTS_ALL = 48


def draw_hits(key):
    base = jax.random.fold_in(key, 17)
    first, second, third, fourth = jax.random.split(base, 4)
    left = jax.random.randint(first, (REQUESTS,), 0, REQUESTS)
    right = jax.random.randint(second, (REQUESTS,), 0, REQUESTS)
    skewed = left * right // REQUESTS
    order = jax.random.permutation(third, REQUESTS)
    owners = order[skewed]
    owners = owners.at[0].set(REQUESTS - 1)
    owners = owners.at[1].set(0)
    served = jax.random.randint(fourth, (REQUESTS,), 0, SLOTS)
    served = served.at[REQUESTS - 1].set(SLOTS - 1)
    served = served.at[0].set(0)
    slots = served[owners]
    return (owners.astype(jnp.int32), slots.astype(jnp.int32))


def draw_hit_owner(key, part):
    return draw_hits(key)[0]


def draw_hit_slot(key, part):
    return draw_hits(key)[1]


def plant(result, rng, smallest, largest):
    longest = result.shape.index(max(result.shape))
    spots = []
    for shift in (0, 1):
        where = [jax.random.randint(jax.random.fold_in(rng, axis), (), 0, length) for axis, length in enumerate(result.shape)]
        where[longest] = (where[longest] + shift) % result.shape[longest]
        spots.append(tuple(where))
    return result.at[spots[0]].set(smallest).at[spots[1]].set(largest)


def level_of(stream_key, shape, cuts, least, high):
    factor_of = 1.0
    for dim, shards_of in cuts:
        steps = jax.random.uniform(jax.random.fold_in(jax.random.fold_in(stream_key, 6), dim), (shards_of,), jnp.float32, least / len(cuts), high / len(cuts))
        factor_of = factor_of * jnp.repeat(jnp.exp(steps), shape[dim] // shards_of).reshape((-1,) + (1,) * (len(shape) - 1 - dim))
    return factor_of


def centred(stream_key, extent, scale, limit, cuts=(), dtype=jnp.bfloat16):
    loudness = level_of(stream_key, extent, cuts, -0.22, 0.18) if cuts else 1.0
    drawn = jax.random.normal(stream_key, extent, jnp.float32) * scale * loudness
    return jnp.minimum(jnp.maximum(drawn, -limit), limit).astype(dtype)


def setup_inputs(seed: int = 0, part: int = 0) -> dict:
    key_of = jax.random.split(jax.random.key(seed), 14)
    part_splits = jax.random.split(jax.random.fold_in(key_of[13], part), 14)
    xbc = centred(part_splits[0], (ROWS, CONV_CH), 1.0, 6.0, ((0, 16),))
    dt_raw = centred(part_splits[1], (ROWS, HEADS), 1.5, 6.0, ((0, 16),), jnp.float32)
    conv_weight = centred(key_of[2], (CONV_WIDTH, CONV_CH), CONV_WIDTH ** -0.5, 3.0, (), jnp.float32)
    conv_bias = centred(key_of[3], (CONV_CH,), 0.5, 3.0, (), jnp.float32)
    dt_bias = jnp.clip(jax.random.uniform(key_of[4], (HEADS,), jnp.float32, -1.0, 1.0), -1.0, 1.0)
    a_log = jnp.clip(jax.random.uniform(key_of[5], (HEADS,), jnp.float32, -6.0, -2.5), -6.0, -2.5)
    d_skip = jnp.clip(jax.random.uniform(key_of[6], (HEADS,), jnp.float32, 0.5, 1.5), 0.5, 1.5)
    cache_states = centred(part_splits[7], (SLOTS_ALL, NST, INNER), 4.0, 24.0, ((0, 16),))
    cache_tails = centred(part_splits[8], (SLOTS_ALL, CONV_WIDTH - 1, CONV_CH), 1.0, 6.0, ((0, 16),))
    hit_owner = draw_hit_owner(jax.random.fold_in(jax.random.fold_in(key_of[13], part), 71), part)
    hit_slot = draw_hit_slot(jax.random.fold_in(jax.random.fold_in(key_of[13], part), 71), part)
    hit_spans = plant(jax.random.randint(part_splits[11], (REQUESTS,), 0, 5), jax.random.fold_in(part_splits[11], 1), 0, 4).astype(jnp.int32)
    request_of = jax.random.permutation(part_splits[12], REQUESTS).astype(jnp.int32)
    return {"xbc": xbc, "dt_raw": dt_raw, "conv_weight": conv_weight, "conv_bias": conv_bias, "dt_bias": dt_bias, "a_log": a_log, "d_skip": d_skip, "cache_states": cache_states, "cache_tails": cache_tails, "hit_owner": hit_owner, "hit_slot": hit_slot, "hit_spans": hit_spans, "request_of": request_of}


def scan_request(xrows, dt_rows, tail, start, conv_weight, conv_bias, dt_bias, a_log, d_skip):
    rows = xrows.shape[0]
    taps = conv_weight.shape[0]
    per_group = HEADS // GROUPS
    extended = jnp.concatenate([tail, xrows], axis=0).astype(jnp.float32)
    conv = jnp.zeros((rows, xrows.shape[1]), jnp.float32) + conv_bias[None, :]
    for k in range(taps):
        conv = conv + conv_weight[k][None, :] * extended[k:k + rows]
    conv_out = jax.nn.silu(conv).astype(jnp.bfloat16)
    inputs = conv_out[:, :INNER].reshape(rows, GROUPS, per_group, HEAD_DIM).astype(jnp.float32)
    b_part = conv_out[:, INNER:INNER + GROUPS * NST].reshape(rows, GROUPS, NST).astype(jnp.float32)
    c_part = conv_out[:, INNER + GROUPS * NST:].reshape(rows, GROUPS, NST).astype(jnp.float32)
    step = jax.nn.softplus(dt_rows + dt_bias[None, :])
    cum = jnp.cumsum(step * (-jnp.exp(a_log))[None, :], axis=0)
    scores = jnp.einsum('tgn,sgn->gts', c_part, b_part)
    diff = cum.T[:, :, None] - cum.T[:, None, :]
    causal = lax.broadcasted_iota(jnp.int32, (rows, rows), 0) >= lax.broadcasted_iota(jnp.int32, (rows, rows), 1)
    decay = jnp.where(causal[None], jnp.exp(jnp.minimum(diff, 0.0)), 0.0)
    mixing = (scores[:, None] * decay.reshape(GROUPS, per_group, rows, rows)
              * step.T.reshape(GROUPS, per_group, 1, rows)).astype(jnp.bfloat16)
    y_intra = jnp.einsum('gjts,sgjp->tgjp', mixing.astype(jnp.float32), inputs)
    start_f = start.reshape(NST, GROUPS, per_group, HEAD_DIM).astype(jnp.float32)
    y_state = jnp.einsum('tgn,ngjp->tgjp', c_part, start_f) * jnp.exp(cum).reshape(rows, GROUPS, per_group, 1)
    skip = d_skip.reshape(1, GROUPS, per_group, 1) * inputs
    y_out = (y_intra + y_state + skip).reshape(rows, INNER).astype(jnp.bfloat16)
    last = cum[rows - 1]
    carried = ((jnp.exp(last[None, :] - cum) * step).reshape(rows, GROUPS, per_group, 1) * inputs).astype(jnp.bfloat16)
    fresh = jnp.einsum('sgn,sgjp->ngjp', b_part, carried.astype(jnp.float32))
    kept = jnp.exp(last).reshape(1, GROUPS, per_group, 1) * start_f
    final = (kept + fresh).reshape(NST, INNER).astype(jnp.bfloat16)
    return y_out, final


def reference(xbc, dt_raw, conv_weight, conv_bias, dt_bias, a_log, d_skip, cache_states, cache_tails, hit_owner, hit_slot, hit_spans, request_of):
    def one_request(item):
        xrows, dt_rows, request = item
        row = (hit_owner[request] * SLOTS + hit_slot[request]).astype(jnp.int32)
        live = hit_spans[request] > 0
        tail_row = lax.dynamic_index_in_dim(cache_tails, row, 0, keepdims=False)
        state_row = lax.dynamic_index_in_dim(cache_states, row, 0, keepdims=False)
        tail = jnp.where(live, tail_row, jnp.zeros_like(tail_row))
        start = jnp.where(live, state_row, jnp.zeros_like(state_row))
        return scan_request(xrows, dt_rows, tail, start, conv_weight, conv_bias, dt_bias, a_log, d_skip)

    outputs, finals = lax.map(one_request, (xbc.reshape(REQUESTS, SPAN, CONV_CH),
                                           dt_raw.reshape(REQUESTS, SPAN, HEADS), request_of))
    return outputs.reshape(ROWS, INNER), finals
```

```python
import functools

import jax
import jax.numpy as jnp
from jax import lax
from jax.experimental import pallas as pl
from jax.experimental.pallas import tpu as pltpu
from jax.sharding import PartitionSpec as P

HEADS = 128
HEAD_DIM = 64
GROUPS = 4
NST = 128
INNER = 8192
PER_STEP = 16
COLS = PER_STEP * HEAD_DIM
STEPS = HEADS // PER_STEP
STEPS_PER_GROUP = STEPS // GROUPS


def pick_kernel(index_ref, parts_ref, out_ref, sem):
    count = out_ref.shape[0]
    copies = []
    for i in range(count):
        copy = pltpu.make_async_copy(parts_ref.at[index_ref[i], :, pl.ds(0, INNER)], out_ref.at[i], sem.at[i])
        copy.start()
        copies.append(copy)
    for copy in copies:
        copy.wait()


def pick(parts, index):
    count = index.shape[0]
    return pl.pallas_call(
        pick_kernel,
        out_shape=jax.ShapeDtypeStruct((count, parts.shape[1], INNER), parts.dtype),
        in_specs=[pl.BlockSpec(memory_space=pltpu.SMEM), pl.BlockSpec(memory_space=pltpu.VMEM)],
        out_specs=pl.BlockSpec(memory_space=pl.ANY),
        scratch_shapes=[pltpu.SemaphoreType.DMA((count,))],
        compiler_params=pltpu.CompilerParams(vmem_limit_bytes=8 * 2**20),
        name="pick",
    )(index, parts)


def conv_block(pad, x_ref, tail_ref, w_ref, b_ref, width):
    rows = x_ref.shape[0]
    pad[0:8, 0:width] = tail_ref[...]
    pad[8 : 8 + rows, 0:width] = x_ref[...].astype(jnp.float32)
    v = jnp.broadcast_to(b_ref[...], (rows, width))
    for k in range(4):
        v = v + w_ref[k : k + 1, :] * pad[5 + k : 5 + k + rows, 0:width]
    return (v / (1.0 + jnp.exp(-v))).astype(jnp.bfloat16)


def local_kernel(
    x_ref, xb_ref, xc_ref, tx_ref, tb_ref, tc_ref, wx_ref, wb_ref, wc_ref, bx_ref, bb_ref, bc_ref,
    cum_ref, cumt_ref, stept_ref, coef_ref, skip_ref,
    y_ref, fresh_ref, c_out_ref, pad,
):
    rows = x_ref.shape[0]
    b_part = conv_block(pad, xb_ref, tb_ref, wb_ref, bb_ref, NST)
    c_part = conv_block(pad, xc_ref, tc_ref, wc_ref, bc_ref, NST)
    c_out_ref[...] = c_part
    x = conv_block(pad, x_ref, tx_ref, wx_ref, bx_ref, COLS)
    scores = lax.dot_general(c_part, b_part, (((1,), (1,)), ((), ())), preferred_element_type=jnp.float32)
    causal = lax.broadcasted_iota(jnp.int32, (rows, rows), 0) >= lax.broadcasted_iota(jnp.int32, (rows, rows), 1)
    scores = jnp.where(causal, scores, 0.0)
    low = lax.broadcasted_iota(jnp.int32, (rows, 128), 1) < HEAD_DIM
    cum = cum_ref[0]
    coef = coef_ref[0]
    zero = jnp.zeros((rows, 128), jnp.bfloat16)
    carried = []
    for j in range(0, PER_STEP, 2):
        xp = x[:, j * HEAD_DIM : (j + 2) * HEAD_DIM]
        mixes = []
        for h in (j, j + 1):
            decay = jnp.exp(jnp.minimum(cum[:, h : h + 1] - cumt_ref[0, h : h + 1, :], 0.0))
            mixes.append((scores * decay * stept_ref[0, h : h + 1, :]).astype(jnp.bfloat16))
        mix = jnp.concatenate(mixes, axis=1)
        both = jnp.concatenate([jnp.where(low, xp, zero), jnp.where(low, zero, xp)], axis=0)
        xf = xp.astype(jnp.float32)
        sl = slice(j * HEAD_DIM, (j + 2) * HEAD_DIM)
        y_ref[:, sl] = jnp.dot(mix, both, preferred_element_type=jnp.float32) + skip_ref[:, sl] * xf
        carried.append((jnp.where(low, coef[:, j : j + 1], coef[:, j + 1 : j + 2]) * xf).astype(jnp.bfloat16))
    fresh_ref[...] = lax.dot_general(
        b_part, jnp.concatenate(carried, axis=1), (((0,), (0,)), ((), ())), preferred_element_type=jnp.float32
    )


def state_kernel(start_ref, y_ref, fresh_ref, c_ref, ecum_ref, elast_ref, y_out_ref, final_ref):
    rows = y_ref.shape[0]
    low = lax.broadcasted_iota(jnp.int32, (rows, 128), 1) < HEAD_DIM
    ecum = ecum_ref[0]
    for half in range(COLS // CC):
        start = start_ref[0, half]
        here = slice(half * CC, (half + 1) * CC)
        ys = jnp.dot(c_ref[...], start, preferred_element_type=jnp.float32)
        for j in range(half * CC // HEAD_DIM, (half + 1) * CC // HEAD_DIM, 2):
            sl = slice(j * HEAD_DIM, (j + 2) * HEAD_DIM)
            factor = jnp.where(low, ecum[:, j : j + 1], ecum[:, j + 1 : j + 2])
            inner = slice(j * HEAD_DIM - half * CC, (j + 2) * HEAD_DIM - half * CC)
            y_out_ref[:, sl] = (y_ref[:, sl] + factor * ys[:, inner]).astype(jnp.bfloat16)
        final_ref[0, :, here] = (
            elast_ref[:, here] * start.astype(jnp.float32) + fresh_ref[:, here]
        ).astype(jnp.bfloat16)


def by_step(a):
    return a.reshape(a.shape[0], STEPS, PER_STEP).transpose(1, 0, 2)


LANES = 4
CHUNKS = 4
WIDE = INNER // LANES
CC = WIDE // CHUNKS
TAIL_ROWS = 16
LAG = 2
MESH = pl.DeviceIdType.MESH


def masked_column(row, rows):
    sub = lax.broadcasted_iota(jnp.int32, (rows, 128), 0)
    lane = lax.broadcasted_iota(jnp.int32, (rows, 128), 1)
    return jnp.sum(jnp.where(sub == lane, jnp.broadcast_to(row, (rows, 128)), 0), axis=1, keepdims=True)


def destinations(wanted, n):
    planes = n // LANES
    sub = lax.broadcasted_iota(jnp.int32, (n, 128), 0) // LANES
    lane = lax.broadcasted_iota(jnp.int32, (n, 128), 1)
    hit = wanted == lane
    top = jnp.max(jnp.where(hit, sub, -1), axis=0, keepdims=True)
    low = jnp.min(jnp.where(hit, sub, planes), axis=0, keepdims=True)
    return top, low


def info_kernel(groups, n, owner_ref, slot_ref, spans_ref, request_ref, table_ref, mine, rows, send_sem, recv_sem):
    planes = n // LANES
    grp, me = lax.axis_index("grp"), lax.axis_index("req")
    total = groups * n
    flat = grp * n + me
    barrier = pltpu.get_barrier_semaphore()

    def other(k):
        to = lax.rem(flat + k, total)
        return lax.div(to, n), lax.rem(to, n)

    for k in range(1, total):
        pl.semaphore_signal(barrier, inc=1, device_id=other(k), device_id_type=MESH)
    request = request_ref[0]
    wanted = jnp.where(spans_ref[request] > 0, owner_ref[request], -1)
    served = jnp.int32(0)
    for r in range(n):
        served = jnp.maximum(served, jnp.where(owner_ref[r] == me, slot_ref[r], 0))
    mine[...] = jnp.full((1, 128), wanted, jnp.int32)
    pl.semaphore_wait(barrier, total - 1)
    copies = []
    for k in range(1, total):
        to_grp, to_req = other(k)
        row = lax.rem(grp - to_grp + groups, groups) * n + me
        copy = pltpu.make_async_remote_copy(
            src_ref=mine, dst_ref=rows.at[row], send_sem=send_sem.at[k], recv_sem=recv_sem.at[k],
            device_id=(to_grp, to_req), device_id_type=MESH,
        )
        copy.start()
        copies.append(copy)
    rows[pl.ds(me, 1)] = mine[...].reshape(1, 1, 128)
    for copy in copies:
        copy.wait()

    need = jnp.zeros((1, 1), jnp.int32)
    lane_row = lax.broadcasted_iota(jnp.int32, (1, 128), 1)
    home = lane_row // LANES
    for g in range(groups):
        top, low = destinations(rows[g * n : (g + 1) * n].reshape(n, 128), n)
        for cut in range(planes - 1):
            up = jnp.sum(((home <= cut) & (top > cut) & (lane_row < n)).astype(jnp.int32), axis=1, keepdims=True)
            down = jnp.sum(((home > cut) & (low <= cut) & (lane_row < n)).astype(jnp.int32), axis=1, keepdims=True)
            need = jnp.maximum(need, jnp.maximum(up, down))

    z = me // LANES
    wants = rows[0:n].reshape(n, 128)
    top, low = destinations(wants, n)
    sub = lax.broadcasted_iota(jnp.int32, (n, 128), 0)
    lane = lax.broadcasted_iota(jnp.int32, (n, 128), 1)
    wants_row = jnp.sum(jnp.where(sub == lane, wants, 0), axis=0, keepdims=True)
    col = lax.broadcasted_iota(jnp.int32, (n, 1), 0)
    col_home = col // LANES
    top_col, low_col = masked_column(top, n), masked_column(low, n)

    def up_set(where_home, where_top, cut):
        return (where_home <= cut) & (where_top > cut)

    def down_set(where_home, where_low, cut):
        return (where_home > cut) & (where_low <= cut)

    def rank(inside, key_row, key_col):
        ahead = inside & (key_row < key_col) & (lane_row < n)
        return jnp.sum(ahead.astype(jnp.int32), axis=1, keepdims=True)

    up_row, up_col = (planes - top) * n + lane_row, (planes - top_col) * n + col
    down_row, down_col = (low + 1) * n + lane_row, (low_col + 1) * n + col
    up_in = rank(up_set(home, top, z - 1), up_row, up_col)
    up_out = rank(up_set(home, top, z), up_row, up_col)
    down_in = rank(down_set(home, low, z), down_row, down_col)
    down_out = rank(down_set(home, low, z - 1), down_row, down_col)
    near = lax.rem(col, LANES)
    src_up = jnp.where(col_home == z, near, LANES + up_in)
    src_down = jnp.where(col_home == z, near, LANES + down_in)
    src_fin = jnp.where(col_home == z, near, jnp.where(col_home < z, LANES + up_in, LANES + n + down_in))
    sel_up = jnp.sum(jnp.where(up_set(col_home, top_col, z) & (up_out == lane), src_up, 0), axis=0, keepdims=True)
    sel_down = jnp.sum(jnp.where(down_set(col_home, low_col, z - 1) & (down_out == lane), src_down, 0), axis=0, keepdims=True)
    sel_fin = jnp.sum(jnp.where(wants_row == col, src_fin, 0), axis=0, keepdims=True)
    sel_fin = jnp.where(wants_row < 0, -1, sel_fin)
    table_ref[...] = jnp.zeros_like(table_ref)
    table_ref[0:1, :] = sel_up
    table_ref[1:2, :] = sel_down
    table_ref[2:3, :] = sel_fin
    table_ref[3:4, :] = jnp.broadcast_to(need, (1, 128))
    table_ref[4:5, :] = jnp.full((1, 128), served, jnp.int32)


def info(mesh, hit_owner, hit_slot, hit_spans, request_of):
    groups, n = mesh.shape["grp"], mesh.shape["req"]
    smem = pl.BlockSpec(memory_space=pltpu.SMEM)
    return pl.pallas_call(
        functools.partial(info_kernel, groups, n),
        out_shape=jax.ShapeDtypeStruct((8, 128), jnp.int32),
        in_specs=[smem] * 4,
        out_specs=pl.BlockSpec(memory_space=pltpu.VMEM),
        scratch_shapes=[
            pltpu.VMEM((1, 128), jnp.int32),
            pltpu.VMEM((groups * n, 1, 128), jnp.int32),
            pltpu.SemaphoreType.DMA((groups * n,)),
            pltpu.SemaphoreType.DMA((groups * n,)),
        ],
        compiler_params=pltpu.CompilerParams(collective_id=0, has_side_effects=True, vmem_limit_bytes=8 * 2**20),
        name="info",
    )(hit_owner, hit_slot, hit_spans, request_of)


def route_kernel(
    n, slots, tab, states_ref, tails_ref, start, tail_out,
    three, own, own_tail, packed, plane, plane_t, up_recv, up_recv_t, down_recv, down_recv_t,
    up_send, up_send_t, down_send, down_send_t, fin_send, fin_send_t,
    load_sem, spread_s, spread_r, spread_ts, spread_tr, up_s, up_r, up_ts, up_tr,
    down_s, down_r, down_ts, down_tr, fin_s, fin_r, fin_ts, fin_tr,
):
    planes = n // LANES
    steps = CHUNKS * slots
    grp, me = lax.axis_index("grp"), lax.axis_index("req")
    z, l = lax.div(me, LANES), lax.rem(me, LANES)
    first, last = z == 0, z == planes - 1

    def mate(k):
        return z * LANES + lax.rem(l + k, LANES)

    loads = []
    for i in range(states_ref.shape[0]):
        load = pltpu.make_async_copy(states_ref.at[i], three.at[i], load_sem.at[i])
        load.start()
        loads.append(load)
    barrier = pltpu.get_barrier_semaphore()
    for k in range(1, LANES):
        pl.semaphore_signal(barrier, inc=1, device_id=(grp, mate(k)), device_id_type=MESH)

    @pl.when(jnp.logical_not(first))
    def _():
        pl.semaphore_signal(barrier, inc=1, device_id=(grp, me - LANES), device_id_type=MESH)

    @pl.when(jnp.logical_not(last))
    def _():
        pl.semaphore_signal(barrier, inc=1, device_id=(grp, me + LANES), device_id_type=MESH)

    served = tab[4, 0]
    tail = tails_ref[served].astype(jnp.float32)
    packed[...] = jnp.zeros_like(packed)
    for q in range(-(-tail.shape[1] // WIDE)):
        for p in range(LANES):
            at = q * WIDE + p * CC
            if at < tail.shape[1]:
                packed[p, 3 * q : 3 * q + 3, :] = tail[:, at : at + CC]
    own_tail[...] = packed[...].astype(jnp.bfloat16)
    for load in loads:
        load.wait()

    def take(c):
        for p in range(LANES):
            own[p, c] = three[served, :, p * WIDE + c * CC : p * WIDE + (c + 1) * CC]

    for c in range(CHUNKS):
        take(c)
    for c in range(CHUNKS):
        plane[c, pl.ds(l, 1)] = own[pl.ds(l, 1), c]
    plane_t[pl.ds(l, 1)] = own_tail[pl.ds(l, 1)]

    pl.semaphore_wait(barrier, LANES - 1 + jnp.where(first | last, 1, 2))

    def remote(src, dst, ss, rs, to):
        return pltpu.make_async_remote_copy(
            src_ref=src, dst_ref=dst, send_sem=ss, recv_sem=rs, device_id=(grp, to), device_id_type=MESH
        )

    def spread(c, k):
        to = lax.rem(l + k, LANES)
        return remote(own.at[to, c], plane.at[c, l], spread_s.at[c, k - 1], spread_r.at[c, k - 1], mate(k))

    def spread_tail(k):
        to = lax.rem(l + k, LANES)
        return remote(own_tail.at[to], plane_t.at[l], spread_ts.at[k - 1], spread_tr.at[k - 1], mate(k))

    def spread_from(c, k):
        frm = lax.rem(l + LANES - k, LANES)
        return remote(own.at[frm, c], plane.at[c, frm], spread_s.at[c, k - 1], spread_r.at[c, k - 1], mate(k))

    def spread_tail_from(k):
        frm = lax.rem(l + LANES - k, LANES)
        return remote(own_tail.at[frm], plane_t.at[frm], spread_ts.at[k - 1], spread_tr.at[k - 1], mate(k))

    def up(s):
        return remote(up_send.at[s], up_recv.at[s], up_s.at[s], up_r.at[s], me + LANES)

    def up_tail(s):
        return remote(up_send_t.at[s], up_recv_t.at[s], up_ts.at[s], up_tr.at[s], me + LANES)

    def down(s):
        return remote(down_send.at[s], down_recv.at[s], down_s.at[s], down_r.at[s], me - LANES)

    def down_tail(s):
        return remote(down_send_t.at[s], down_recv_t.at[s], down_ts.at[s], down_tr.at[s], me - LANES)

    def fin(c, k):
        to = lax.rem(l + k, LANES)
        return remote(fin_send.at[c, k - 1], start.at[l, c], fin_s.at[c, k - 1], fin_r.at[c, k - 1], mate(k))

    def fin_from(c, k):
        frm = lax.rem(l + LANES - k, LANES)
        return remote(fin_send.at[c, k - 1], start.at[frm, c], fin_s.at[c, k - 1], fin_r.at[c, k - 1], mate(k))

    def fin_tail(k):
        return remote(fin_send_t.at[k - 1], tail_out.at[l], fin_ts.at[k - 1], fin_tr.at[k - 1], mate(k))

    def fin_tail_from(k):
        frm = lax.rem(l + LANES - k, LANES)
        return remote(fin_send_t.at[k - 1], tail_out.at[frm], fin_ts.at[k - 1], fin_tr.at[k - 1], mate(k))

    for k in range(1, LANES):
        spread_tail(k).start()
    for c in range(min(2, CHUNKS)):
        for k in range(1, LANES):
            spread(c, k).start()

    def fill(dst, at, sel, near, c, far, base, j, inner):
        value = near[c, 0]
        for p in range(1, LANES):
            value = lax.select_n(sel == p, value, near[c, p])
        dst[at] = value

        @pl.when(inner)
        def _():
            def one(i, _):
                dst[at] = lax.select_n(sel == LANES + i, dst[at], far[base + i])
                return 0

            lax.fori_loop(0, j + 1, one, 0)

    def fill_tail(dst, j, sel, far, inner):
        value = plane_t[0]
        for p in range(1, LANES):
            value = lax.select_n(sel == p, value, plane_t[p])
        dst[j] = value

        @pl.when(inner)
        def _():
            def one(i, _):
                dst[j] = lax.select_n(sel == LANES + i, dst[j], far[i])
                return 0

            lax.fori_loop(0, j + 1, one, 0)

    def tick(t, _):
        tp = t - LAG * jnp.minimum(z, planes - 1 - z)

        @pl.when((tp >= 0) & (tp < steps) & (lax.rem(jnp.maximum(tp, 0), slots) == 0))
        def _():
            c = lax.div(tp, slots)

            @pl.when(c == 0)
            def _():
                for k in range(1, LANES):
                    spread_tail_from(k).wait_recv()

            for k in range(1, LANES):
                spread_from(c, k).wait_recv()

            @pl.when(c + 2 < CHUNKS)
            def _():
                for k in range(1, LANES):
                    spread(c + 2, k).start()

        def along(s, row, edge_in, edge_out, copy, copy_tail, send, send_t, recv, recv_t):
            @pl.when((s >= 0) & (s < steps))
            def _():
                c, j = lax.div(s, slots), lax.rem(s, slots)
                inner = jnp.logical_not(edge_in)

                @pl.when(inner)
                def _():
                    @pl.when(c == 0)
                    def _():
                        copy_tail(j).wait_recv()

                    copy(s).wait_recv()

                @pl.when(jnp.logical_not(edge_out))
                def _():
                    sel = tab[row, j]

                    @pl.when(c == 0)
                    def _():
                        fill_tail(send_t, j, sel, recv_t, inner)
                        copy_tail(j).start()

                    fill(send, s, sel, plane, c, recv, c * slots, j, inner)

                    @pl.when(s >= 2)
                    def _():
                        copy(s - 2).wait_send()

                    copy(s).start()

        along(t - LAG * z, 0, first, last, up, up_tail, up_send, up_send_t, up_recv, up_recv_t)
        along(t - LAG * (planes - 1 - z), 1, last, first, down, down_tail, down_send, down_send_t, down_recv, down_recv_t)

        tf = t - LAG * jnp.maximum(z, planes - 1 - z)

        @pl.when((tf >= 0) & (tf < steps) & (lax.rem(jnp.maximum(tf, 0), slots) == slots - 1))
        def _():
            c = lax.div(tf, slots)
            sels = [tab[2, mate(k)] for k in range(LANES)]

            def choose(near, far_up, far_down, write, read):
                acc = [jnp.zeros(near(0).shape, jnp.bfloat16)] * LANES
                for p in range(LANES):
                    value = near(p)
                    acc = [lax.select_n(sel == p, a, value) for sel, a in zip(sels, acc)]
                for k in range(LANES):
                    write(k, acc[k])

                def far(get, base):
                    acc = [read(k) for k in range(LANES)]
                    for i in range(slots):
                        value = get(i)
                        acc = [lax.select_n(sel == base + i, a, value) for sel, a in zip(sels, acc)]
                    for k in range(LANES):
                        write(k, acc[k])

                @pl.when(jnp.logical_not(first))
                def _():
                    far(far_up, LANES)

                @pl.when(jnp.logical_not(last))
                def _():
                    far(far_down, LANES + n)

            def rows_of(b, _):
                at = pl.ds(pl.multiple_of(b * 16, 16), 16)

                def write(k, v):
                    if k == 0:
                        start[l, c, at] = v
                    else:
                        fin_send[c, k - 1, at] = v

                def read(k):
                    return start[l, c, at] if k == 0 else fin_send[c, k - 1, at]

                choose(lambda p: plane[c, p, at], lambda i: up_recv[c * slots + i, at],
                       lambda i: down_recv[c * slots + i, at], write, read)
                return 0

            lax.fori_loop(0, NST // 16, rows_of, 0)
            for k in range(1, LANES):
                fin(c, k).start()

            @pl.when(c == 0)
            def _():
                def write(k, v):
                    if k == 0:
                        tail_out[l] = v
                    else:
                        fin_send_t[k - 1] = v

                def read(k):
                    return tail_out[l] if k == 0 else fin_send_t[k - 1]

                choose(lambda p: plane_t[p], lambda i: up_recv_t[i], lambda i: down_recv_t[i], write, read)
                for k in range(1, LANES):
                    fin_tail(k).start()

        return 0

    lax.fori_loop(0, steps + LAG * (planes - 1), tick, 0)

    for k in range(1, LANES):
        spread_tail(k).wait_send()
        fin_tail(k).wait_send()
        fin_tail_from(k).wait_recv()
        for c in range(CHUNKS):
            spread(c, k).wait_send()
            fin(c, k).wait_send()
            fin_from(c, k).wait_recv()

    @pl.when(jnp.logical_not(last))
    def _():
        for j in range(slots):
            up_tail(j).wait_send()
        for s in range(max(steps - 2, 0), steps):
            up(s).wait_send()

    @pl.when(jnp.logical_not(first))
    def _():
        for j in range(slots):
            down_tail(j).wait_send()
        for s in range(max(steps - 2, 0), steps):
            down(s).wait_send()


def route(n, slots, number, table, cache_states, cache_tails):
    steps = CHUNKS * slots
    big = lambda *lead: pltpu.VMEM(lead + (NST, CC), jnp.bfloat16)
    small = lambda *lead: pltpu.VMEM(lead + (TAIL_ROWS, CC), jnp.bfloat16)
    sem = lambda *shape: [pltpu.SemaphoreType.DMA(shape)] * 2
    vmem = pl.BlockSpec(memory_space=pltpu.VMEM)
    return pl.pallas_call(
        functools.partial(route_kernel, n, slots),
        out_shape=(
            jax.ShapeDtypeStruct((LANES, CHUNKS, NST, CC), jnp.bfloat16),
            jax.ShapeDtypeStruct((LANES, TAIL_ROWS, CC), jnp.bfloat16),
        ),
        in_specs=[pl.BlockSpec(memory_space=pltpu.SMEM), pl.BlockSpec(memory_space=pl.ANY), vmem],
        out_specs=(vmem, vmem),
        scratch_shapes=[
            pltpu.VMEM(cache_states.shape, jnp.bfloat16),
            big(LANES, CHUNKS), small(LANES), pltpu.VMEM((LANES, TAIL_ROWS, CC), jnp.float32),
            big(CHUNKS, LANES), small(LANES),
            big(steps), small(slots), big(steps), small(slots),
            big(steps), small(slots), big(steps), small(slots),
            big(CHUNKS, LANES - 1), small(LANES - 1),
            pltpu.SemaphoreType.DMA((cache_states.shape[0],)),
            *sem(CHUNKS, LANES - 1), *sem(LANES - 1),
            *sem(steps), *sem(slots), *sem(steps), *sem(slots),
            *sem(CHUNKS, LANES - 1), *sem(LANES - 1),
        ],
        compiler_params=pltpu.CompilerParams(
            collective_id=number, has_side_effects=True, vmem_limit_bytes=48 * 2**20
        ),
        name=f"route{slots}",
    )(table, cache_states, cache_tails)


def fetch(mesh, cache_states, cache_tails, hit_owner, hit_slot, hit_spans, request_of):
    n = mesh.shape["req"]
    table = info(mesh, hit_owner, hit_slot, hit_spans, request_of)
    need = table[3, 0]
    sizes = [3, 4, n // 2]
    which = sum((need > size).astype(jnp.int32) for size in sizes[:-1])
    start, tail = lax.switch(
        which,
        [functools.partial(route, n, size, 1 + i) for i, size in enumerate(sizes)],
        table, cache_states, cache_tails,
    )
    tail = tail.transpose(1, 0, 2).reshape(TAIL_ROWS, WIDE)[:15].reshape(5, 3, WIDE)
    tail = tail.transpose(1, 0, 2).reshape(3, 5 * WIDE)[:, : cache_tails.shape[2]]
    return start, tail


def fetch_any(cache_states, cache_tails, hit_owner, hit_slot, hit_spans, request_of):
    count = hit_owner.shape[0]
    mine = request_of[0]
    live = (hit_spans[mine] > 0).astype(jnp.int32)
    device = lax.axis_index("req")
    served = jnp.max(jnp.where(hit_owner == device, hit_slot, 0))
    send = lax.dynamic_slice_in_dim(cache_states, served, 1, 0).reshape(count, NST // count, INNER)
    number = jnp.broadcast_to(mine.astype(send.dtype), send.shape[:2] + (128,))
    parts = lax.all_to_all(
        jnp.concatenate([send, number], axis=2), "req", split_axis=0, concat_axis=0, tiled=True
    )
    every_request = parts[:, 0, INNER].astype(jnp.int32)
    own_tail = lax.dynamic_slice_in_dim(cache_tails, served, 1, 0)
    own_tail = jnp.pad(own_tail, ((0, 0), (0, 1), (0, 0)))
    every_tail = lax.all_gather(own_tail, "req", axis=0, tiled=True)[:, :3]
    owners = jnp.sum(
        jnp.where(every_request[:, None] == jnp.arange(count)[None, :], hit_owner[None, :], 0), axis=1
    )
    chosen = pick(parts, owners)
    start = lax.all_to_all(chosen, "req", split_axis=0, concat_axis=0, tiled=True).reshape(NST, INNER)
    start = jnp.where(live > 0, start, jnp.zeros_like(start))
    start = start.reshape(NST, LANES, CHUNKS, CC).transpose(1, 2, 0, 3)
    tail = lax.dynamic_index_in_dim(every_tail, hit_owner[mine], 0, keepdims=False)
    return start, jnp.where(live > 0, tail, jnp.zeros_like(tail))


def local(
    mesh, xbc, dt_raw, conv_weight, conv_bias, dt_bias, a_log, d_skip, cache_states, cache_tails,
    hit_owner, hit_slot, hit_spans, request_of,
):
    rows = xbc.shape[0]
    if mesh.shape["req"] == 16:
        start, tail = fetch(mesh, cache_states, cache_tails, hit_owner, hit_slot, hit_spans, request_of)
    else:
        start, tail = fetch_any(cache_states, cache_tails, hit_owner, hit_slot, hit_spans, request_of)
    tail = jnp.pad(tail.astype(jnp.float32), ((5, 0), (0, 0)))
    step = jax.nn.softplus(dt_raw + dt_bias[None, :])
    below = jnp.tril(jnp.ones((rows, rows), jnp.float32))
    cum = jnp.dot(below, step * (-jnp.exp(a_log))[None, :], precision=lax.Precision.HIGHEST)
    last = cum[rows - 1]
    coef = jnp.exp(last[None, :] - cum) * step
    skip = jnp.repeat(d_skip, HEAD_DIM)[None, :]
    elast = jnp.repeat(jnp.exp(last), HEAD_DIM)[None, :]
    cumt = cum.T.reshape(STEPS, PER_STEP, rows)
    stept = step.T.reshape(STEPS, PER_STEP, rows)
    bias = conv_bias[None, :]

    first_b, first_c = INNER // NST, INNER // NST + GROUPS
    per = STEPS_PER_GROUP
    triple = lambda r: [
        pl.BlockSpec((r, COLS), lambda i: (0, i)),
        pl.BlockSpec((r, NST), lambda i: (0, first_b + i // per)),
        pl.BlockSpec((r, NST), lambda i: (0, first_c + i // per)),
    ]
    wide = lambda r: pl.BlockSpec((r, COLS), lambda i: (0, i))
    tall = pl.BlockSpec((1, rows, PER_STEP), lambda i: (i, 0, 0))
    flat = pl.BlockSpec((1, PER_STEP, rows), lambda i: (i, 0, 0))
    group = pl.BlockSpec((rows, NST), lambda i: (0, i // per))
    y_local, fresh, c_part = pl.pallas_call(
        local_kernel,
        grid=(STEPS,),
        out_shape=(
            jax.ShapeDtypeStruct((rows, INNER), jnp.float32),
            jax.ShapeDtypeStruct((NST, INNER), jnp.float32),
            jax.ShapeDtypeStruct((rows, GROUPS * NST), jnp.bfloat16),
        ),
        in_specs=triple(rows) + triple(8) + triple(4) + triple(1) + [tall, flat, flat, tall, wide(1)],
        out_specs=(wide(rows), wide(NST), group),
        scratch_shapes=[pltpu.VMEM((8 + rows, COLS), jnp.float32)],
        compiler_params=pltpu.CompilerParams(vmem_limit_bytes=58 * 2**20),
        cost_estimate=pl.CostEstimate(flops=10**9, bytes_accessed=40 * 10**6, transcendentals=4 * 10**6),
        name="local",
    )(xbc, xbc, xbc, tail, tail, tail, conv_weight, conv_weight, conv_weight, bias, bias, bias,
      by_step(cum), cumt, stept, by_step(coef), skip)

    return pl.pallas_call(
        state_kernel,
        grid=(STEPS,),
        out_shape=(
            jax.ShapeDtypeStruct((rows, INNER), jnp.bfloat16),
            jax.ShapeDtypeStruct((1, NST, INNER), jnp.bfloat16),
        ),
        in_specs=[
            pl.BlockSpec((1, COLS // CC, NST, CC), lambda i: (i // 2, i % 2, 0, 0)),
            wide(rows), wide(NST), group, tall, wide(1),
        ],
        out_specs=(wide(rows), pl.BlockSpec((1, NST, COLS), lambda i: (0, 0, i))),
        compiler_params=pltpu.CompilerParams(vmem_limit_bytes=58 * 2**20),
        name="state",
    )(start, y_local, fresh, c_part, by_step(jnp.exp(cum)), elast)


def solution(mesh):
    rows = P(("grp", "req"), None)
    slots = P(("grp", "req"), None, None)
    in_specs = (
        rows, rows, P(), P(), P(), P(), P(), slots, slots, P("grp"), P("grp"), P("grp"), P(("grp", "req")),
    )
    return jax.shard_map(functools.partial(local, mesh), mesh=mesh, in_specs=in_specs, out_specs=(rows, slots), check_vma=False)
```

```python
import functools

import jax
import jax.numpy as jnp
from jax import lax
from jax.experimental import pallas as pl
from jax.experimental.pallas import tpu as pltpu
from jax.sharding import PartitionSpec as P

HEADS = 128
HEAD_DIM = 64
GROUPS = 4
NST = 128
INNER = 8192
PER_STEP = 16
COLS = PER_STEP * HEAD_DIM
STEPS = HEADS // PER_STEP
STEPS_PER_GROUP = STEPS // GROUPS


def pick_kernel(index_ref, parts_ref, out_ref, sem):
    count = out_ref.shape[0]
    copies = []
    for i in range(count):
        copy = pltpu.make_async_copy(parts_ref.at[index_ref[i], :, pl.ds(0, INNER)], out_ref.at[i], sem.at[i])
        copy.start()
        copies.append(copy)
    for copy in copies:
        copy.wait()


def pick(parts, index):
    count = index.shape[0]
    return pl.pallas_call(
        pick_kernel,
        out_shape=jax.ShapeDtypeStruct((count, parts.shape[1], INNER), parts.dtype),
        in_specs=[pl.BlockSpec(memory_space=pltpu.SMEM), pl.BlockSpec(memory_space=pltpu.VMEM)],
        out_specs=pl.BlockSpec(memory_space=pl.ANY),
        scratch_shapes=[pltpu.SemaphoreType.DMA((count,))],
        compiler_params=pltpu.CompilerParams(vmem_limit_bytes=8 * 2**20),
        name="pick",
    )(index, parts)


def conv_block(pad, x_ref, tail_ref, w_ref, b_ref, width):
    rows = x_ref.shape[0]
    pad[0:8, 0:width] = tail_ref[...]
    pad[8 : 8 + rows, 0:width] = x_ref[...].astype(jnp.float32)
    v = jnp.broadcast_to(b_ref[...], (rows, width))
    for k in range(4):
        v = v + w_ref[k : k + 1, :] * pad[5 + k : 5 + k + rows, 0:width]
    return (v / (1.0 + jnp.exp(-v))).astype(jnp.bfloat16)


def local_kernel(
    x_ref, xb_ref, xc_ref, tx_ref, tb_ref, tc_ref, wx_ref, wb_ref, wc_ref, bx_ref, bb_ref, bc_ref,
    cum_ref, cumt_ref, stept_ref, coef_ref, skip_ref,
    y_ref, fresh_ref, c_out_ref, pad,
):
    rows = x_ref.shape[0]
    b_part = conv_block(pad, xb_ref, tb_ref, wb_ref, bb_ref, NST)
    c_part = conv_block(pad, xc_ref, tc_ref, wc_ref, bc_ref, NST)
    c_out_ref[...] = c_part
    x = conv_block(pad, x_ref, tx_ref, wx_ref, bx_ref, COLS)
    scores = lax.dot_general(c_part, b_part, (((1,), (1,)), ((), ())), preferred_element_type=jnp.float32)
    causal = lax.broadcasted_iota(jnp.int32, (rows, rows), 0) >= lax.broadcasted_iota(jnp.int32, (rows, rows), 1)
    scores = jnp.where(causal, scores, 0.0)
    low = lax.broadcasted_iota(jnp.int32, (rows, 128), 1) < HEAD_DIM
    cum = cum_ref[0]
    coef = coef_ref[0]
    zero = jnp.zeros((rows, 128), jnp.bfloat16)
    carried = []
    for j in range(0, PER_STEP, 2):
        xp = x[:, j * HEAD_DIM : (j + 2) * HEAD_DIM]
        mixes = []
        for h in (j, j + 1):
            decay = jnp.exp(jnp.minimum(cum[:, h : h + 1] - cumt_ref[0, h : h + 1, :], 0.0))
            mixes.append((scores * decay * stept_ref[0, h : h + 1, :]).astype(jnp.bfloat16))
        mix = jnp.concatenate(mixes, axis=1)
        both = jnp.concatenate([jnp.where(low, xp, zero), jnp.where(low, zero, xp)], axis=0)
        xf = xp.astype(jnp.float32)
        sl = slice(j * HEAD_DIM, (j + 2) * HEAD_DIM)
        y_ref[:, sl] = jnp.dot(mix, both, preferred_element_type=jnp.float32) + skip_ref[:, sl] * xf
        carried.append((jnp.where(low, coef[:, j : j + 1], coef[:, j + 1 : j + 2]) * xf).astype(jnp.bfloat16))
    fresh_ref[...] = lax.dot_general(
        b_part, jnp.concatenate(carried, axis=1), (((0,), (0,)), ((), ())), preferred_element_type=jnp.float32
    )


def state_kernel(live_ref, start_ref, y_ref, fresh_ref, c_ref, ecum_ref, elast_ref, y_out_ref, final_ref):
    rows = y_ref.shape[0]
    start = start_ref[...]
    start = jnp.where(live_ref[0] > 0, start, jnp.zeros_like(start))
    low = lax.broadcasted_iota(jnp.int32, (rows, 128), 1) < HEAD_DIM
    ecum = ecum_ref[0]
    ys = jnp.dot(c_ref[...], start, preferred_element_type=jnp.float32)
    for j in range(0, PER_STEP, 2):
        sl = slice(j * HEAD_DIM, (j + 2) * HEAD_DIM)
        factor = jnp.where(low, ecum[:, j : j + 1], ecum[:, j + 1 : j + 2])
        y_out_ref[:, sl] = (y_ref[:, sl] + factor * ys[:, sl]).astype(jnp.bfloat16)
    final_ref[0] = (elast_ref[...] * start.astype(jnp.float32) + fresh_ref[...]).astype(jnp.bfloat16)


def by_step(a):
    return a.reshape(a.shape[0], STEPS, PER_STEP).transpose(1, 0, 2)


LANES = 4
CHUNKS = 4
WIDE = INNER // LANES
CC = WIDE // CHUNKS
TAIL_ROWS = 16
LAG = 2
MESH = pl.DeviceIdType.MESH


def masked_column(row, rows):
    sub = lax.broadcasted_iota(jnp.int32, (rows, 128), 0)
    lane = lax.broadcasted_iota(jnp.int32, (rows, 128), 1)
    return jnp.sum(jnp.where(sub == lane, jnp.broadcast_to(row, (rows, 128)), 0), axis=1, keepdims=True)


def destinations(wanted, n):
    planes = n // LANES
    sub = lax.broadcasted_iota(jnp.int32, (n, 128), 0) // LANES
    lane = lax.broadcasted_iota(jnp.int32, (n, 128), 1)
    hit = wanted == lane
    top = jnp.max(jnp.where(hit, sub, -1), axis=0, keepdims=True)
    low = jnp.min(jnp.where(hit, sub, planes), axis=0, keepdims=True)
    return top, low


def info_kernel(groups, n, owner_ref, slot_ref, spans_ref, request_ref, table_ref, mine, rows, send_sem, recv_sem):
    planes = n // LANES
    grp, me = lax.axis_index("grp"), lax.axis_index("req")
    total = groups * n
    flat = grp * n + me
    barrier = pltpu.get_barrier_semaphore()

    def other(k):
        to = lax.rem(flat + k, total)
        return lax.div(to, n), lax.rem(to, n)

    for k in range(1, total):
        pl.semaphore_signal(barrier, inc=1, device_id=other(k), device_id_type=MESH)
    request = request_ref[0]
    wanted = jnp.where(spans_ref[request] > 0, owner_ref[request], -1)
    served = jnp.int32(0)
    for r in range(n):
        served = jnp.maximum(served, jnp.where(owner_ref[r] == me, slot_ref[r], 0))
    mine[...] = jnp.full((1, 128), wanted, jnp.int32)
    pl.semaphore_wait(barrier, total - 1)
    copies = []
    for k in range(1, total):
        to_grp, to_req = other(k)
        row = lax.rem(grp - to_grp + groups, groups) * n + me
        copy = pltpu.make_async_remote_copy(
            src_ref=mine, dst_ref=rows.at[row], send_sem=send_sem.at[k], recv_sem=recv_sem.at[k],
            device_id=(to_grp, to_req), device_id_type=MESH,
        )
        copy.start()
        copies.append(copy)
    rows[pl.ds(me, 1)] = mine[...].reshape(1, 1, 128)
    for copy in copies:
        copy.wait()

    need = jnp.zeros((1, 1), jnp.int32)
    lane_row = lax.broadcasted_iota(jnp.int32, (1, 128), 1)
    home = lane_row // LANES
    for g in range(groups):
        top, low = destinations(rows[g * n : (g + 1) * n].reshape(n, 128), n)
        for cut in range(planes - 1):
            up = jnp.sum(((home <= cut) & (top > cut) & (lane_row < n)).astype(jnp.int32), axis=1, keepdims=True)
            down = jnp.sum(((home > cut) & (low <= cut) & (lane_row < n)).astype(jnp.int32), axis=1, keepdims=True)
            need = jnp.maximum(need, jnp.maximum(up, down))

    z = me // LANES
    wants = rows[0:n].reshape(n, 128)
    top, low = destinations(wants, n)
    sub = lax.broadcasted_iota(jnp.int32, (n, 128), 0)
    lane = lax.broadcasted_iota(jnp.int32, (n, 128), 1)
    wants_row = jnp.sum(jnp.where(sub == lane, wants, 0), axis=0, keepdims=True)
    col = lax.broadcasted_iota(jnp.int32, (n, 1), 0)
    col_home = col // LANES
    top_col, low_col = masked_column(top, n), masked_column(low, n)

    def up_set(where_home, where_top, cut):
        return (where_home <= cut) & (where_top > cut)

    def down_set(where_home, where_low, cut):
        return (where_home > cut) & (where_low <= cut)

    def rank(inside, key_row, key_col):
        ahead = inside & (key_row < key_col) & (lane_row < n)
        return jnp.sum(ahead.astype(jnp.int32), axis=1, keepdims=True)

    up_row, up_col = (planes - top) * n + lane_row, (planes - top_col) * n + col
    down_row, down_col = (low + 1) * n + lane_row, (low_col + 1) * n + col
    up_in = rank(up_set(home, top, z - 1), up_row, up_col)
    up_out = rank(up_set(home, top, z), up_row, up_col)
    down_in = rank(down_set(home, low, z), down_row, down_col)
    down_out = rank(down_set(home, low, z - 1), down_row, down_col)
    near = lax.rem(col, LANES)
    src_up = jnp.where(col_home == z, near, LANES + up_in)
    src_down = jnp.where(col_home == z, near, LANES + down_in)
    src_fin = jnp.where(col_home == z, near, jnp.where(col_home < z, LANES + up_in, LANES + n + down_in))
    sel_up = jnp.sum(jnp.where(up_set(col_home, top_col, z) & (up_out == lane), src_up, 0), axis=0, keepdims=True)
    sel_down = jnp.sum(jnp.where(down_set(col_home, low_col, z - 1) & (down_out == lane), src_down, 0), axis=0, keepdims=True)
    sel_fin = jnp.sum(jnp.where(wants_row == col, src_fin, 0), axis=0, keepdims=True)
    sel_fin = jnp.where(wants_row < 0, -1, sel_fin)
    table_ref[...] = jnp.zeros_like(table_ref)
    table_ref[0:1, :] = sel_up
    table_ref[1:2, :] = sel_down
    table_ref[2:3, :] = sel_fin
    table_ref[3:4, :] = jnp.broadcast_to(need, (1, 128))
    table_ref[4:5, :] = jnp.full((1, 128), served, jnp.int32)


def info(mesh, hit_owner, hit_slot, hit_spans, request_of):
    groups, n = mesh.shape["grp"], mesh.shape["req"]
    smem = pl.BlockSpec(memory_space=pltpu.SMEM)
    return pl.pallas_call(
        functools.partial(info_kernel, groups, n),
        out_shape=jax.ShapeDtypeStruct((8, 128), jnp.int32),
        in_specs=[smem] * 4,
        out_specs=pl.BlockSpec(memory_space=pltpu.VMEM),
        scratch_shapes=[
            pltpu.VMEM((1, 128), jnp.int32),
            pltpu.VMEM((groups * n, 1, 128), jnp.int32),
            pltpu.SemaphoreType.DMA((groups * n,)),
            pltpu.SemaphoreType.DMA((groups * n,)),
        ],
        compiler_params=pltpu.CompilerParams(collective_id=0, has_side_effects=True, vmem_limit_bytes=8 * 2**20),
        name="info",
    )(hit_owner, hit_slot, hit_spans, request_of)


def conv(taps, bias, pad, rows):
    v = jnp.broadcast_to(bias, (rows, bias.shape[1]))
    for k in range(4):
        v = v + taps[k : k + 1, :] * pad[5 + k : 5 + k + rows, :]
    return (v / (1.0 + jnp.exp(-v))).astype(jnp.bfloat16)


def route_kernel(
    n, slots, tab, states_ref, tails_ref, xbc_ref, dt_ref, weight_ref, bias_ref, dt_bias_ref, a_log_ref, skip_ref,
    y_out, final_out,
    start, tail_out, xs, pad, head_pad, tail_rows, cum_ref, cumt_ref, stept_ref, coef_ref, ecum_ref, elast_ref,
    scores_ref, y_local, fresh, y_stage, f_stage, y_sem, f_sem,
    three, own, own_tail, packed, plane, plane_t, up_recv, up_recv_t, down_recv, down_recv_t,
    up_send, up_send_t, down_send, down_send_t, fin_send, fin_send_t,
    load_sem, spread_s, spread_r, spread_ts, spread_tr, up_s, up_r, up_ts, up_tr,
    down_s, down_r, down_ts, down_tr, fin_s, fin_r, fin_ts, fin_tr,
):
    planes = n // LANES
    steps = CHUNKS * slots
    grp, me = lax.axis_index("grp"), lax.axis_index("req")
    z, l = lax.div(me, LANES), lax.rem(me, LANES)
    first, last = z == 0, z == planes - 1

    def mate(k):
        return z * LANES + lax.rem(l + k, LANES)

    loads = []
    for i in range(states_ref.shape[0]):
        load = pltpu.make_async_copy(states_ref.at[i], three.at[i], load_sem.at[i])
        load.start()
        loads.append(load)
    barrier = pltpu.get_barrier_semaphore()
    for k in range(1, LANES):
        pl.semaphore_signal(barrier, inc=1, device_id=(grp, mate(k)), device_id_type=MESH)

    @pl.when(jnp.logical_not(first))
    def _():
        pl.semaphore_signal(barrier, inc=1, device_id=(grp, me - LANES), device_id_type=MESH)

    @pl.when(jnp.logical_not(last))
    def _():
        pl.semaphore_signal(barrier, inc=1, device_id=(grp, me + LANES), device_id_type=MESH)

    served = tab[4, 0]
    tail = tails_ref[served].astype(jnp.float32)
    packed[...] = jnp.zeros_like(packed)
    for q in range(-(-tail.shape[1] // WIDE)):
        for p in range(LANES):
            at = q * WIDE + p * CC
            if at < tail.shape[1]:
                packed[p, 3 * q : 3 * q + 3, :] = tail[:, at : at + CC]
    own_tail[...] = packed[...].astype(jnp.bfloat16)
    for load in loads:
        load.wait()

    def take(c):
        for p in range(LANES):
            own[p, c] = three[served, :, p * WIDE + c * CC : p * WIDE + (c + 1) * CC]

    for c in range(CHUNKS):
        take(c)
    for c in range(CHUNKS):
        plane[c, pl.ds(l, 1)] = own[pl.ds(l, 1), c]
    plane_t[pl.ds(l, 1)] = own_tail[pl.ds(l, 1)]

    pl.semaphore_wait(barrier, LANES - 1 + jnp.where(first | last, 1, 2))

    def remote(src, dst, ss, rs, to):
        return pltpu.make_async_remote_copy(
            src_ref=src, dst_ref=dst, send_sem=ss, recv_sem=rs, device_id=(grp, to), device_id_type=MESH
        )

    def spread(c, k):
        to = lax.rem(l + k, LANES)
        return remote(own.at[to, c], plane.at[c, l], spread_s.at[c, k - 1], spread_r.at[c, k - 1], mate(k))

    def spread_tail(k):
        to = lax.rem(l + k, LANES)
        return remote(own_tail.at[to], plane_t.at[l], spread_ts.at[k - 1], spread_tr.at[k - 1], mate(k))

    def spread_from(c, k):
        frm = lax.rem(l + LANES - k, LANES)
        return remote(own.at[frm, c], plane.at[c, frm], spread_s.at[c, k - 1], spread_r.at[c, k - 1], mate(k))

    def spread_tail_from(k):
        frm = lax.rem(l + LANES - k, LANES)
        return remote(own_tail.at[frm], plane_t.at[frm], spread_ts.at[k - 1], spread_tr.at[k - 1], mate(k))

    def up(s):
        return remote(up_send.at[s], up_recv.at[s], up_s.at[s], up_r.at[s], me + LANES)

    def up_tail(s):
        return remote(up_send_t.at[s], up_recv_t.at[s], up_ts.at[s], up_tr.at[s], me + LANES)

    def down(s):
        return remote(down_send.at[s], down_recv.at[s], down_s.at[s], down_r.at[s], me - LANES)

    def down_tail(s):
        return remote(down_send_t.at[s], down_recv_t.at[s], down_ts.at[s], down_tr.at[s], me - LANES)

    def fin(c, k):
        to = lax.rem(l + k, LANES)
        return remote(fin_send.at[c, k - 1], start.at[l, c], fin_s.at[c, k - 1], fin_r.at[c, k - 1], mate(k))

    def fin_from(c, k):
        frm = lax.rem(l + LANES - k, LANES)
        return remote(fin_send.at[c, k - 1], start.at[frm, c], fin_s.at[c, k - 1], fin_r.at[c, k - 1], mate(k))

    def fin_tail(k):
        return remote(fin_send_t.at[k - 1], tail_out.at[l], fin_ts.at[k - 1], fin_tr.at[k - 1], mate(k))

    def fin_tail_from(k):
        frm = lax.rem(l + LANES - k, LANES)
        return remote(fin_send_t.at[k - 1], tail_out.at[frm], fin_ts.at[k - 1], fin_tr.at[k - 1], mate(k))

    for k in range(1, LANES):
        spread_tail(k).start()
    for c in range(min(2, CHUNKS)):
        for k in range(1, LANES):
            spread(c, k).start()

    rows = xbc_ref.shape[0]
    channels = xbc_ref.shape[1]
    pieces = channels // CC
    heads = CC // HEAD_DIM
    first_b, first_c = INNER, INNER + GROUPS * NST
    low = lax.broadcasted_iota(jnp.int32, (rows, 128), 1) < HEAD_DIM
    low_n = lax.broadcasted_iota(jnp.int32, (NST, 128), 1) < HEAD_DIM

    def columns(i):
        return pl.ds(pl.multiple_of(i * CC, CC), CC)

    def head_terms():
        step = jax.nn.softplus(dt_ref[...] + dt_bias_ref[...])
        below = (
            lax.broadcasted_iota(jnp.int32, (rows, rows), 0) >= lax.broadcasted_iota(jnp.int32, (rows, rows), 1)
        ).astype(jnp.float32)
        cum = jnp.dot(below, step * (-jnp.exp(a_log_ref[...])), precision=lax.Precision.HIGHEST,
                      preferred_element_type=jnp.float32)
        last = cum[rows - 1 : rows, :]
        cum_ref[...] = cum
        cumt_ref[...] = cum.T
        stept_ref[...] = step.T
        coef_ref[...] = jnp.exp(last - cum) * step
        ecum_ref[...] = jnp.exp(cum)
        elast_ref[...] = jnp.broadcast_to(jnp.exp(last), elast_ref.shape)

    def conv_piece(i):
        at = columns(i)
        pad[0:8, :] = jnp.zeros((8, CC), jnp.float32)
        pad[8 : 8 + rows, :] = xbc_ref[:, at].astype(jnp.float32)
        xs[:, at] = conv(weight_ref[:, at], bias_ref[:, at], pad, rows)

    def head_piece(i, _):
        at = columns(i)
        head_pad[0:8, :] = tail_rows[:, at]
        head_pad[8:24, :] = xbc_ref[0:16, at].astype(jnp.float32)
        xs[0:16, at] = conv(weight_ref[:, at], bias_ref[:, at], head_pad, 16)
        return 0

    def with_tail():
        tail_rows[...] = jnp.zeros_like(tail_rows)
        for p in range(LANES):
            got = tail_out[p].astype(jnp.float32)
            for q in range(-(-channels // WIDE)):
                at = q * WIDE + p * CC
                if at < channels:
                    tail_rows[5:8, at : at + CC] = got[3 * q : 3 * q + 3, :]
        lax.fori_loop(0, pieces, head_piece, 0)
        causal = lax.broadcasted_iota(jnp.int32, (rows, rows), 0) >= lax.broadcasted_iota(jnp.int32, (rows, rows), 1)
        for g in range(GROUPS):
            b = xs[:, first_b + g * NST : first_b + (g + 1) * NST]
            c = xs[:, first_c + g * NST : first_c + (g + 1) * NST]
            scores = lax.dot_general(c, b, (((1,), (1,)), ((), ())), preferred_element_type=jnp.float32)
            scores_ref[g] = jnp.where(causal, scores, 0.0)

    def turned(ref, i):
        return pltpu.roll(ref[...], lax.rem(128 - heads * i, 128), axis=1)

    def scan_piece(p, c):
        i = p * CHUNKS + c
        at = columns(i)
        x = xs[:, at]
        scores = scores_ref[p]
        cum, coef, skip = turned(cum_ref, i), turned(coef_ref, i), turned(skip_ref, i)
        here = pl.ds(pl.multiple_of(i * heads, heads), heads)
        cumt, stept = cumt_ref[here, :], stept_ref[here, :]
        zero = jnp.zeros((rows, 128), jnp.bfloat16)
        ys, carried = [], []
        for j in range(0, heads, 2):
            xp = x[:, j * HEAD_DIM : (j + 2) * HEAD_DIM]
            mixes = []
            for h in (j, j + 1):
                decay = jnp.exp(jnp.minimum(cum[:, h : h + 1] - cumt[h : h + 1, :], 0.0))
                mixes.append((scores * decay * stept[h : h + 1, :]).astype(jnp.bfloat16))
            mix = jnp.concatenate(mixes, axis=1)
            both = jnp.concatenate([jnp.where(low, xp, zero), jnp.where(low, zero, xp)], axis=0)
            xf = xp.astype(jnp.float32)
            d = jnp.where(low[0:1], skip[0:1, j : j + 1], skip[0:1, j + 1 : j + 2])
            ys.append(jnp.dot(mix, both, preferred_element_type=jnp.float32) + d * xf)
            carried.append((jnp.where(low, coef[:, j : j + 1], coef[:, j + 1 : j + 2]) * xf).astype(jnp.bfloat16))
        y_local[i] = jnp.concatenate(ys, axis=1)
        b = xs[:, pl.ds(pl.multiple_of(first_b + p * NST, NST), NST)]
        fresh[i] = lax.dot_general(
            b, jnp.concatenate(carried, axis=1), (((0,), (0,)), ((), ())), preferred_element_type=jnp.float32
        )

    def outputs(i):
        return (
            pltpu.make_async_copy(y_stage.at[i], y_out.at[:, columns(i)], y_sem.at[i]),
            pltpu.make_async_copy(f_stage.at[i], final_out.at[0, :, columns(i)], f_sem.at[i]),
        )

    def last_piece(p, c):
        i = p * CHUNKS + c
        held = start[p, c]
        ys = jnp.dot(xs[:, pl.ds(pl.multiple_of(first_c + p * NST, NST), NST)], held,
                     preferred_element_type=jnp.float32)
        ecum, elast = turned(ecum_ref, i), turned(elast_ref, i)
        for j in range(0, heads, 2):
            sl = slice(j * HEAD_DIM, (j + 2) * HEAD_DIM)
            factor = jnp.where(low, ecum[:, j : j + 1], ecum[:, j + 1 : j + 2])
            y_stage[i, :, sl] = (y_local[i, :, sl] + factor * ys[:, sl]).astype(jnp.bfloat16)
            kept = jnp.where(low_n[0:1], elast[0:1, j : j + 1], elast[0:1, j + 1 : j + 2])
            f_stage[i, :, sl] = (kept * held[:, sl].astype(jnp.float32) + fresh[i, :, sl]).astype(jnp.bfloat16)
        for copy in outputs(i):
            copy.start()

    def last_chunk(c):
        for k in range(1, LANES):
            fin_from(c, k).wait_recv()

        def one(p, _):
            last_piece(p, c)
            return 0

        lax.fori_loop(0, LANES, one, 0)

    ready = slots + LAG * (planes - 1)
    total = steps + LAG * (planes - 1)
    per_conv = -(-pieces // ready)
    per_scan = -(-(LANES * CHUNKS) // (total - ready - 1))

    lead = -(-LANES // per_scan)

    def compute(t):
        @pl.when(t < ready)
        def _():
            def one(u, _):
                i = t * per_conv + u

                @pl.when(i < pieces)
                def _():
                    conv_piece(i)

                return 0

            lax.fori_loop(0, per_conv, one, 0)

        @pl.when(t == ready)
        def _():
            for k in range(1, LANES):
                fin_tail_from(k).wait_recv()
            with_tail()

        @pl.when(t > ready)
        def _():
            def one(u, _):
                i = (t - ready - 1) * per_scan + u

                @pl.when(i < LANES * CHUNKS)
                def _():
                    scan_piece(lax.rem(i, LANES), lax.div(i, LANES))

                return 0

            lax.fori_loop(0, per_scan, one, 0)
            since = t - ready - lead

            @pl.when((since >= 0) & (lax.rem(jnp.maximum(since, 0), slots) == 0))
            def _():
                last_chunk(lax.div(since, slots))

    def fill(dst, at, sel, near, c, far, base, j, inner):
        value = near[c, 0]
        for p in range(1, LANES):
            value = lax.select_n(sel == p, value, near[c, p])
        dst[at] = value

        @pl.when(inner)
        def _():
            def one(i, _):
                dst[at] = lax.select_n(sel == LANES + i, dst[at], far[base + i])
                return 0

            lax.fori_loop(0, j + 1, one, 0)

    def fill_tail(dst, j, sel, far, inner):
        value = plane_t[0]
        for p in range(1, LANES):
            value = lax.select_n(sel == p, value, plane_t[p])
        dst[j] = value

        @pl.when(inner)
        def _():
            def one(i, _):
                dst[j] = lax.select_n(sel == LANES + i, dst[j], far[i])
                return 0

            lax.fori_loop(0, j + 1, one, 0)

    def tick(t, _):
        tp = t - LAG * jnp.minimum(z, planes - 1 - z)

        @pl.when((tp >= 0) & (tp < steps) & (lax.rem(jnp.maximum(tp, 0), slots) == 0))
        def _():
            c = lax.div(tp, slots)

            @pl.when(c == 0)
            def _():
                for k in range(1, LANES):
                    spread_tail_from(k).wait_recv()

            for k in range(1, LANES):
                spread_from(c, k).wait_recv()

            @pl.when(c + 2 < CHUNKS)
            def _():
                for k in range(1, LANES):
                    spread(c + 2, k).start()

        def along(s, row, edge_in, edge_out, copy, copy_tail, send, send_t, recv, recv_t):
            @pl.when((s >= 0) & (s < steps))
            def _():
                c, j = lax.div(s, slots), lax.rem(s, slots)
                inner = jnp.logical_not(edge_in)

                @pl.when(inner)
                def _():
                    @pl.when(c == 0)
                    def _():
                        copy_tail(j).wait_recv()

                    copy(s).wait_recv()

                @pl.when(jnp.logical_not(edge_out))
                def _():
                    sel = tab[row, j]

                    @pl.when(c == 0)
                    def _():
                        fill_tail(send_t, j, sel, recv_t, inner)
                        copy_tail(j).start()

                    fill(send, s, sel, plane, c, recv, c * slots, j, inner)

                    @pl.when(s >= 2)
                    def _():
                        copy(s - 2).wait_send()

                    copy(s).start()

        along(t - LAG * z, 0, first, last, up, up_tail, up_send, up_send_t, up_recv, up_recv_t)
        along(t - LAG * (planes - 1 - z), 1, last, first, down, down_tail, down_send, down_send_t, down_recv, down_recv_t)

        tf = t - LAG * jnp.maximum(z, planes - 1 - z)

        @pl.when((tf >= 0) & (tf < steps) & (lax.rem(jnp.maximum(tf, 0), slots) == slots - 1))
        def _():
            c = lax.div(tf, slots)
            sels = [tab[2, mate(k)] for k in range(LANES)]

            def choose(near, far_up, far_down, write, read):
                acc = [jnp.zeros(near(0).shape, jnp.bfloat16)] * LANES
                for p in range(LANES):
                    value = near(p)
                    acc = [lax.select_n(sel == p, a, value) for sel, a in zip(sels, acc)]
                for k in range(LANES):
                    write(k, acc[k])

                def far(get, base):
                    acc = [read(k) for k in range(LANES)]
                    for i in range(slots):
                        value = get(i)
                        acc = [lax.select_n(sel == base + i, a, value) for sel, a in zip(sels, acc)]
                    for k in range(LANES):
                        write(k, acc[k])

                @pl.when(jnp.logical_not(first))
                def _():
                    far(far_up, LANES)

                @pl.when(jnp.logical_not(last))
                def _():
                    far(far_down, LANES + n)

            def rows_of(b, _):
                at = pl.ds(pl.multiple_of(b * 16, 16), 16)

                def write(k, v):
                    if k == 0:
                        start[l, c, at] = v
                    else:
                        fin_send[c, k - 1, at] = v

                def read(k):
                    return start[l, c, at] if k == 0 else fin_send[c, k - 1, at]

                choose(lambda p: plane[c, p, at], lambda i: up_recv[c * slots + i, at],
                       lambda i: down_recv[c * slots + i, at], write, read)
                return 0

            lax.fori_loop(0, NST // 16, rows_of, 0)
            for k in range(1, LANES):
                fin(c, k).start()

            @pl.when(c == 0)
            def _():
                def write(k, v):
                    if k == 0:
                        tail_out[l] = v
                    else:
                        fin_send_t[k - 1] = v

                def read(k):
                    return tail_out[l] if k == 0 else fin_send_t[k - 1]

                choose(lambda p: plane_t[p], lambda i: up_recv_t[i], lambda i: down_recv_t[i], write, read)
                for k in range(1, LANES):
                    fin_tail(k).start()

        compute(t)
        return 0

    head_terms()
    lax.fori_loop(0, total, tick, 0)
    for c in range((total - 1 - ready - lead) // slots + 1, CHUNKS):
        last_chunk(c)

    for k in range(1, LANES):
        spread_tail(k).wait_send()
        fin_tail(k).wait_send()
        for c in range(CHUNKS):
            spread(c, k).wait_send()
            fin(c, k).wait_send()

    @pl.when(jnp.logical_not(last))
    def _():
        for j in range(slots):
            up_tail(j).wait_send()
        for s in range(max(steps - 2, 0), steps):
            up(s).wait_send()

    @pl.when(jnp.logical_not(first))
    def _():
        for j in range(slots):
            down_tail(j).wait_send()
        for s in range(max(steps - 2, 0), steps):
            down(s).wait_send()

    for i in range(LANES * CHUNKS):
        for copy in outputs(i):
            copy.wait()


def route(n, slots, number, table, cache_states, cache_tails, xbc, dt_raw, weight, bias, dt_bias, a_log, skip):
    steps = CHUNKS * slots
    rows, channels = xbc.shape
    pieces = LANES * CHUNKS
    f32 = lambda *shape: pltpu.VMEM(shape, jnp.float32)
    big = lambda *lead: pltpu.VMEM(lead + (NST, CC), jnp.bfloat16)
    small = lambda *lead: pltpu.VMEM(lead + (TAIL_ROWS, CC), jnp.bfloat16)
    sem = lambda *shape: [pltpu.SemaphoreType.DMA(shape)] * 2
    vmem = pl.BlockSpec(memory_space=pltpu.VMEM)
    hbm = pl.BlockSpec(memory_space=pl.ANY)
    return pl.pallas_call(
        functools.partial(route_kernel, n, slots),
        out_shape=(
            jax.ShapeDtypeStruct((rows, INNER), jnp.bfloat16),
            jax.ShapeDtypeStruct((1, NST, INNER), jnp.bfloat16),
        ),
        in_specs=[pl.BlockSpec(memory_space=pltpu.SMEM), hbm] + [vmem] * 8,
        out_specs=(hbm, hbm),
        scratch_shapes=[
            big(LANES, CHUNKS), small(LANES),
            pltpu.VMEM((rows, channels), jnp.bfloat16), f32(8 + rows, CC), f32(24, CC), f32(8, channels),
            f32(rows, HEADS), f32(HEADS, rows), f32(HEADS, rows), f32(rows, HEADS), f32(rows, HEADS), f32(8, HEADS),
            f32(GROUPS, rows, rows), f32(pieces, rows, CC), f32(pieces, NST, CC),
            pltpu.VMEM((pieces, rows, CC), jnp.bfloat16), big(pieces), *sem(pieces),
            pltpu.VMEM(cache_states.shape, jnp.bfloat16),
            big(LANES, CHUNKS), small(LANES), f32(LANES, TAIL_ROWS, CC),
            big(CHUNKS, LANES), small(LANES),
            big(steps), small(slots), big(steps), small(slots),
            big(steps), small(slots), big(steps), small(slots),
            big(CHUNKS, LANES - 1), small(LANES - 1),
            pltpu.SemaphoreType.DMA((cache_states.shape[0],)),
            *sem(CHUNKS, LANES - 1), *sem(LANES - 1),
            *sem(steps), *sem(slots), *sem(steps), *sem(slots),
            *sem(CHUNKS, LANES - 1), *sem(LANES - 1),
        ],
        compiler_params=pltpu.CompilerParams(
            collective_id=number, has_side_effects=True, vmem_limit_bytes=58 * 2**20
        ),
        name=f"route{slots}",
    )(table, cache_states, cache_tails, xbc, dt_raw, weight, bias, dt_bias, a_log, skip)


def local_routed(
    mesh, xbc, dt_raw, conv_weight, conv_bias, dt_bias, a_log, d_skip, cache_states, cache_tails,
    hit_owner, hit_slot, hit_spans, request_of,
):
    n = mesh.shape["req"]
    table = info(mesh, hit_owner, hit_slot, hit_spans, request_of)
    need = table[3, 0]
    sizes = [3, 4, n // 2]
    which = sum((need > size).astype(jnp.int32) for size in sizes[:-1])
    return lax.switch(
        which,
        [functools.partial(route, n, size, 1 + i) for i, size in enumerate(sizes)],
        table, cache_states, cache_tails, xbc, dt_raw, conv_weight, conv_bias[None], dt_bias[None], a_log[None],
        jnp.broadcast_to(d_skip[None], (8, HEADS)),
    )


def local(
    xbc, dt_raw, conv_weight, conv_bias, dt_bias, a_log, d_skip, cache_states, cache_tails,
    hit_owner, hit_slot, hit_spans, request_of,
):
    count = hit_owner.shape[0]
    rows = xbc.shape[0]
    mine = request_of[0]
    live = (hit_spans[mine] > 0).astype(jnp.int32)
    device = lax.axis_index("req")
    served = jnp.max(jnp.where(hit_owner == device, hit_slot, 0))
    send = lax.dynamic_slice_in_dim(cache_states, served, 1, 0).reshape(count, NST // count, INNER)
    number = jnp.broadcast_to(mine.astype(send.dtype), send.shape[:2] + (128,))
    parts = lax.all_to_all(
        jnp.concatenate([send, number], axis=2), "req", split_axis=0, concat_axis=0, tiled=True
    )
    every_request = parts[:, 0, INNER].astype(jnp.int32)
    own_tail = lax.dynamic_slice_in_dim(cache_tails, served, 1, 0)
    own_tail = jnp.pad(own_tail, ((0, 0), (0, 1), (0, 0)))
    every_tail = lax.all_gather(own_tail, "req", axis=0, tiled=True)[:, :3]
    owners = jnp.sum(
        jnp.where(every_request[:, None] == jnp.arange(count)[None, :], hit_owner[None, :], 0), axis=1
    )
    chosen = pick(parts, owners)
    start = lax.all_to_all(chosen, "req", split_axis=0, concat_axis=0, tiled=True).reshape(NST, INNER)

    tail = lax.dynamic_index_in_dim(every_tail, hit_owner[mine], 0, keepdims=False)
    tail = jnp.where(live > 0, tail, jnp.zeros_like(tail)).astype(jnp.float32)
    tail = jnp.pad(tail, ((5, 0), (0, 0)))
    step = jax.nn.softplus(dt_raw + dt_bias[None, :])
    below = jnp.tril(jnp.ones((rows, rows), jnp.float32))
    cum = jnp.dot(below, step * (-jnp.exp(a_log))[None, :], precision=lax.Precision.HIGHEST)
    last = cum[rows - 1]
    coef = jnp.exp(last[None, :] - cum) * step
    skip = jnp.repeat(d_skip, HEAD_DIM)[None, :]
    elast = jnp.repeat(jnp.exp(last), HEAD_DIM)[None, :]
    cumt = cum.T.reshape(STEPS, PER_STEP, rows)
    stept = step.T.reshape(STEPS, PER_STEP, rows)
    bias = conv_bias[None, :]

    first_b, first_c = INNER // NST, INNER // NST + GROUPS
    per = STEPS_PER_GROUP
    triple = lambda r: [
        pl.BlockSpec((r, COLS), lambda i: (0, i)),
        pl.BlockSpec((r, NST), lambda i: (0, first_b + i // per)),
        pl.BlockSpec((r, NST), lambda i: (0, first_c + i // per)),
    ]
    wide = lambda r: pl.BlockSpec((r, COLS), lambda i: (0, i))
    tall = pl.BlockSpec((1, rows, PER_STEP), lambda i: (i, 0, 0))
    flat = pl.BlockSpec((1, PER_STEP, rows), lambda i: (i, 0, 0))
    group = pl.BlockSpec((rows, NST), lambda i: (0, i // per))
    y_local, fresh, c_part = pl.pallas_call(
        local_kernel,
        grid=(STEPS,),
        out_shape=(
            jax.ShapeDtypeStruct((rows, INNER), jnp.float32),
            jax.ShapeDtypeStruct((NST, INNER), jnp.float32),
            jax.ShapeDtypeStruct((rows, GROUPS * NST), jnp.bfloat16),
        ),
        in_specs=triple(rows) + triple(8) + triple(4) + triple(1) + [tall, flat, flat, tall, wide(1)],
        out_specs=(wide(rows), wide(NST), group),
        scratch_shapes=[pltpu.VMEM((8 + rows, COLS), jnp.float32)],
        compiler_params=pltpu.CompilerParams(vmem_limit_bytes=58 * 2**20),
        cost_estimate=pl.CostEstimate(flops=10**9, bytes_accessed=40 * 10**6, transcendentals=4 * 10**6),
        name="local",
    )(xbc, xbc, xbc, tail, tail, tail, conv_weight, conv_weight, conv_weight, bias, bias, bias,
      by_step(cum), cumt, stept, by_step(coef), skip)

    return pl.pallas_call(
        state_kernel,
        grid=(STEPS,),
        out_shape=(
            jax.ShapeDtypeStruct((rows, INNER), jnp.bfloat16),
            jax.ShapeDtypeStruct((1, NST, INNER), jnp.bfloat16),
        ),
        in_specs=[pl.BlockSpec(memory_space=pltpu.SMEM), wide(NST), wide(rows), wide(NST), group, tall, wide(1)],
        out_specs=(wide(rows), pl.BlockSpec((1, NST, COLS), lambda i: (0, 0, i))),
        compiler_params=pltpu.CompilerParams(vmem_limit_bytes=58 * 2**20),
        name="state",
    )(live[None], start, y_local, fresh, c_part, by_step(jnp.exp(cum)), elast)


def solution(mesh):
    rows = P(("grp", "req"), None)
    slots = P(("grp", "req"), None, None)
    in_specs = (
        rows, rows, P(), P(), P(), P(), P(), slots, slots, P("grp"), P("grp"), P("grp"), P(("grp", "req")),
    )
    body = functools.partial(local_routed, mesh) if mesh.shape["req"] == 16 else local
    return jax.shard_map(body, mesh=mesh, in_specs=in_specs, out_specs=(rows, slots), check_vma=False)
```

```python
import functools

import jax
import jax.numpy as jnp
from jax import lax
from jax.experimental import pallas as pl
from jax.experimental.pallas import tpu as pltpu
from jax.sharding import PartitionSpec as P

HEADS = 128
HEAD_DIM = 64
GROUPS = 4
NST = 128
INNER = 8192
PER_STEP = 16
COLS = PER_STEP * HEAD_DIM
STEPS = HEADS // PER_STEP
STEPS_PER_GROUP = STEPS // GROUPS


def pick_kernel(index_ref, parts_ref, out_ref, sem):
    count = out_ref.shape[0]
    copies = []
    for i in range(count):
        copy = pltpu.make_async_copy(parts_ref.at[index_ref[i], :, pl.ds(0, INNER)], out_ref.at[i], sem.at[i])
        copy.start()
        copies.append(copy)
    for copy in copies:
        copy.wait()


def pick(parts, index):
    count = index.shape[0]
    return pl.pallas_call(
        pick_kernel,
        out_shape=jax.ShapeDtypeStruct((count, parts.shape[1], INNER), parts.dtype),
        in_specs=[pl.BlockSpec(memory_space=pltpu.SMEM), pl.BlockSpec(memory_space=pltpu.VMEM)],
        out_specs=pl.BlockSpec(memory_space=pl.ANY),
        scratch_shapes=[pltpu.SemaphoreType.DMA((count,))],
        compiler_params=pltpu.CompilerParams(vmem_limit_bytes=8 * 2**20),
        name="pick",
    )(index, parts)


def conv_block(pad, x_ref, tail_ref, w_ref, b_ref, width):
    rows = x_ref.shape[0]
    pad[0:8, 0:width] = tail_ref[...]
    pad[8 : 8 + rows, 0:width] = x_ref[...].astype(jnp.float32)
    v = jnp.broadcast_to(b_ref[...], (rows, width))
    for k in range(4):
        v = v + w_ref[k : k + 1, :] * pad[5 + k : 5 + k + rows, 0:width]
    return (v / (1.0 + jnp.exp(-v))).astype(jnp.bfloat16)


def local_kernel(
    x_ref, xb_ref, xc_ref, tx_ref, tb_ref, tc_ref, wx_ref, wb_ref, wc_ref, bx_ref, bb_ref, bc_ref,
    cum_ref, cumt_ref, stept_ref, coef_ref, skip_ref,
    y_ref, fresh_ref, c_out_ref, pad,
):
    rows = x_ref.shape[0]
    b_part = conv_block(pad, xb_ref, tb_ref, wb_ref, bb_ref, NST)
    c_part = conv_block(pad, xc_ref, tc_ref, wc_ref, bc_ref, NST)
    c_out_ref[...] = c_part
    x = conv_block(pad, x_ref, tx_ref, wx_ref, bx_ref, COLS)
    scores = lax.dot_general(c_part, b_part, (((1,), (1,)), ((), ())), preferred_element_type=jnp.float32)
    causal = lax.broadcasted_iota(jnp.int32, (rows, rows), 0) >= lax.broadcasted_iota(jnp.int32, (rows, rows), 1)
    scores = jnp.where(causal, scores, 0.0)
    low = lax.broadcasted_iota(jnp.int32, (rows, 128), 1) < HEAD_DIM
    cum = cum_ref[0]
    coef = coef_ref[0]
    zero = jnp.zeros((rows, 128), jnp.bfloat16)
    carried = []
    for j in range(0, PER_STEP, 2):
        xp = x[:, j * HEAD_DIM : (j + 2) * HEAD_DIM]
        mixes = []
        for h in (j, j + 1):
            decay = jnp.exp(jnp.minimum(cum[:, h : h + 1] - cumt_ref[0, h : h + 1, :], 0.0))
            mixes.append((scores * decay * stept_ref[0, h : h + 1, :]).astype(jnp.bfloat16))
        mix = jnp.concatenate(mixes, axis=1)
        both = jnp.concatenate([jnp.where(low, xp, zero), jnp.where(low, zero, xp)], axis=0)
        xf = xp.astype(jnp.float32)
        sl = slice(j * HEAD_DIM, (j + 2) * HEAD_DIM)
        y_ref[:, sl] = jnp.dot(mix, both, preferred_element_type=jnp.float32) + skip_ref[:, sl] * xf
        carried.append((jnp.where(low, coef[:, j : j + 1], coef[:, j + 1 : j + 2]) * xf).astype(jnp.bfloat16))
    fresh_ref[...] = lax.dot_general(
        b_part, jnp.concatenate(carried, axis=1), (((0,), (0,)), ((), ())), preferred_element_type=jnp.float32
    )


def state_kernel(live_ref, start_ref, y_ref, fresh_ref, c_ref, ecum_ref, elast_ref, y_out_ref, final_ref):
    rows = y_ref.shape[0]
    start = start_ref[...]
    start = jnp.where(live_ref[0] > 0, start, jnp.zeros_like(start))
    low = lax.broadcasted_iota(jnp.int32, (rows, 128), 1) < HEAD_DIM
    ecum = ecum_ref[0]
    ys = jnp.dot(c_ref[...], start, preferred_element_type=jnp.float32)
    for j in range(0, PER_STEP, 2):
        sl = slice(j * HEAD_DIM, (j + 2) * HEAD_DIM)
        factor = jnp.where(low, ecum[:, j : j + 1], ecum[:, j + 1 : j + 2])
        y_out_ref[:, sl] = (y_ref[:, sl] + factor * ys[:, sl]).astype(jnp.bfloat16)
    final_ref[0] = (elast_ref[...] * start.astype(jnp.float32) + fresh_ref[...]).astype(jnp.bfloat16)


def by_step(a):
    return a.reshape(a.shape[0], STEPS, PER_STEP).transpose(1, 0, 2)


LANES = 4
CHUNKS = 8
WIDE = INNER // LANES
CC = WIDE // CHUNKS
PW = 512
TC = WIDE // LANES
DEPTH = 4
EARLY = 2
AHEAD = 2
PACE = 2
TAIL_ROWS = 16
LAG = 4
SETTLE = 4
SETTLE_LIMIT = 60 * 2**20
MESH = pl.DeviceIdType.MESH


def masked_column(row, rows):
    sub = lax.broadcasted_iota(jnp.int32, (rows, 128), 0)
    lane = lax.broadcasted_iota(jnp.int32, (rows, 128), 1)
    return jnp.sum(jnp.where(sub == lane, jnp.broadcast_to(row, (rows, 128)), 0), axis=1, keepdims=True)


def destinations(wanted, n):
    planes = n // LANES
    sub = lax.broadcasted_iota(jnp.int32, (n, 128), 0) // LANES
    lane = lax.broadcasted_iota(jnp.int32, (n, 128), 1)
    hit = wanted == lane
    top = jnp.max(jnp.where(hit, sub, -1), axis=0, keepdims=True)
    low = jnp.min(jnp.where(hit, sub, planes), axis=0, keepdims=True)
    return top, low


def head_terms(dt_ref, dt_bias_ref, a_log_ref, cum_ref, cumt_ref, stept_ref, coef_ref, ecum_ref, elast_ref):
    rows = dt_ref.shape[0]
    step = jax.nn.softplus(dt_ref[...] + dt_bias_ref[...])
    below = (
        lax.broadcasted_iota(jnp.int32, (rows, rows), 0) >= lax.broadcasted_iota(jnp.int32, (rows, rows), 1)
    ).astype(jnp.float32)
    cum = jnp.dot(below, step * (-jnp.exp(a_log_ref[...])), precision=lax.Precision.HIGHEST,
                  preferred_element_type=jnp.float32)
    last = cum[rows - 1 : rows, :]
    cum_ref[...] = cum
    cumt_ref[...] = cum.T
    stept_ref[...] = step.T
    coef_ref[...] = jnp.exp(last - cum) * step
    ecum_ref[...] = jnp.exp(cum)
    elast_ref[...] = jnp.broadcast_to(jnp.exp(last), elast_ref.shape)


def info_kernel(
    groups, n, sizes, owner_ref, slot_ref, spans_ref, request_ref, states_ref, tails_ref,
    dt_ref, dt_bias_ref, a_log_ref,
    table_ref, which_ref, own_out, plane, plane_t, cum_ref, cumt_ref, stept_ref, coef_ref, ecum_ref, elast_ref,
    three, own, own_tail, packed, mine, rows, load_sem, send_sem, recv_sem, spread_s, spread_r, spread_ts, spread_tr,
    out_sem,
):
    planes = n // LANES
    grp, me = lax.axis_index("grp"), lax.axis_index("req")
    total = groups * n
    flat = grp * n + me
    z, l = lax.div(me, LANES), lax.rem(me, LANES)
    loads = []
    for i in range(states_ref.shape[0]):
        load = pltpu.make_async_copy(states_ref.at[i], three.at[i], load_sem.at[i])
        load.start()
        loads.append(load)
    barrier = pltpu.get_barrier_semaphore()

    def other(k):
        to = lax.rem(flat + k, total)
        return lax.div(to, n), lax.rem(to, n)

    for k in range(1, total):
        pl.semaphore_signal(barrier, inc=1, device_id=other(k), device_id_type=MESH)
    request = request_ref[0]
    wanted = jnp.where(spans_ref[request] > 0, owner_ref[request], -1)
    served = jnp.int32(0)
    for r in range(n):
        served = jnp.maximum(served, jnp.where(owner_ref[r] == me, slot_ref[r], 0))
    mine[...] = jnp.full((1, 128), wanted, jnp.int32)
    tail = tails_ref[served].astype(jnp.float32)
    packed[...] = jnp.zeros_like(packed)
    for q in range(-(-tail.shape[1] // WIDE)):
        for p in range(LANES):
            at = q * WIDE + p * TC
            if at < tail.shape[1]:
                packed[p, 3 * q : 3 * q + 3, :] = tail[:, at : at + TC]
    own_tail[...] = packed[...].astype(jnp.bfloat16)
    outs = []

    def put(src, dst):
        copy = pltpu.make_async_copy(src, dst, out_sem.at[len(outs)])
        copy.start()
        outs.append(copy)

    put(own_tail.at[l], plane_t.at[l])
    for load in loads:
        load.wait()

    def take(c):
        for p in range(LANES):
            own[p, c] = three[served, :, p * WIDE + c * CC : p * WIDE + (c + 1) * CC]

    for c in range(EARLY):
        take(c)
        put(own.at[l, c], plane.at[c, l])
    pl.semaphore_wait(barrier, total - 1)
    for k in range(1, total):
        to_grp, to_req = other(k)
        row = lax.rem(grp - to_grp + groups, groups) * n + me
        copy = pltpu.make_async_remote_copy(
            src_ref=mine, dst_ref=rows.at[row], send_sem=send_sem, recv_sem=recv_sem,
            device_id=(to_grp, to_req), device_id_type=MESH,
        )
        copy.start()

    def spread(src, dst, ss, rs, k):
        return pltpu.make_async_remote_copy(
            src_ref=src, dst_ref=dst, send_sem=ss, recv_sem=rs,
            device_id=(grp, z * LANES + lax.rem(l + k, LANES)), device_id_type=MESH,
        )

    spreads = []
    for k in range(1, LANES):
        to, frm = lax.rem(l + k, LANES), lax.rem(l + LANES - k, LANES)
        sems = (spread_ts.at[k - 1], spread_tr.at[k - 1], k)
        spread(own_tail.at[to], plane_t.at[l], *sems).start()
        spreads.append((spread(own_tail.at[to], plane_t.at[l], *sems), spread(own_tail.at[frm], plane_t.at[frm], *sems)))
    for c in range(EARLY):
        for k in range(1, LANES):
            to, frm = lax.rem(l + k, LANES), lax.rem(l + LANES - k, LANES)
            sems = (spread_s.at[c, k - 1], spread_r.at[c, k - 1], k)
            spread(own.at[to, c], plane.at[c, l], *sems).start()
            spreads.append((spread(own.at[to, c], plane.at[c, l], *sems), spread(own.at[frm, c], plane.at[c, frm], *sems)))
    for c in range(EARLY, CHUNKS):
        take(c)
        for p in range(LANES):
            put(own.at[p, c], own_out.at[p, c])
    head_terms(dt_ref, dt_bias_ref, a_log_ref, cum_ref, cumt_ref, stept_ref, coef_ref, ecum_ref, elast_ref)
    everyone = rows.at[pl.ds(0, total - 1)]
    pltpu.make_async_copy(everyone, everyone, send_sem).wait()
    pltpu.make_async_copy(everyone, everyone, recv_sem).wait()
    rows[pl.ds(me, 1)] = mine[...].reshape(1, 1, 128)

    need = jnp.zeros((1, 1), jnp.int32)
    lane_row = lax.broadcasted_iota(jnp.int32, (1, 128), 1)
    home = lane_row // LANES
    for g in range(groups):
        top, low = destinations(rows[g * n : (g + 1) * n].reshape(n, 128), n)
        for cut in range(planes - 1):
            up = jnp.sum(((home <= cut) & (top > cut) & (lane_row < n)).astype(jnp.int32), axis=1, keepdims=True)
            down = jnp.sum(((home > cut) & (low <= cut) & (lane_row < n)).astype(jnp.int32), axis=1, keepdims=True)
            need = jnp.maximum(need, jnp.maximum(up, down))

    wants = rows[0:n].reshape(n, 128)
    top, low = destinations(wants, n)
    sub = lax.broadcasted_iota(jnp.int32, (n, 128), 0)
    lane = lax.broadcasted_iota(jnp.int32, (n, 128), 1)
    wants_row = jnp.sum(jnp.where(sub == lane, wants, 0), axis=0, keepdims=True)
    col = lax.broadcasted_iota(jnp.int32, (n, 1), 0)
    col_home = col // LANES
    top_col, low_col = masked_column(top, n), masked_column(low, n)

    def up_set(where_home, where_top, cut):
        return (where_home <= cut) & (where_top > cut)

    def down_set(where_home, where_low, cut):
        return (where_home > cut) & (where_low <= cut)

    def rank(inside, key_row, key_col):
        ahead = inside & (key_row < key_col) & (lane_row < n)
        return jnp.sum(ahead.astype(jnp.int32), axis=1, keepdims=True)

    up_row, up_col = (planes - top) * n + lane_row, (planes - top_col) * n + col
    down_row, down_col = (low + 1) * n + lane_row, (low_col + 1) * n + col
    up_in = rank(up_set(home, top, z - 1), up_row, up_col)
    up_out = rank(up_set(home, top, z), up_row, up_col)
    down_in = rank(down_set(home, low, z), down_row, down_col)
    down_out = rank(down_set(home, low, z - 1), down_row, down_col)
    near = lax.rem(col, LANES)
    src_up = jnp.where(col_home == z, near, LANES + up_in)
    src_down = jnp.where(col_home == z, near, LANES + down_in)
    src_fin = jnp.where(col_home == z, near, jnp.where(col_home < z, LANES + up_in, LANES + n + down_in))
    sel_up = jnp.sum(jnp.where(up_set(col_home, top_col, z) & (up_out == lane), src_up, 0), axis=0, keepdims=True)
    sel_down = jnp.sum(jnp.where(down_set(col_home, low_col, z - 1) & (down_out == lane), src_down, 0), axis=0, keepdims=True)
    sel_fin = jnp.sum(jnp.where(wants_row == col, src_fin, 0), axis=0, keepdims=True)
    sel_fin = jnp.where(wants_row < 0, -1, sel_fin)
    table_ref[...] = jnp.zeros_like(table_ref)
    table_ref[0:1, :] = sel_up
    table_ref[1:2, :] = sel_down
    table_ref[2:3, :] = sel_fin
    which = jnp.zeros((1, 1), jnp.int32)
    for size in sizes[:-1]:
        which += (need > size).astype(jnp.int32)
    which_ref[...] = which
    for sent, come in spreads:
        sent.wait_send()
        come.wait_recv()
    for copy in outs:
        copy.wait()


def info(
    mesh, sizes, hit_owner, hit_slot, hit_spans, request_of, cache_states, cache_tails, dt_raw, dt_bias, a_log
):
    groups, n = mesh.shape["grp"], mesh.shape["req"]
    smem = pl.BlockSpec(memory_space=pltpu.SMEM)
    vmem = pl.BlockSpec(memory_space=pltpu.VMEM)
    hbm = pl.BlockSpec(memory_space=pl.ANY)
    rows = dt_raw.shape[0]
    bf16 = lambda *shape: jax.ShapeDtypeStruct(shape, jnp.bfloat16)
    f32 = lambda *shape: jax.ShapeDtypeStruct(shape, jnp.float32)
    sem = lambda *shape: [pltpu.SemaphoreType.DMA(shape)] * 2
    return pl.pallas_call(
        functools.partial(info_kernel, groups, n, sizes),
        out_shape=(
            jax.ShapeDtypeStruct((8, 128), jnp.int32),
            jax.ShapeDtypeStruct((1, 1), jnp.int32),
            bf16(LANES, CHUNKS, NST, CC),
            bf16(EARLY, LANES, NST, CC),
            bf16(LANES, TAIL_ROWS, TC),
            f32(rows, HEADS), f32(HEADS, rows), f32(HEADS, rows), f32(rows, HEADS), f32(rows, HEADS), f32(8, HEADS),
        ),
        in_specs=[smem] * 4 + [hbm] + [vmem] * 4,
        out_specs=(vmem, vmem, hbm, hbm, hbm) + (vmem,) * 6,
        scratch_shapes=[
            pltpu.VMEM(cache_states.shape, jnp.bfloat16),
            pltpu.VMEM((LANES, CHUNKS, NST, CC), jnp.bfloat16),
            pltpu.VMEM((LANES, TAIL_ROWS, TC), jnp.bfloat16),
            pltpu.VMEM((LANES, TAIL_ROWS, TC), jnp.float32),
            pltpu.VMEM((1, 128), jnp.int32),
            pltpu.VMEM((groups * n, 1, 128), jnp.int32),
            pltpu.SemaphoreType.DMA((cache_states.shape[0],)),
            pltpu.SemaphoreType.DMA, pltpu.SemaphoreType.DMA,
            *sem(EARLY, LANES - 1), *sem(LANES - 1),
            pltpu.SemaphoreType.DMA((LANES * (CHUNKS - EARLY) + EARLY + 1,)),
        ],
        compiler_params=pltpu.CompilerParams(collective_id=0, has_side_effects=True, vmem_limit_bytes=58 * 2**20),
        name="info",
    )(hit_owner, hit_slot, hit_spans, request_of, cache_states, cache_tails, dt_raw, dt_bias, a_log)


def conv(taps, bias, pad, rows):
    v = jnp.broadcast_to(bias, (rows, bias.shape[1]))
    for k in range(4):
        v = v + taps[k : k + 1, :] * pad[5 + k : 5 + k + rows, :]
    return (v / (1.0 + jnp.exp(-v))).astype(jnp.bfloat16)


def route_kernel(
    n, slots, tab, own, plane_in, plane_t_in,
    cum_ref, cumt_ref, stept_ref, coef_ref, ecum_ref, elast_ref, xbc_ref, weight_ref, bias_ref, skip_ref,
    y_out, final_out,
    start, tail_out, xs, pad, head_pad, tail_rows, scores_ref, y_local, fresh, y_stage, f_stage, y_sem, f_sem,
    skips, plane, plane_t, up_recv, up_recv_t, down_recv, down_recv_t,
    up_send, up_send_t, down_send, down_send_t, fin_send, fin_send_t,
    load_sem, spread_s, spread_r, up_s, up_r, up_ts, up_tr,
    down_s, down_r, down_ts, down_tr, fin_s, fin_r, fin_ts, fin_tr,
):
    planes = n // LANES
    steps = CHUNKS * slots
    grp, me = lax.axis_index("grp"), lax.axis_index("req")
    z, l = lax.div(me, LANES), lax.rem(me, LANES)
    first, last = z == 0, z == planes - 1

    def mate(k):
        return z * LANES + lax.rem(l + k, LANES)

    loads = [
        pltpu.make_async_copy(plane_t_in, plane_t, load_sem.at[0]),
        pltpu.make_async_copy(plane_in, plane.at[pl.ds(0, EARLY)], load_sem.at[1]),
    ]
    for c in range(EARLY, CHUNKS):
        loads.append(pltpu.make_async_copy(own.at[l, c], plane.at[c, l], load_sem.at[2 + c - EARLY]))
    for load in loads:
        load.start()
    barrier = pltpu.get_barrier_semaphore()
    for k in range(1, LANES):
        pl.semaphore_signal(barrier, inc=1, device_id=(grp, mate(k)), device_id_type=MESH)

    @pl.when(jnp.logical_not(first))
    def _():
        pl.semaphore_signal(barrier, inc=1, device_id=(grp, me - LANES), device_id_type=MESH)

    @pl.when(jnp.logical_not(last))
    def _():
        pl.semaphore_signal(barrier, inc=1, device_id=(grp, me + LANES), device_id_type=MESH)

    pl.semaphore_wait(barrier, LANES - 1 + jnp.where(first | last, 1, 2))

    def remote(src, dst, ss, rs, to):
        return pltpu.make_async_remote_copy(
            src_ref=src, dst_ref=dst, send_sem=ss, recv_sem=rs, device_id=(grp, to), device_id_type=MESH
        )

    def spread(c, k):
        to = lax.rem(l + k, LANES)
        return remote(own.at[to, c], plane.at[c, l], spread_s.at[c, k - 1], spread_r.at[c, k - 1], mate(k))

    def spread_from(c, k):
        frm = lax.rem(l + LANES - k, LANES)
        return remote(own.at[frm, c], plane.at[c, frm], spread_s.at[c, k - 1], spread_r.at[c, k - 1], mate(k))

    def up(s):
        return remote(up_send.at[s], up_recv.at[s], up_s.at[s], up_r.at[s], me + LANES)

    def up_tail(s):
        return remote(up_send_t.at[s], up_recv_t.at[s], up_ts.at[s], up_tr.at[s], me + LANES)

    def down(s):
        return remote(down_send.at[s], down_recv.at[s], down_s.at[s], down_r.at[s], me - LANES)

    def down_tail(s):
        return remote(down_send_t.at[s], down_recv_t.at[s], down_ts.at[s], down_tr.at[s], me - LANES)

    def fin(c, k):
        to = lax.rem(l + k, LANES)
        return remote(fin_send.at[c, k - 1], start.at[l, c], fin_s.at[c, k - 1], fin_r.at[c, k - 1], mate(k))

    def fin_from(c, k):
        frm = lax.rem(l + LANES - k, LANES)
        return remote(fin_send.at[c, k - 1], start.at[frm, c], fin_s.at[c, k - 1], fin_r.at[c, k - 1], mate(k))

    def fin_tail(k):
        return remote(fin_send_t.at[k - 1], tail_out.at[l], fin_ts.at[k - 1], fin_tr.at[k - 1], mate(k))

    def fin_tail_from(k):
        frm = lax.rem(l + LANES - k, LANES)
        return remote(fin_send_t.at[k - 1], tail_out.at[frm], fin_ts.at[k - 1], fin_tr.at[k - 1], mate(k))

    for c in range(EARLY, min(EARLY + AHEAD, CHUNKS)):
        for k in range(1, LANES):
            spread(c, k).start()
    rows = xbc_ref.shape[0]
    channels = xbc_ref.shape[1]
    pieces = channels // PW
    scans = INNER // PW
    first_b, first_c = INNER, INNER + GROUPS * NST
    low = lax.broadcasted_iota(jnp.int32, (rows, 128), 1) < HEAD_DIM
    low_n = lax.broadcasted_iota(jnp.int32, (NST, 128), 1) < HEAD_DIM

    def columns(i):
        return pl.ds(pl.multiple_of(i * PW, PW), PW)

    def conv_piece(i):
        at = columns(i)
        pad[0:8, :] = jnp.zeros((8, PW), jnp.float32)
        pad[8 : 8 + rows, :] = xbc_ref[:, at].astype(jnp.float32)
        xs[:, at] = conv(weight_ref[:, at], bias_ref[:, at], pad, rows)

    def head_piece(i, _):
        at = columns(i)
        head_pad[0:8, :] = tail_rows[:, at]
        head_pad[8:24, :] = xbc_ref[0:16, at].astype(jnp.float32)
        xs[0:16, at] = conv(weight_ref[:, at], bias_ref[:, at], head_pad, 16)
        return 0

    def with_tail():
        tail_rows[...] = jnp.zeros_like(tail_rows)
        for p in range(LANES):
            got = tail_out[p].astype(jnp.float32)
            for q in range(-(-channels // WIDE)):
                at = q * WIDE + p * TC
                if at < channels:
                    tail_rows[5:8, at : at + TC] = got[3 * q : 3 * q + 3, :]
        lax.fori_loop(0, pieces, head_piece, 0)
        causal = lax.broadcasted_iota(jnp.int32, (rows, rows), 0) >= lax.broadcasted_iota(jnp.int32, (rows, rows), 1)
        for g in range(GROUPS):
            b = xs[:, first_b + g * NST : first_b + (g + 1) * NST]
            c = xs[:, first_c + g * NST : first_c + (g + 1) * NST]
            scores = lax.dot_general(c, b, (((1,), (1,)), ((), ())), preferred_element_type=jnp.float32)
            scores_ref[g] = jnp.where(causal, scores, 0.0)

    def turned(ref, head):
        return pltpu.roll(ref[...], lax.rem(128 - head, 128), axis=1)

    def scan_piece(p, c):
        i = p * (scans // LANES) + c
        heads = PW // HEAD_DIM
        at = columns(i)
        x = xs[:, at]
        scores = scores_ref[p]
        cum, coef, skip = turned(cum_ref, heads * i), turned(coef_ref, heads * i), turned(skips, heads * i)
        here = pl.ds(pl.multiple_of(i * heads, heads), heads)
        cumt, stept = cumt_ref[here, :], stept_ref[here, :]
        zero = jnp.zeros((rows, 128), jnp.bfloat16)
        ys, carried = [], []
        for j in range(0, heads, 2):
            xp = x[:, j * HEAD_DIM : (j + 2) * HEAD_DIM]
            mixes = []
            for h in (j, j + 1):
                decay = jnp.exp(jnp.minimum(cum[:, h : h + 1] - cumt[h : h + 1, :], 0.0))
                mixes.append((scores * decay * stept[h : h + 1, :]).astype(jnp.bfloat16))
            mix = jnp.concatenate(mixes, axis=1)
            both = jnp.concatenate([jnp.where(low, xp, zero), jnp.where(low, zero, xp)], axis=0)
            xf = xp.astype(jnp.float32)
            d = jnp.where(low[0:1], skip[0:1, j : j + 1], skip[0:1, j + 1 : j + 2])
            ys.append(jnp.dot(mix, both, preferred_element_type=jnp.float32) + d * xf)
            carried.append((jnp.where(low, coef[:, j : j + 1], coef[:, j + 1 : j + 2]) * xf).astype(jnp.bfloat16))
        per = CC // 128
        for u in range(PW // CC):
            y_local[i * (PW // CC) + u] = jnp.concatenate(ys[u * per : (u + 1) * per], axis=1)
        b = xs[:, pl.ds(pl.multiple_of(first_b + p * NST, NST), NST)]
        new = lax.dot_general(
            b, jnp.concatenate(carried, axis=1), (((0,), (0,)), ((), ())), preferred_element_type=jnp.float32
        )
        for u in range(PW // CC):
            fresh[i * (PW // CC) + u] = new[:, u * CC : (u + 1) * CC]

    def outputs(i):
        at = pl.ds(pl.multiple_of(i * CC, CC), CC)
        return (
            pltpu.make_async_copy(y_stage.at[i], y_out.at[:, at], y_sem.at[i]),
            pltpu.make_async_copy(f_stage.at[i], final_out.at[0, :, at], f_sem.at[i]),
        )

    def last_piece(p, c):
        i = p * CHUNKS + c
        held = start[p, c]
        ys = jnp.dot(xs[:, pl.ds(pl.multiple_of(first_c + p * NST, NST), NST)], held,
                     preferred_element_type=jnp.float32)
        heads = CC // HEAD_DIM
        ecum, elast = turned(ecum_ref, heads * i), turned(elast_ref, heads * i)
        for j in range(0, heads, 2):
            sl = slice(j * HEAD_DIM, (j + 2) * HEAD_DIM)
            factor = jnp.where(low, ecum[:, j : j + 1], ecum[:, j + 1 : j + 2])
            y_stage[i, :, sl] = (y_local[i, :, sl] + factor * ys[:, sl]).astype(jnp.bfloat16)
            kept = jnp.where(low_n[0:1], elast[0:1, j : j + 1], elast[0:1, j + 1 : j + 2])
            f_stage[i, :, sl] = (kept * held[:, sl].astype(jnp.float32) + fresh[i, :, sl]).astype(jnp.bfloat16)
        for copy in outputs(i):
            copy.start()

    def last_chunk(c):
        for k in range(1, LANES):
            fin_from(c, k).wait_recv()

        def one(p, _):
            last_piece(p, c)
            return 0

        lax.fori_loop(0, LANES, one, 0)

    ready = slots + LAG * (planes - 1)
    total = steps + LAG * (planes - 1)
    per_conv = -(-pieces // ready)
    per_scan = -(-scans // (total - ready - 1))

    lead = -(-LANES // per_scan)

    def compute(t):
        @pl.when(t < ready)
        def _():
            def one(u, _):
                i = t * per_conv + u

                @pl.when(i < pieces)
                def _():
                    conv_piece(i)

                return 0

            lax.fori_loop(0, per_conv, one, 0)

        @pl.when(t == ready)
        def _():
            for k in range(1, LANES):
                fin_tail_from(k).wait_recv()
            with_tail()

        @pl.when(t > ready)
        def _():
            def one(u, _):
                i = (t - ready - 1) * per_scan + u

                @pl.when(i < scans)
                def _():
                    scan_piece(lax.rem(i, LANES), lax.div(i, LANES))

                return 0

            lax.fori_loop(0, per_scan, one, 0)
            since = t - ready - lead

            @pl.when((since >= 0) & (lax.rem(jnp.maximum(since, 0), slots) == 0))
            def _():
                last_chunk(lax.div(since, slots))

    def fill(dst, at, sel, near, c, far, base, j, inner):
        value = near[c, 0]
        for p in range(1, LANES):
            value = lax.select_n(sel == p, value, near[c, p])
        dst[at] = value

        @pl.when(inner)
        def _():
            def one(i, _):
                dst[at] = lax.select_n(sel == LANES + i, dst[at], far[base + i])
                return 0

            lax.fori_loop(0, j + 1, one, 0)

    def fill_tail(dst, j, sel, far, inner):
        value = plane_t[0]
        for p in range(1, LANES):
            value = lax.select_n(sel == p, value, plane_t[p])
        dst[j] = value

        @pl.when(inner)
        def _():
            def one(i, _):
                dst[j] = lax.select_n(sel == LANES + i, dst[j], far[i])
                return 0

            lax.fori_loop(0, j + 1, one, 0)

    def tick(t, _):
        tp = t - LAG * jnp.minimum(z, planes - 1 - z)

        @pl.when((tp >= 0) & (tp < steps) & (lax.rem(jnp.maximum(tp, 0), slots) == 0))
        def _():
            c = lax.div(tp, slots)

            @pl.when(c >= EARLY)
            def _():
                for k in range(1, LANES):
                    spread_from(c, k).wait_recv()

        more = EARLY + AHEAD + lax.div(t, PACE)

        @pl.when((more < CHUNKS) & (lax.rem(t, PACE) == 0))
        def _():
            for k in range(1, LANES):
                spread(more, k).start()

        def along(s, row, edge_in, edge_out, copy, copy_tail, send, send_t, recv, recv_t):
            @pl.when((s >= 0) & (s < steps))
            def _():
                c, j = lax.div(s, slots), lax.rem(s, slots)
                inner = jnp.logical_not(edge_in)

                @pl.when(inner)
                def _():
                    @pl.when(c == 0)
                    def _():
                        copy_tail(j).wait_recv()

                    copy(s).wait_recv()

                @pl.when(jnp.logical_not(edge_out))
                def _():
                    sel = tab[row, j]

                    @pl.when(c == 0)
                    def _():
                        fill_tail(send_t, j, sel, recv_t, inner)
                        copy_tail(j).start()

                    fill(send, s, sel, plane, c, recv, c * slots, j, inner)

                    @pl.when(s >= DEPTH)
                    def _():
                        copy(s - DEPTH).wait_send()

                    copy(s).start()

        along(t - LAG * z, 0, first, last, up, up_tail, up_send, up_send_t, up_recv, up_recv_t)
        along(t - LAG * (planes - 1 - z), 1, last, first, down, down_tail, down_send, down_send_t, down_recv, down_recv_t)

        tf = t - LAG * jnp.maximum(z, planes - 1 - z)

        @pl.when((tf >= 0) & (tf < steps) & (lax.rem(jnp.maximum(tf, 0), slots) == slots - 1))
        def _():
            c = lax.div(tf, slots)
            sels = [tab[2, mate(k)] for k in range(LANES)]

            def choose(near, far_up, far_down, write, read):
                acc = [jnp.zeros(near(0).shape, jnp.bfloat16)] * LANES
                for p in range(LANES):
                    value = near(p)
                    acc = [lax.select_n(sel == p, a, value) for sel, a in zip(sels, acc)]
                for k in range(LANES):
                    write(k, acc[k])

                def far(get, base):
                    acc = [read(k) for k in range(LANES)]
                    for i in range(slots):
                        value = get(i)
                        acc = [lax.select_n(sel == base + i, a, value) for sel, a in zip(sels, acc)]
                    for k in range(LANES):
                        write(k, acc[k])

                @pl.when(jnp.logical_not(first))
                def _():
                    far(far_up, LANES)

                @pl.when(jnp.logical_not(last))
                def _():
                    far(far_down, LANES + n)

            def rows_of(b, _):
                at = pl.ds(pl.multiple_of(b * 16, 16), 16)

                def write(k, v):
                    if k == 0:
                        start[l, c, at] = v
                    else:
                        fin_send[c, k - 1, at] = v

                def read(k):
                    return start[l, c, at] if k == 0 else fin_send[c, k - 1, at]

                choose(lambda p: plane[c, p, at], lambda i: up_recv[c * slots + i, at],
                       lambda i: down_recv[c * slots + i, at], write, read)
                return 0

            lax.fori_loop(0, NST // 16, rows_of, 0)
            for k in range(1, LANES):
                fin(c, k).start()

            @pl.when(c == 0)
            def _():
                def write(k, v):
                    if k == 0:
                        tail_out[l] = v
                    else:
                        fin_send_t[k - 1] = v

                def read(k):
                    return tail_out[l] if k == 0 else fin_send_t[k - 1]

                choose(lambda p: plane_t[p], lambda i: up_recv_t[i], lambda i: down_recv_t[i], write, read)
                for k in range(1, LANES):
                    fin_tail(k).start()

        compute(t)
        return 0

    skips[...] = jnp.broadcast_to(skip_ref[...], skips.shape)
    for load in loads:
        load.wait()
    lax.fori_loop(0, total, tick, 0)
    for c in range((total - 1 - ready - lead) // slots + 1, CHUNKS):
        last_chunk(c)

    for k in range(1, LANES):
        fin_tail(k).wait_send()
        for c in range(CHUNKS):
            if c >= EARLY:
                spread(c, k).wait_send()
            fin(c, k).wait_send()

    @pl.when(jnp.logical_not(last))
    def _():
        for j in range(slots):
            up_tail(j).wait_send()
        for s in range(max(steps - DEPTH, 0), steps):
            up(s).wait_send()

    @pl.when(jnp.logical_not(first))
    def _():
        for j in range(slots):
            down_tail(j).wait_send()
        for s in range(max(steps - DEPTH, 0), steps):
            down(s).wait_send()

    for i in range(LANES * CHUNKS):
        for copy in outputs(i):
            copy.wait()


def route(n, slots, number, table, own, plane, plane_t, terms, xbc, weight, bias, skip):
    steps = CHUNKS * slots
    rows, channels = xbc.shape
    pieces = LANES * CHUNKS
    f32 = lambda *shape: pltpu.VMEM(shape, jnp.float32)
    big = lambda *lead: pltpu.VMEM(lead + (NST, CC), jnp.bfloat16)
    small = lambda *lead: pltpu.VMEM(lead + (TAIL_ROWS, TC), jnp.bfloat16)
    sem = lambda *shape: [pltpu.SemaphoreType.DMA(shape)] * 2
    vmem = pl.BlockSpec(memory_space=pltpu.VMEM)
    hbm = pl.BlockSpec(memory_space=pl.ANY)
    return pl.pallas_call(
        functools.partial(route_kernel, n, slots),
        out_shape=(
            jax.ShapeDtypeStruct((rows, INNER), jnp.bfloat16),
            jax.ShapeDtypeStruct((1, NST, INNER), jnp.bfloat16),
        ),
        in_specs=[pl.BlockSpec(memory_space=pltpu.SMEM)] + [hbm] * 3 + [vmem] * 10,
        out_specs=(hbm, hbm),
        scratch_shapes=[
            big(LANES, CHUNKS), small(LANES),
            pltpu.VMEM((rows, channels), jnp.bfloat16), f32(8 + rows, PW), f32(24, PW), f32(8, channels),
            f32(GROUPS, rows, rows), f32(pieces, rows, CC), f32(pieces, NST, CC),
            pltpu.VMEM((pieces, rows, CC), jnp.bfloat16), big(pieces), *sem(pieces),
            f32(8, HEADS), big(CHUNKS, LANES), small(LANES),
            big(steps), small(slots), big(steps), small(slots),
            big(steps), small(slots), big(steps), small(slots),
            big(CHUNKS, LANES - 1), small(LANES - 1),
            pltpu.SemaphoreType.DMA((2 + CHUNKS - EARLY,)),
            *sem(CHUNKS, LANES - 1),
            *sem(steps), *sem(slots), *sem(steps), *sem(slots),
            *sem(CHUNKS, LANES - 1), *sem(LANES - 1),
        ],
        compiler_params=pltpu.CompilerParams(
            collective_id=number, has_side_effects=True, vmem_limit_bytes=(34 + 2 * slots) * 2**20
        ),
        name=f"route{slots}",
    )(table, own, plane, plane_t, *terms, xbc, weight, bias, skip)


def settle_kernel(y_ref, f_ref, y_out, f_out, y_held, f_held, in_sem, out_sem):
    pieces = []
    for i in range(SETTLE):
        at = pl.ds(i * (y_ref.shape[0] // SETTLE), y_ref.shape[0] // SETTLE)
        pieces.append((y_ref.at[at], y_held.at[at], y_out.at[at]))
        at = pl.ds(i * (NST // SETTLE), NST // SETTLE)
        pieces.append((f_ref.at[0, at], f_held.at[at], f_out.at[0, at]))
    come = [pltpu.make_async_copy(a, b, in_sem.at[i]) for i, (a, b, _) in enumerate(pieces)]
    go = [pltpu.make_async_copy(b, c, out_sem.at[i]) for i, (_, b, c) in enumerate(pieces)]
    for copy in come:
        copy.start()
    for first, second in zip(come, go):
        first.wait()
        second.start()
    for copy in go:
        copy.wait()


def settle(y, final):
    hbm = pl.BlockSpec(memory_space=pl.ANY)
    return pl.pallas_call(
        settle_kernel,
        out_shape=(jax.ShapeDtypeStruct(y.shape, y.dtype), jax.ShapeDtypeStruct(final.shape, final.dtype)),
        in_specs=[hbm, hbm],
        out_specs=(hbm, hbm),
        scratch_shapes=[
            pltpu.VMEM(y.shape, y.dtype), pltpu.VMEM(final.shape[1:], final.dtype),
            pltpu.SemaphoreType.DMA((2 * SETTLE,)), pltpu.SemaphoreType.DMA((2 * SETTLE,)),
        ],
        compiler_params=pltpu.CompilerParams(vmem_limit_bytes=SETTLE_LIMIT),
        name="settle",
    )(y, final)


def local_routed(
    mesh, xbc, dt_raw, conv_weight, conv_bias, dt_bias, a_log, d_skip, cache_states, cache_tails,
    hit_owner, hit_slot, hit_spans, request_of,
):
    n = mesh.shape["req"]
    sizes = [3, 4, 5, n // 2]
    table, which, own, plane, plane_t, *terms = info(
        mesh, sizes, hit_owner, hit_slot, hit_spans, request_of, cache_states, cache_tails,
        dt_raw, dt_bias[None], a_log[None],
    )
    return settle(*lax.switch(
        which[0, 0],
        [functools.partial(route, n, size, 1 + i) for i, size in enumerate(sizes)],
        table, own, plane, plane_t, terms, xbc, conv_weight, conv_bias[None], d_skip[None],
    ))


def local(
    xbc, dt_raw, conv_weight, conv_bias, dt_bias, a_log, d_skip, cache_states, cache_tails,
    hit_owner, hit_slot, hit_spans, request_of,
):
    count = hit_owner.shape[0]
    rows = xbc.shape[0]
    mine = request_of[0]
    live = (hit_spans[mine] > 0).astype(jnp.int32)
    device = lax.axis_index("req")
    served = jnp.max(jnp.where(hit_owner == device, hit_slot, 0))
    send = lax.dynamic_slice_in_dim(cache_states, served, 1, 0).reshape(count, NST // count, INNER)
    number = jnp.broadcast_to(mine.astype(send.dtype), send.shape[:2] + (128,))
    parts = lax.all_to_all(
        jnp.concatenate([send, number], axis=2), "req", split_axis=0, concat_axis=0, tiled=True
    )
    every_request = parts[:, 0, INNER].astype(jnp.int32)
    own_tail = lax.dynamic_slice_in_dim(cache_tails, served, 1, 0)
    own_tail = jnp.pad(own_tail, ((0, 0), (0, 1), (0, 0)))
    every_tail = lax.all_gather(own_tail, "req", axis=0, tiled=True)[:, :3]
    owners = jnp.sum(
        jnp.where(every_request[:, None] == jnp.arange(count)[None, :], hit_owner[None, :], 0), axis=1
    )
    chosen = pick(parts, owners)
    start = lax.all_to_all(chosen, "req", split_axis=0, concat_axis=0, tiled=True).reshape(NST, INNER)

    tail = lax.dynamic_index_in_dim(every_tail, hit_owner[mine], 0, keepdims=False)
    tail = jnp.where(live > 0, tail, jnp.zeros_like(tail)).astype(jnp.float32)
    tail = jnp.pad(tail, ((5, 0), (0, 0)))
    step = jax.nn.softplus(dt_raw + dt_bias[None, :])
    below = jnp.tril(jnp.ones((rows, rows), jnp.float32))
    cum = jnp.dot(below, step * (-jnp.exp(a_log))[None, :], precision=lax.Precision.HIGHEST)
    last = cum[rows - 1]
    coef = jnp.exp(last[None, :] - cum) * step
    skip = jnp.repeat(d_skip, HEAD_DIM)[None, :]
    elast = jnp.repeat(jnp.exp(last), HEAD_DIM)[None, :]
    cumt = cum.T.reshape(STEPS, PER_STEP, rows)
    stept = step.T.reshape(STEPS, PER_STEP, rows)
    bias = conv_bias[None, :]

    first_b, first_c = INNER // NST, INNER // NST + GROUPS
    per = STEPS_PER_GROUP
    triple = lambda r: [
        pl.BlockSpec((r, COLS), lambda i: (0, i)),
        pl.BlockSpec((r, NST), lambda i: (0, first_b + i // per)),
        pl.BlockSpec((r, NST), lambda i: (0, first_c + i // per)),
    ]
    wide = lambda r: pl.BlockSpec((r, COLS), lambda i: (0, i))
    tall = pl.BlockSpec((1, rows, PER_STEP), lambda i: (i, 0, 0))
    flat = pl.BlockSpec((1, PER_STEP, rows), lambda i: (i, 0, 0))
    group = pl.BlockSpec((rows, NST), lambda i: (0, i // per))
    y_local, fresh, c_part = pl.pallas_call(
        local_kernel,
        grid=(STEPS,),
        out_shape=(
            jax.ShapeDtypeStruct((rows, INNER), jnp.float32),
            jax.ShapeDtypeStruct((NST, INNER), jnp.float32),
            jax.ShapeDtypeStruct((rows, GROUPS * NST), jnp.bfloat16),
        ),
        in_specs=triple(rows) + triple(8) + triple(4) + triple(1) + [tall, flat, flat, tall, wide(1)],
        out_specs=(wide(rows), wide(NST), group),
        scratch_shapes=[pltpu.VMEM((8 + rows, COLS), jnp.float32)],
        compiler_params=pltpu.CompilerParams(vmem_limit_bytes=58 * 2**20),
        cost_estimate=pl.CostEstimate(flops=10**9, bytes_accessed=40 * 10**6, transcendentals=4 * 10**6),
        name="local",
    )(xbc, xbc, xbc, tail, tail, tail, conv_weight, conv_weight, conv_weight, bias, bias, bias,
      by_step(cum), cumt, stept, by_step(coef), skip)

    return pl.pallas_call(
        state_kernel,
        grid=(STEPS,),
        out_shape=(
            jax.ShapeDtypeStruct((rows, INNER), jnp.bfloat16),
            jax.ShapeDtypeStruct((1, NST, INNER), jnp.bfloat16),
        ),
        in_specs=[pl.BlockSpec(memory_space=pltpu.SMEM), wide(NST), wide(rows), wide(NST), group, tall, wide(1)],
        out_specs=(wide(rows), pl.BlockSpec((1, NST, COLS), lambda i: (0, 0, i))),
        compiler_params=pltpu.CompilerParams(vmem_limit_bytes=58 * 2**20),
        name="state",
    )(live[None], start, y_local, fresh, c_part, by_step(jnp.exp(cum)), elast)


def solution(mesh):
    rows = P(("grp", "req"), None)
    slots = P(("grp", "req"), None, None)
    in_specs = (
        rows, rows, P(), P(), P(), P(), P(), slots, slots, P("grp"), P("grp"), P("grp"), P(("grp", "req")),
    )
    body = functools.partial(local_routed, mesh) if mesh.shape["req"] == 16 else local
    return jax.shard_map(body, mesh=mesh, in_specs=in_specs, out_specs=(rows, slots), check_vma=False)
```

```python
import functools

import jax
import jax.numpy as jnp
from jax import lax
from jax.experimental import pallas as pl
from jax.experimental.pallas import tpu as pltpu
from jax.sharding import PartitionSpec as P

HEADS = 128
HEAD_DIM = 64
GROUPS = 4
NST = 128
INNER = 8192
PER_STEP = 16
COLS = PER_STEP * HEAD_DIM
STEPS = HEADS // PER_STEP
STEPS_PER_GROUP = STEPS // GROUPS


def pick_kernel(index_ref, parts_ref, out_ref, sem):
    count = out_ref.shape[0]
    copies = []
    for i in range(count):
        copy = pltpu.make_async_copy(parts_ref.at[index_ref[i], :, pl.ds(0, INNER)], out_ref.at[i], sem.at[i])
        copy.start()
        copies.append(copy)
    for copy in copies:
        copy.wait()


def pick(parts, index):
    count = index.shape[0]
    return pl.pallas_call(
        pick_kernel,
        out_shape=jax.ShapeDtypeStruct((count, parts.shape[1], INNER), parts.dtype),
        in_specs=[pl.BlockSpec(memory_space=pltpu.SMEM), pl.BlockSpec(memory_space=pltpu.VMEM)],
        out_specs=pl.BlockSpec(memory_space=pl.ANY),
        scratch_shapes=[pltpu.SemaphoreType.DMA((count,))],
        compiler_params=pltpu.CompilerParams(vmem_limit_bytes=8 * 2**20),
        name="pick",
    )(index, parts)


def conv_block(pad, x_ref, tail_ref, w_ref, b_ref, width):
    rows = x_ref.shape[0]
    pad[0:8, 0:width] = tail_ref[...]
    pad[8 : 8 + rows, 0:width] = x_ref[...].astype(jnp.float32)
    v = jnp.broadcast_to(b_ref[...], (rows, width))
    for k in range(4):
        v = v + w_ref[k : k + 1, :] * pad[5 + k : 5 + k + rows, 0:width]
    return (v / (1.0 + jnp.exp(-v))).astype(jnp.bfloat16)


def local_kernel(
    x_ref, xb_ref, xc_ref, tx_ref, tb_ref, tc_ref, wx_ref, wb_ref, wc_ref, bx_ref, bb_ref, bc_ref,
    cum_ref, cumt_ref, stept_ref, coef_ref, skip_ref,
    y_ref, fresh_ref, c_out_ref, pad,
):
    rows = x_ref.shape[0]
    b_part = conv_block(pad, xb_ref, tb_ref, wb_ref, bb_ref, NST)
    c_part = conv_block(pad, xc_ref, tc_ref, wc_ref, bc_ref, NST)
    c_out_ref[...] = c_part
    x = conv_block(pad, x_ref, tx_ref, wx_ref, bx_ref, COLS)
    scores = lax.dot_general(c_part, b_part, (((1,), (1,)), ((), ())), preferred_element_type=jnp.float32)
    causal = lax.broadcasted_iota(jnp.int32, (rows, rows), 0) >= lax.broadcasted_iota(jnp.int32, (rows, rows), 1)
    scores = jnp.where(causal, scores, 0.0)
    low = lax.broadcasted_iota(jnp.int32, (rows, 128), 1) < HEAD_DIM
    cum = cum_ref[0]
    coef = coef_ref[0]
    zero = jnp.zeros((rows, 128), jnp.bfloat16)
    carried = []
    for j in range(0, PER_STEP, 2):
        xp = x[:, j * HEAD_DIM : (j + 2) * HEAD_DIM]
        mixes = []
        for h in (j, j + 1):
            decay = jnp.exp(jnp.minimum(cum[:, h : h + 1] - cumt_ref[0, h : h + 1, :], 0.0))
            mixes.append((scores * decay * stept_ref[0, h : h + 1, :]).astype(jnp.bfloat16))
        mix = jnp.concatenate(mixes, axis=1)
        both = jnp.concatenate([jnp.where(low, xp, zero), jnp.where(low, zero, xp)], axis=0)
        xf = xp.astype(jnp.float32)
        sl = slice(j * HEAD_DIM, (j + 2) * HEAD_DIM)
        y_ref[:, sl] = jnp.dot(mix, both, preferred_element_type=jnp.float32) + skip_ref[:, sl] * xf
        carried.append((jnp.where(low, coef[:, j : j + 1], coef[:, j + 1 : j + 2]) * xf).astype(jnp.bfloat16))
    fresh_ref[...] = lax.dot_general(
        b_part, jnp.concatenate(carried, axis=1), (((0,), (0,)), ((), ())), preferred_element_type=jnp.float32
    )


def state_kernel(live_ref, start_ref, y_ref, fresh_ref, c_ref, ecum_ref, elast_ref, y_out_ref, final_ref):
    rows = y_ref.shape[0]
    start = start_ref[...]
    start = jnp.where(live_ref[0] > 0, start, jnp.zeros_like(start))
    low = lax.broadcasted_iota(jnp.int32, (rows, 128), 1) < HEAD_DIM
    ecum = ecum_ref[0]
    ys = jnp.dot(c_ref[...], start, preferred_element_type=jnp.float32)
    for j in range(0, PER_STEP, 2):
        sl = slice(j * HEAD_DIM, (j + 2) * HEAD_DIM)
        factor = jnp.where(low, ecum[:, j : j + 1], ecum[:, j + 1 : j + 2])
        y_out_ref[:, sl] = (y_ref[:, sl] + factor * ys[:, sl]).astype(jnp.bfloat16)
    final_ref[0] = (elast_ref[...] * start.astype(jnp.float32) + fresh_ref[...]).astype(jnp.bfloat16)


def by_step(a):
    return a.reshape(a.shape[0], STEPS, PER_STEP).transpose(1, 0, 2)


LANES = 4
CHUNKS = 8
WIDE = INNER // LANES
CC = WIDE // CHUNKS
PW = 512
TC = WIDE // LANES
DEPTH = 4
EARLY = 2
AHEAD = 1
PACE = 3
TAIL_ROWS = 16
LAG = 4
SETTLE = 4
SETTLE_LIMIT = 60 * 2**20
MESH = pl.DeviceIdType.MESH


def masked_column(row, rows):
    sub = lax.broadcasted_iota(jnp.int32, (rows, 128), 0)
    lane = lax.broadcasted_iota(jnp.int32, (rows, 128), 1)
    return jnp.sum(jnp.where(sub == lane, jnp.broadcast_to(row, (rows, 128)), 0), axis=1, keepdims=True)


def destinations(wanted, n):
    planes = n // LANES
    sub = lax.broadcasted_iota(jnp.int32, (n, 128), 0) // LANES
    lane = lax.broadcasted_iota(jnp.int32, (n, 128), 1)
    hit = wanted == lane
    top = jnp.max(jnp.where(hit, sub, -1), axis=0, keepdims=True)
    low = jnp.min(jnp.where(hit, sub, planes), axis=0, keepdims=True)
    return top, low


def head_terms(dt_ref, dt_bias_ref, a_log_ref, cum_ref, cumt_ref, stept_ref, coef_ref, ecum_ref, elast_ref):
    rows = dt_ref.shape[0]
    step = jax.nn.softplus(dt_ref[...] + dt_bias_ref[...])
    below = (
        lax.broadcasted_iota(jnp.int32, (rows, rows), 0) >= lax.broadcasted_iota(jnp.int32, (rows, rows), 1)
    ).astype(jnp.float32)
    cum = jnp.dot(below, step * (-jnp.exp(a_log_ref[...])), precision=lax.Precision.HIGHEST,
                  preferred_element_type=jnp.float32)
    last = cum[rows - 1 : rows, :]
    cum_ref[...] = cum
    cumt_ref[...] = cum.T
    stept_ref[...] = step.T
    coef_ref[...] = jnp.exp(last - cum) * step
    ecum_ref[...] = jnp.exp(cum)
    elast_ref[...] = jnp.broadcast_to(jnp.exp(last), elast_ref.shape)


def info_kernel(
    groups, n, sizes, owner_ref, slot_ref, spans_ref, request_ref, states_ref, tails_ref,
    dt_ref, dt_bias_ref, a_log_ref,
    table_ref, which_ref, own_out, plane, plane_t, cum_ref, cumt_ref, stept_ref, coef_ref, ecum_ref, elast_ref,
    three, own, own_tail, packed, mine, rows, load_sem, send_sem, recv_sem, spread_s, spread_r, spread_ts, spread_tr,
    out_sem, needs, need_s, need_r,
):
    planes = n // LANES
    grp, me = lax.axis_index("grp"), lax.axis_index("req")
    z, l = lax.div(me, LANES), lax.rem(me, LANES)
    loads = []
    for i in range(states_ref.shape[0]):
        load = pltpu.make_async_copy(states_ref.at[i], three.at[i], load_sem.at[i])
        load.start()
        loads.append(load)
    barrier = pltpu.get_barrier_semaphore()

    def other(k):
        return grp, lax.rem(me + k, n)

    def counterpart(k):
        return lax.rem(grp + k, groups), me

    for k in range(1, n):
        pl.semaphore_signal(barrier, inc=1, device_id=other(k), device_id_type=MESH)
    for k in range(1, groups):
        pl.semaphore_signal(barrier, inc=1, device_id=counterpart(k), device_id_type=MESH)
    request = request_ref[0]
    wanted = jnp.where(spans_ref[request] > 0, owner_ref[request], -1)
    served = jnp.int32(0)
    for r in range(n):
        served = jnp.maximum(served, jnp.where(owner_ref[r] == me, slot_ref[r], 0))
    mine[...] = jnp.full((1, 128), wanted, jnp.int32)
    tail = tails_ref[served].astype(jnp.float32)
    packed[...] = jnp.zeros_like(packed)
    for q in range(-(-tail.shape[1] // WIDE)):
        for p in range(LANES):
            at = q * WIDE + p * TC
            if at < tail.shape[1]:
                packed[p, 3 * q : 3 * q + 3, :] = tail[:, at : at + TC]
    own_tail[...] = packed[...].astype(jnp.bfloat16)
    outs = []

    def put(src, dst):
        copy = pltpu.make_async_copy(src, dst, out_sem.at[len(outs)])
        copy.start()
        outs.append(copy)

    put(own_tail.at[l], plane_t.at[l])
    for load in loads:
        load.wait()

    def take(c):
        for p in range(LANES):
            own[p, c] = three[served, :, p * WIDE + c * CC : p * WIDE + (c + 1) * CC]

    for c in range(EARLY):
        take(c)
        put(own.at[l, c], plane.at[c, l])
    pl.semaphore_wait(barrier, n + groups - 2)
    for k in range(1, n):
        pltpu.make_async_remote_copy(
            src_ref=mine, dst_ref=rows.at[me], send_sem=send_sem, recv_sem=recv_sem,
            device_id=other(k), device_id_type=MESH,
        ).start()

    def spread(src, dst, ss, rs, k):
        return pltpu.make_async_remote_copy(
            src_ref=src, dst_ref=dst, send_sem=ss, recv_sem=rs,
            device_id=(grp, z * LANES + lax.rem(l + k, LANES)), device_id_type=MESH,
        )

    spreads = []
    for k in range(1, LANES):
        to, frm = lax.rem(l + k, LANES), lax.rem(l + LANES - k, LANES)
        sems = (spread_ts.at[k - 1], spread_tr.at[k - 1], k)
        spread(own_tail.at[to], plane_t.at[l], *sems).start()
        spreads.append((spread(own_tail.at[to], plane_t.at[l], *sems), spread(own_tail.at[frm], plane_t.at[frm], *sems)))
    for c in range(EARLY):
        for k in range(1, LANES):
            to, frm = lax.rem(l + k, LANES), lax.rem(l + LANES - k, LANES)
            sems = (spread_s.at[c, k - 1], spread_r.at[c, k - 1], k)
            spread(own.at[to, c], plane.at[c, l], *sems).start()
            spreads.append((spread(own.at[to, c], plane.at[c, l], *sems), spread(own.at[frm, c], plane.at[c, frm], *sems)))
    for c in range(EARLY, CHUNKS):
        take(c)
        for p in range(LANES):
            put(own.at[p, c], own_out.at[p, c])
    head_terms(dt_ref, dt_bias_ref, a_log_ref, cum_ref, cumt_ref, stept_ref, coef_ref, ecum_ref, elast_ref)
    everyone = rows.at[pl.ds(0, n - 1)]
    pltpu.make_async_copy(everyone, everyone, send_sem).wait()
    pltpu.make_async_copy(everyone, everyone, recv_sem).wait()
    rows[pl.ds(me, 1)] = mine[...].reshape(1, 1, 128)

    need = jnp.zeros((1, 1), jnp.int32)
    lane_row = lax.broadcasted_iota(jnp.int32, (1, 128), 1)
    home = lane_row // LANES
    wants = rows[0:n].reshape(n, 128)
    top, low = destinations(wants, n)
    for cut in range(planes - 1):
        up = jnp.sum(((home <= cut) & (top > cut) & (lane_row < n)).astype(jnp.int32), axis=1, keepdims=True)
        down = jnp.sum(((home > cut) & (low <= cut) & (lane_row < n)).astype(jnp.int32), axis=1, keepdims=True)
        need = jnp.maximum(need, jnp.maximum(up, down))
    needs[0] = jnp.broadcast_to(need, (1, 128))
    swaps = []
    for k in range(1, groups):
        swap = pltpu.make_async_remote_copy(
            src_ref=needs.at[0], dst_ref=needs.at[k], send_sem=need_s.at[k], recv_sem=need_r.at[k],
            device_id=counterpart(k), device_id_type=MESH,
        )
        swap.start()
        swaps.append(swap)

    sub = lax.broadcasted_iota(jnp.int32, (n, 128), 0)
    lane = lax.broadcasted_iota(jnp.int32, (n, 128), 1)
    wants_row = jnp.sum(jnp.where(sub == lane, wants, 0), axis=0, keepdims=True)
    col = lax.broadcasted_iota(jnp.int32, (n, 1), 0)
    col_home = col // LANES
    top_col, low_col = masked_column(top, n), masked_column(low, n)

    def up_set(where_home, where_top, cut):
        return (where_home <= cut) & (where_top > cut)

    def down_set(where_home, where_low, cut):
        return (where_home > cut) & (where_low <= cut)

    def rank(inside, key_row, key_col):
        ahead = inside & (key_row < key_col) & (lane_row < n)
        return jnp.sum(ahead.astype(jnp.int32), axis=1, keepdims=True)

    up_row, up_col = (planes - top) * n + lane_row, (planes - top_col) * n + col
    down_row, down_col = (low + 1) * n + lane_row, (low_col + 1) * n + col
    up_in = rank(up_set(home, top, z - 1), up_row, up_col)
    up_out = rank(up_set(home, top, z), up_row, up_col)
    down_in = rank(down_set(home, low, z), down_row, down_col)
    down_out = rank(down_set(home, low, z - 1), down_row, down_col)
    near = lax.rem(col, LANES)
    src_up = jnp.where(col_home == z, near, LANES + up_in)
    src_down = jnp.where(col_home == z, near, LANES + down_in)
    src_fin = jnp.where(col_home == z, near, jnp.where(col_home < z, LANES + up_in, LANES + n + down_in))
    sel_up = jnp.sum(jnp.where(up_set(col_home, top_col, z) & (up_out == lane), src_up, 0), axis=0, keepdims=True)
    sel_down = jnp.sum(jnp.where(down_set(col_home, low_col, z - 1) & (down_out == lane), src_down, 0), axis=0, keepdims=True)
    sel_fin = jnp.sum(jnp.where(wants_row == col, src_fin, 0), axis=0, keepdims=True)
    sel_fin = jnp.where(wants_row < 0, -1, sel_fin)
    table_ref[...] = jnp.zeros_like(table_ref)
    table_ref[0:1, :] = sel_up
    table_ref[1:2, :] = sel_down
    table_ref[2:3, :] = sel_fin
    for swap in swaps:
        swap.wait()
    for k in range(1, groups):
        need = jnp.maximum(need, needs[k][:, 0:1])
    which = jnp.zeros((1, 1), jnp.int32)
    for size in sizes[:-1]:
        which += (need > size).astype(jnp.int32)
    which_ref[...] = which
    for sent, come in spreads:
        sent.wait_send()
        come.wait_recv()
    for copy in outs:
        copy.wait()


def info(
    mesh, sizes, hit_owner, hit_slot, hit_spans, request_of, cache_states, cache_tails, dt_raw, dt_bias, a_log
):
    groups, n = mesh.shape["grp"], mesh.shape["req"]
    smem = pl.BlockSpec(memory_space=pltpu.SMEM)
    vmem = pl.BlockSpec(memory_space=pltpu.VMEM)
    hbm = pl.BlockSpec(memory_space=pl.ANY)
    rows = dt_raw.shape[0]
    bf16 = lambda *shape: jax.ShapeDtypeStruct(shape, jnp.bfloat16)
    f32 = lambda *shape: jax.ShapeDtypeStruct(shape, jnp.float32)
    sem = lambda *shape: [pltpu.SemaphoreType.DMA(shape)] * 2
    return pl.pallas_call(
        functools.partial(info_kernel, groups, n, sizes),
        out_shape=(
            jax.ShapeDtypeStruct((8, 128), jnp.int32),
            jax.ShapeDtypeStruct((1, 1), jnp.int32),
            bf16(LANES, CHUNKS, NST, CC),
            bf16(EARLY, LANES, NST, CC),
            bf16(LANES, TAIL_ROWS, TC),
            f32(rows, HEADS), f32(HEADS, rows), f32(HEADS, rows), f32(rows, HEADS), f32(rows, HEADS), f32(8, HEADS),
        ),
        in_specs=[smem] * 4 + [hbm] + [vmem] * 4,
        out_specs=(vmem, vmem, hbm, hbm, hbm) + (vmem,) * 6,
        scratch_shapes=[
            pltpu.VMEM(cache_states.shape, jnp.bfloat16),
            pltpu.VMEM((LANES, CHUNKS, NST, CC), jnp.bfloat16),
            pltpu.VMEM((LANES, TAIL_ROWS, TC), jnp.bfloat16),
            pltpu.VMEM((LANES, TAIL_ROWS, TC), jnp.float32),
            pltpu.VMEM((1, 128), jnp.int32),
            pltpu.VMEM((n, 1, 128), jnp.int32),
            pltpu.SemaphoreType.DMA((cache_states.shape[0],)),
            pltpu.SemaphoreType.DMA, pltpu.SemaphoreType.DMA,
            *sem(EARLY, LANES - 1), *sem(LANES - 1),
            pltpu.SemaphoreType.DMA((LANES * (CHUNKS - EARLY) + EARLY + 1,)),
            pltpu.VMEM((groups, 1, 128), jnp.int32), *sem(groups),
        ],
        compiler_params=pltpu.CompilerParams(collective_id=0, has_side_effects=True, vmem_limit_bytes=58 * 2**20),
        name="info",
    )(hit_owner, hit_slot, hit_spans, request_of, cache_states, cache_tails, dt_raw, dt_bias, a_log)


def conv(taps, bias, pad, rows):
    v = jnp.broadcast_to(bias, (rows, bias.shape[1]))
    for k in range(4):
        v = v + taps[k : k + 1, :] * pad[5 + k : 5 + k + rows, :]
    return (v / (1.0 + jnp.exp(-v))).astype(jnp.bfloat16)


def route_kernel(
    n, slots, tab, own, plane_in, plane_t_in,
    cum_ref, cumt_ref, stept_ref, coef_ref, ecum_ref, elast_ref, xbc_ref, weight_ref, bias_ref, skip_ref,
    y_out, final_out,
    start, tail_out, xs, pad, head_pad, tail_rows, scores_ref, y_local, fresh, y_stage, f_stage, y_sem, f_sem,
    skips, plane, plane_t, up_recv, up_recv_t, down_recv, down_recv_t,
    up_send, up_send_t, down_send, down_send_t, fin_send, fin_send_t,
    load_sem, spread_s, spread_r, up_s, up_r, up_ts, up_tr,
    down_s, down_r, down_ts, down_tr, fin_s, fin_r, fin_ts, fin_tr,
):
    planes = n // LANES
    steps = CHUNKS * slots
    grp, me = lax.axis_index("grp"), lax.axis_index("req")
    z, l = lax.div(me, LANES), lax.rem(me, LANES)
    first, last = z == 0, z == planes - 1

    def mate(k):
        return z * LANES + lax.rem(l + k, LANES)

    loads = [
        pltpu.make_async_copy(plane_t_in, plane_t, load_sem.at[0]),
        pltpu.make_async_copy(plane_in, plane.at[pl.ds(0, EARLY)], load_sem.at[1]),
    ]
    for c in range(EARLY, CHUNKS):
        loads.append(pltpu.make_async_copy(own.at[l, c], plane.at[c, l], load_sem.at[2 + c - EARLY]))
    for load in loads:
        load.start()
    barrier = pltpu.get_barrier_semaphore()
    for k in range(1, LANES):
        pl.semaphore_signal(barrier, inc=1, device_id=(grp, mate(k)), device_id_type=MESH)

    @pl.when(jnp.logical_not(first))
    def _():
        pl.semaphore_signal(barrier, inc=1, device_id=(grp, me - LANES), device_id_type=MESH)

    @pl.when(jnp.logical_not(last))
    def _():
        pl.semaphore_signal(barrier, inc=1, device_id=(grp, me + LANES), device_id_type=MESH)

    pl.semaphore_wait(barrier, LANES - 1 + jnp.where(first | last, 1, 2))

    def remote(src, dst, ss, rs, to):
        return pltpu.make_async_remote_copy(
            src_ref=src, dst_ref=dst, send_sem=ss, recv_sem=rs, device_id=(grp, to), device_id_type=MESH
        )

    def spread(c, k):
        to = lax.rem(l + k, LANES)
        return remote(own.at[to, c], plane.at[c, l], spread_s.at[c, k - 1], spread_r.at[c, k - 1], mate(k))

    def spread_from(c, k):
        frm = lax.rem(l + LANES - k, LANES)
        return remote(own.at[frm, c], plane.at[c, frm], spread_s.at[c, k - 1], spread_r.at[c, k - 1], mate(k))

    def up(s):
        return remote(up_send.at[s], up_recv.at[s], up_s.at[s], up_r.at[s], me + LANES)

    def up_tail(s):
        return remote(up_send_t.at[s], up_recv_t.at[s], up_ts.at[s], up_tr.at[s], me + LANES)

    def down(s):
        return remote(down_send.at[s], down_recv.at[s], down_s.at[s], down_r.at[s], me - LANES)

    def down_tail(s):
        return remote(down_send_t.at[s], down_recv_t.at[s], down_ts.at[s], down_tr.at[s], me - LANES)

    def fin(c, k):
        to = lax.rem(l + k, LANES)
        return remote(fin_send.at[c, k - 1], start.at[l, c], fin_s.at[c, k - 1], fin_r.at[c, k - 1], mate(k))

    def fin_from(c, k):
        frm = lax.rem(l + LANES - k, LANES)
        return remote(fin_send.at[c, k - 1], start.at[frm, c], fin_s.at[c, k - 1], fin_r.at[c, k - 1], mate(k))

    def fin_tail(k):
        return remote(fin_send_t.at[k - 1], tail_out.at[l], fin_ts.at[k - 1], fin_tr.at[k - 1], mate(k))

    def fin_tail_from(k):
        frm = lax.rem(l + LANES - k, LANES)
        return remote(fin_send_t.at[k - 1], tail_out.at[frm], fin_ts.at[k - 1], fin_tr.at[k - 1], mate(k))

    for c in range(EARLY, min(EARLY + AHEAD, CHUNKS)):
        for k in range(1, LANES):
            spread(c, k).start()
    rows = xbc_ref.shape[0]
    channels = xbc_ref.shape[1]
    pieces = channels // PW
    scans = INNER // PW
    first_b, first_c = INNER, INNER + GROUPS * NST
    low = lax.broadcasted_iota(jnp.int32, (rows, 128), 1) < HEAD_DIM
    low_n = lax.broadcasted_iota(jnp.int32, (NST, 128), 1) < HEAD_DIM

    def columns(i):
        return pl.ds(pl.multiple_of(i * PW, PW), PW)

    def conv_piece(i):
        at = columns(i)
        pad[0:8, :] = jnp.zeros((8, PW), jnp.float32)
        pad[8 : 8 + rows, :] = xbc_ref[:, at].astype(jnp.float32)
        xs[:, at] = conv(weight_ref[:, at], bias_ref[:, at], pad, rows)

    def head_piece(i, _):
        at = columns(i)
        head_pad[0:8, :] = tail_rows[:, at]
        head_pad[8:24, :] = xbc_ref[0:16, at].astype(jnp.float32)
        xs[0:16, at] = conv(weight_ref[:, at], bias_ref[:, at], head_pad, 16)
        return 0

    def with_tail():
        tail_rows[...] = jnp.zeros_like(tail_rows)
        for p in range(LANES):
            got = tail_out[p].astype(jnp.float32)
            for q in range(-(-channels // WIDE)):
                at = q * WIDE + p * TC
                if at < channels:
                    tail_rows[5:8, at : at + TC] = got[3 * q : 3 * q + 3, :]
        lax.fori_loop(0, pieces, head_piece, 0)
        causal = lax.broadcasted_iota(jnp.int32, (rows, rows), 0) >= lax.broadcasted_iota(jnp.int32, (rows, rows), 1)
        for g in range(GROUPS):
            b = xs[:, first_b + g * NST : first_b + (g + 1) * NST]
            c = xs[:, first_c + g * NST : first_c + (g + 1) * NST]
            scores = lax.dot_general(c, b, (((1,), (1,)), ((), ())), preferred_element_type=jnp.float32)
            scores_ref[g] = jnp.where(causal, scores, 0.0)

    def turned(ref, head):
        return pltpu.roll(ref[...], lax.rem(128 - head, 128), axis=1)

    def scan_piece(p, c):
        i = p * (scans // LANES) + c
        heads = PW // HEAD_DIM
        at = columns(i)
        x = xs[:, at]
        scores = scores_ref[p]
        cum, coef, skip = turned(cum_ref, heads * i), turned(coef_ref, heads * i), turned(skips, heads * i)
        here = pl.ds(pl.multiple_of(i * heads, heads), heads)
        cumt, stept = cumt_ref[here, :], stept_ref[here, :]
        zero = jnp.zeros((rows, 128), jnp.bfloat16)
        ys, carried = [], []
        for j in range(0, heads, 2):
            xp = x[:, j * HEAD_DIM : (j + 2) * HEAD_DIM]
            mixes = []
            for h in (j, j + 1):
                decay = jnp.exp(jnp.minimum(cum[:, h : h + 1] - cumt[h : h + 1, :], 0.0))
                mixes.append((scores * decay * stept[h : h + 1, :]).astype(jnp.bfloat16))
            mix = jnp.concatenate(mixes, axis=1)
            both = jnp.concatenate([jnp.where(low, xp, zero), jnp.where(low, zero, xp)], axis=0)
            xf = xp.astype(jnp.float32)
            d = jnp.where(low[0:1], skip[0:1, j : j + 1], skip[0:1, j + 1 : j + 2])
            ys.append(jnp.dot(mix, both, preferred_element_type=jnp.float32) + d * xf)
            carried.append((jnp.where(low, coef[:, j : j + 1], coef[:, j + 1 : j + 2]) * xf).astype(jnp.bfloat16))
        per = CC // 128
        for u in range(PW // CC):
            y_local[i * (PW // CC) + u] = jnp.concatenate(ys[u * per : (u + 1) * per], axis=1)
        b = xs[:, pl.ds(pl.multiple_of(first_b + p * NST, NST), NST)]
        new = lax.dot_general(
            b, jnp.concatenate(carried, axis=1), (((0,), (0,)), ((), ())), preferred_element_type=jnp.float32
        )
        for u in range(PW // CC):
            fresh[i * (PW // CC) + u] = new[:, u * CC : (u + 1) * CC]

    def outputs(i):
        at = pl.ds(pl.multiple_of(i * CC, CC), CC)
        return (
            pltpu.make_async_copy(y_stage.at[i], y_out.at[:, at], y_sem.at[i]),
            pltpu.make_async_copy(f_stage.at[i], final_out.at[0, :, at], f_sem.at[i]),
        )

    def last_piece(p, c):
        i = p * CHUNKS + c
        held = start[p, c]
        ys = jnp.dot(xs[:, pl.ds(pl.multiple_of(first_c + p * NST, NST), NST)], held,
                     preferred_element_type=jnp.float32)
        heads = CC // HEAD_DIM
        ecum, elast = turned(ecum_ref, heads * i), turned(elast_ref, heads * i)
        for j in range(0, heads, 2):
            sl = slice(j * HEAD_DIM, (j + 2) * HEAD_DIM)
            factor = jnp.where(low, ecum[:, j : j + 1], ecum[:, j + 1 : j + 2])
            y_stage[i, :, sl] = (y_local[i, :, sl] + factor * ys[:, sl]).astype(jnp.bfloat16)
            kept = jnp.where(low_n[0:1], elast[0:1, j : j + 1], elast[0:1, j + 1 : j + 2])
            f_stage[i, :, sl] = (kept * held[:, sl].astype(jnp.float32) + fresh[i, :, sl]).astype(jnp.bfloat16)
        for copy in outputs(i):
            copy.start()

    def last_chunk(c):
        for k in range(1, LANES):
            fin_from(c, k).wait_recv()

        def one(p, _):
            last_piece(p, c)
            return 0

        lax.fori_loop(0, LANES, one, 0)

    ready = slots + LAG * (planes - 1)
    total = steps + LAG * (planes - 1)
    per_conv = -(-pieces // ready)
    per_scan = -(-scans // (total - ready - 1))

    lead = -(-LANES // per_scan)

    def compute(t):
        @pl.when(t < ready)
        def _():
            def one(u, _):
                i = t * per_conv + u

                @pl.when(i < pieces)
                def _():
                    conv_piece(i)

                return 0

            lax.fori_loop(0, per_conv, one, 0)

        @pl.when(t == ready)
        def _():
            for k in range(1, LANES):
                fin_tail_from(k).wait_recv()
            with_tail()

        @pl.when(t > ready)
        def _():
            def one(u, _):
                i = (t - ready - 1) * per_scan + u

                @pl.when(i < scans)
                def _():
                    scan_piece(lax.rem(i, LANES), lax.div(i, LANES))

                return 0

            lax.fori_loop(0, per_scan, one, 0)
            since = t - ready - lead

            @pl.when((since >= 0) & (lax.rem(jnp.maximum(since, 0), slots) == 0))
            def _():
                last_chunk(lax.div(since, slots))

    def fill(dst, at, sel, near, c, far, base, j, inner):
        value = near[c, 0]
        for p in range(1, LANES):
            value = lax.select_n(sel == p, value, near[c, p])
        dst[at] = value

        @pl.when(inner)
        def _():
            def one(i, _):
                dst[at] = lax.select_n(sel == LANES + i, dst[at], far[base + i])
                return 0

            lax.fori_loop(0, j + 1, one, 0)

    def fill_tail(dst, j, sel, far, inner):
        value = plane_t[0]
        for p in range(1, LANES):
            value = lax.select_n(sel == p, value, plane_t[p])
        dst[j] = value

        @pl.when(inner)
        def _():
            def one(i, _):
                dst[j] = lax.select_n(sel == LANES + i, dst[j], far[i])
                return 0

            lax.fori_loop(0, j + 1, one, 0)

    def tick(t, _):
        tp = t - LAG * jnp.minimum(z, planes - 1 - z)

        @pl.when((tp >= 0) & (tp < steps) & (lax.rem(jnp.maximum(tp, 0), slots) == 0))
        def _():
            c = lax.div(tp, slots)

            @pl.when(c >= EARLY)
            def _():
                for k in range(1, LANES):
                    spread_from(c, k).wait_recv()

        more = EARLY + AHEAD + lax.div(t, PACE)

        @pl.when((more < CHUNKS) & (lax.rem(t, PACE) == 0))
        def _():
            for k in range(1, LANES):
                spread(more, k).start()

        def along(s, row, edge_in, edge_out, copy, copy_tail, send, send_t, recv, recv_t):
            @pl.when((s >= 0) & (s < steps))
            def _():
                c, j = lax.div(s, slots), lax.rem(s, slots)
                inner = jnp.logical_not(edge_in)

                @pl.when(inner)
                def _():
                    @pl.when(c == 0)
                    def _():
                        copy_tail(j).wait_recv()

                    copy(s).wait_recv()

                @pl.when(jnp.logical_not(edge_out))
                def _():
                    sel = tab[row, j]

                    @pl.when(c == 0)
                    def _():
                        fill_tail(send_t, j, sel, recv_t, inner)
                        copy_tail(j).start()

                    fill(send, s, sel, plane, c, recv, c * slots, j, inner)

                    @pl.when(s >= DEPTH)
                    def _():
                        copy(s - DEPTH).wait_send()

                    copy(s).start()

        along(t - LAG * z, 0, first, last, up, up_tail, up_send, up_send_t, up_recv, up_recv_t)
        along(t - LAG * (planes - 1 - z), 1, last, first, down, down_tail, down_send, down_send_t, down_recv, down_recv_t)

        tf = t - LAG * jnp.maximum(z, planes - 1 - z)

        @pl.when((tf >= 0) & (tf < steps) & (lax.rem(jnp.maximum(tf, 0), slots) == slots - 1))
        def _():
            c = lax.div(tf, slots)
            sels = [tab[2, mate(k)] for k in range(LANES)]

            def choose(near, far_up, far_down, write, read):
                acc = [jnp.zeros(near(0).shape, jnp.bfloat16)] * LANES
                for p in range(LANES):
                    value = near(p)
                    acc = [lax.select_n(sel == p, a, value) for sel, a in zip(sels, acc)]
                for k in range(LANES):
                    write(k, acc[k])

                def far(get, base):
                    acc = [read(k) for k in range(LANES)]
                    for i in range(slots):
                        value = get(i)
                        acc = [lax.select_n(sel == base + i, a, value) for sel, a in zip(sels, acc)]
                    for k in range(LANES):
                        write(k, acc[k])

                @pl.when(jnp.logical_not(first))
                def _():
                    far(far_up, LANES)

                @pl.when(jnp.logical_not(last))
                def _():
                    far(far_down, LANES + n)

            def rows_of(b, _):
                at = pl.ds(pl.multiple_of(b * 16, 16), 16)

                def write(k, v):
                    if k == 0:
                        start[l, c, at] = v
                    else:
                        fin_send[c, k - 1, at] = v

                def read(k):
                    return start[l, c, at] if k == 0 else fin_send[c, k - 1, at]

                choose(lambda p: plane[c, p, at], lambda i: up_recv[c * slots + i, at],
                       lambda i: down_recv[c * slots + i, at], write, read)
                return 0

            lax.fori_loop(0, NST // 16, rows_of, 0)
            for k in range(1, LANES):
                fin(c, k).start()

            @pl.when(c == 0)
            def _():
                def write(k, v):
                    if k == 0:
                        tail_out[l] = v
                    else:
                        fin_send_t[k - 1] = v

                def read(k):
                    return tail_out[l] if k == 0 else fin_send_t[k - 1]

                choose(lambda p: plane_t[p], lambda i: up_recv_t[i], lambda i: down_recv_t[i], write, read)
                for k in range(1, LANES):
                    fin_tail(k).start()

        compute(t)
        return 0

    skips[...] = jnp.broadcast_to(skip_ref[...], skips.shape)
    for load in loads:
        load.wait()
    lax.fori_loop(0, total, tick, 0)
    for c in range((total - 1 - ready - lead) // slots + 1, CHUNKS):
        last_chunk(c)

    for k in range(1, LANES):
        fin_tail(k).wait_send()
        for c in range(CHUNKS):
            if c >= EARLY:
                spread(c, k).wait_send()
            fin(c, k).wait_send()

    @pl.when(jnp.logical_not(last))
    def _():
        for j in range(slots):
            up_tail(j).wait_send()
        for s in range(max(steps - DEPTH, 0), steps):
            up(s).wait_send()

    @pl.when(jnp.logical_not(first))
    def _():
        for j in range(slots):
            down_tail(j).wait_send()
        for s in range(max(steps - DEPTH, 0), steps):
            down(s).wait_send()

    for i in range(LANES * CHUNKS):
        for copy in outputs(i):
            copy.wait()


def route(n, slots, number, table, own, plane, plane_t, terms, xbc, weight, bias, skip):
    steps = CHUNKS * slots
    rows, channels = xbc.shape
    pieces = LANES * CHUNKS
    f32 = lambda *shape: pltpu.VMEM(shape, jnp.float32)
    big = lambda *lead: pltpu.VMEM(lead + (NST, CC), jnp.bfloat16)
    small = lambda *lead: pltpu.VMEM(lead + (TAIL_ROWS, TC), jnp.bfloat16)
    sem = lambda *shape: [pltpu.SemaphoreType.DMA(shape)] * 2
    vmem = pl.BlockSpec(memory_space=pltpu.VMEM)
    hbm = pl.BlockSpec(memory_space=pl.ANY)
    return pl.pallas_call(
        functools.partial(route_kernel, n, slots),
        out_shape=(
            jax.ShapeDtypeStruct((rows, INNER), jnp.bfloat16),
            jax.ShapeDtypeStruct((1, NST, INNER), jnp.bfloat16),
        ),
        in_specs=[pl.BlockSpec(memory_space=pltpu.SMEM)] + [hbm] * 3 + [vmem] * 10,
        out_specs=(hbm, hbm),
        scratch_shapes=[
            big(LANES, CHUNKS), small(LANES),
            pltpu.VMEM((rows, channels), jnp.bfloat16), f32(8 + rows, PW), f32(24, PW), f32(8, channels),
            f32(GROUPS, rows, rows), f32(pieces, rows, CC), f32(pieces, NST, CC),
            pltpu.VMEM((pieces, rows, CC), jnp.bfloat16), big(pieces), *sem(pieces),
            f32(8, HEADS), big(CHUNKS, LANES), small(LANES),
            big(steps), small(slots), big(steps), small(slots),
            big(steps), small(slots), big(steps), small(slots),
            big(CHUNKS, LANES - 1), small(LANES - 1),
            pltpu.SemaphoreType.DMA((2 + CHUNKS - EARLY,)),
            *sem(CHUNKS, LANES - 1),
            *sem(steps), *sem(slots), *sem(steps), *sem(slots),
            *sem(CHUNKS, LANES - 1), *sem(LANES - 1),
        ],
        compiler_params=pltpu.CompilerParams(
            collective_id=number, has_side_effects=True, vmem_limit_bytes=(34 + 2 * slots) * 2**20
        ),
        name=f"route{slots}",
    )(table, own, plane, plane_t, *terms, xbc, weight, bias, skip)


def settle_kernel(y_ref, f_ref, y_out, f_out, y_held, f_held, in_sem, out_sem):
    pieces = []
    for i in range(SETTLE):
        at = pl.ds(i * (y_ref.shape[0] // SETTLE), y_ref.shape[0] // SETTLE)
        pieces.append((y_ref.at[at], y_held.at[at], y_out.at[at]))
        at = pl.ds(i * (NST // SETTLE), NST // SETTLE)
        pieces.append((f_ref.at[0, at], f_held.at[at], f_out.at[0, at]))
    come = [pltpu.make_async_copy(a, b, in_sem.at[i]) for i, (a, b, _) in enumerate(pieces)]
    go = [pltpu.make_async_copy(b, c, out_sem.at[i]) for i, (_, b, c) in enumerate(pieces)]
    for copy in come:
        copy.start()
    for first, second in zip(come, go):
        first.wait()
        second.start()
    for copy in go:
        copy.wait()


def settle(y, final):
    hbm = pl.BlockSpec(memory_space=pl.ANY)
    return pl.pallas_call(
        settle_kernel,
        out_shape=(jax.ShapeDtypeStruct(y.shape, y.dtype), jax.ShapeDtypeStruct(final.shape, final.dtype)),
        in_specs=[hbm, hbm],
        out_specs=(hbm, hbm),
        scratch_shapes=[
            pltpu.VMEM(y.shape, y.dtype), pltpu.VMEM(final.shape[1:], final.dtype),
            pltpu.SemaphoreType.DMA((2 * SETTLE,)), pltpu.SemaphoreType.DMA((2 * SETTLE,)),
        ],
        compiler_params=pltpu.CompilerParams(vmem_limit_bytes=SETTLE_LIMIT),
        name="settle",
    )(y, final)


def local_routed(
    mesh, xbc, dt_raw, conv_weight, conv_bias, dt_bias, a_log, d_skip, cache_states, cache_tails,
    hit_owner, hit_slot, hit_spans, request_of,
):
    n = mesh.shape["req"]
    sizes = [3, 4, 5, n // 2]
    table, which, own, plane, plane_t, *terms = info(
        mesh, sizes, hit_owner, hit_slot, hit_spans, request_of, cache_states, cache_tails,
        dt_raw, dt_bias[None], a_log[None],
    )
    return settle(*lax.switch(
        which[0, 0],
        [functools.partial(route, n, size, 1 + i) for i, size in enumerate(sizes)],
        table, own, plane, plane_t, terms, xbc, conv_weight, conv_bias[None], d_skip[None],
    ))


def local(
    xbc, dt_raw, conv_weight, conv_bias, dt_bias, a_log, d_skip, cache_states, cache_tails,
    hit_owner, hit_slot, hit_spans, request_of,
):
    count = hit_owner.shape[0]
    rows = xbc.shape[0]
    mine = request_of[0]
    live = (hit_spans[mine] > 0).astype(jnp.int32)
    device = lax.axis_index("req")
    served = jnp.max(jnp.where(hit_owner == device, hit_slot, 0))
    send = lax.dynamic_slice_in_dim(cache_states, served, 1, 0).reshape(count, NST // count, INNER)
    number = jnp.broadcast_to(mine.astype(send.dtype), send.shape[:2] + (128,))
    parts = lax.all_to_all(
        jnp.concatenate([send, number], axis=2), "req", split_axis=0, concat_axis=0, tiled=True
    )
    every_request = parts[:, 0, INNER].astype(jnp.int32)
    own_tail = lax.dynamic_slice_in_dim(cache_tails, served, 1, 0)
    own_tail = jnp.pad(own_tail, ((0, 0), (0, 1), (0, 0)))
    every_tail = lax.all_gather(own_tail, "req", axis=0, tiled=True)[:, :3]
    owners = jnp.sum(
        jnp.where(every_request[:, None] == jnp.arange(count)[None, :], hit_owner[None, :], 0), axis=1
    )
    chosen = pick(parts, owners)
    start = lax.all_to_all(chosen, "req", split_axis=0, concat_axis=0, tiled=True).reshape(NST, INNER)

    tail = lax.dynamic_index_in_dim(every_tail, hit_owner[mine], 0, keepdims=False)
    tail = jnp.where(live > 0, tail, jnp.zeros_like(tail)).astype(jnp.float32)
    tail = jnp.pad(tail, ((5, 0), (0, 0)))
    step = jax.nn.softplus(dt_raw + dt_bias[None, :])
    below = jnp.tril(jnp.ones((rows, rows), jnp.float32))
    cum = jnp.dot(below, step * (-jnp.exp(a_log))[None, :], precision=lax.Precision.HIGHEST)
    last = cum[rows - 1]
    coef = jnp.exp(last[None, :] - cum) * step
    skip = jnp.repeat(d_skip, HEAD_DIM)[None, :]
    elast = jnp.repeat(jnp.exp(last), HEAD_DIM)[None, :]
    cumt = cum.T.reshape(STEPS, PER_STEP, rows)
    stept = step.T.reshape(STEPS, PER_STEP, rows)
    bias = conv_bias[None, :]

    first_b, first_c = INNER // NST, INNER // NST + GROUPS
    per = STEPS_PER_GROUP
    triple = lambda r: [
        pl.BlockSpec((r, COLS), lambda i: (0, i)),
        pl.BlockSpec((r, NST), lambda i: (0, first_b + i // per)),
        pl.BlockSpec((r, NST), lambda i: (0, first_c + i // per)),
    ]
    wide = lambda r: pl.BlockSpec((r, COLS), lambda i: (0, i))
    tall = pl.BlockSpec((1, rows, PER_STEP), lambda i: (i, 0, 0))
    flat = pl.BlockSpec((1, PER_STEP, rows), lambda i: (i, 0, 0))
    group = pl.BlockSpec((rows, NST), lambda i: (0, i // per))
    y_local, fresh, c_part = pl.pallas_call(
        local_kernel,
        grid=(STEPS,),
        out_shape=(
            jax.ShapeDtypeStruct((rows, INNER), jnp.float32),
            jax.ShapeDtypeStruct((NST, INNER), jnp.float32),
            jax.ShapeDtypeStruct((rows, GROUPS * NST), jnp.bfloat16),
        ),
        in_specs=triple(rows) + triple(8) + triple(4) + triple(1) + [tall, flat, flat, tall, wide(1)],
        out_specs=(wide(rows), wide(NST), group),
        scratch_shapes=[pltpu.VMEM((8 + rows, COLS), jnp.float32)],
        compiler_params=pltpu.CompilerParams(vmem_limit_bytes=58 * 2**20),
        cost_estimate=pl.CostEstimate(flops=10**9, bytes_accessed=40 * 10**6, transcendentals=4 * 10**6),
        name="local",
    )(xbc, xbc, xbc, tail, tail, tail, conv_weight, conv_weight, conv_weight, bias, bias, bias,
      by_step(cum), cumt, stept, by_step(coef), skip)

    return pl.pallas_call(
        state_kernel,
        grid=(STEPS,),
        out_shape=(
            jax.ShapeDtypeStruct((rows, INNER), jnp.bfloat16),
            jax.ShapeDtypeStruct((1, NST, INNER), jnp.bfloat16),
        ),
        in_specs=[pl.BlockSpec(memory_space=pltpu.SMEM), wide(NST), wide(rows), wide(NST), group, tall, wide(1)],
        out_specs=(wide(rows), pl.BlockSpec((1, NST, COLS), lambda i: (0, 0, i))),
        compiler_params=pltpu.CompilerParams(vmem_limit_bytes=58 * 2**20),
        name="state",
    )(live[None], start, y_local, fresh, c_part, by_step(jnp.exp(cum)), elast)


def solution(mesh):
    rows = P(("grp", "req"), None)
    slots = P(("grp", "req"), None, None)
    in_specs = (
        rows, rows, P(), P(), P(), P(), P(), slots, slots, P("grp"), P("grp"), P("grp"), P(("grp", "req")),
    )
    body = functools.partial(local_routed, mesh) if mesh.shape["req"] == 16 else local
    return jax.shard_map(body, mesh=mesh, in_specs=in_specs, out_specs=(rows, slots), check_vma=False)
```

```python
import functools

import jax
import jax.numpy as jnp
from jax import lax
from jax.experimental import pallas as pl
from jax.experimental.pallas import tpu as pltpu
from jax.sharding import PartitionSpec as P

HEADS = 128
HEAD_DIM = 64
GROUPS = 4
NST = 128
INNER = 8192
PER_STEP = 16
COLS = PER_STEP * HEAD_DIM
STEPS = HEADS // PER_STEP
STEPS_PER_GROUP = STEPS // GROUPS


def pick_kernel(index_ref, parts_ref, out_ref, sem):
    count = out_ref.shape[0]
    copies = []
    for i in range(count):
        copy = pltpu.make_async_copy(parts_ref.at[index_ref[i], :, pl.ds(0, INNER)], out_ref.at[i], sem.at[i])
        copy.start()
        copies.append(copy)
    for copy in copies:
        copy.wait()


def pick(parts, index):
    count = index.shape[0]
    return pl.pallas_call(
        pick_kernel,
        out_shape=jax.ShapeDtypeStruct((count, parts.shape[1], INNER), parts.dtype),
        in_specs=[pl.BlockSpec(memory_space=pltpu.SMEM), pl.BlockSpec(memory_space=pltpu.VMEM)],
        out_specs=pl.BlockSpec(memory_space=pl.ANY),
        scratch_shapes=[pltpu.SemaphoreType.DMA((count,))],
        compiler_params=pltpu.CompilerParams(vmem_limit_bytes=8 * 2**20),
        name="pick",
    )(index, parts)


def conv_block(pad, x_ref, tail_ref, w_ref, b_ref, width):
    rows = x_ref.shape[0]
    pad[0:8, 0:width] = tail_ref[...]
    pad[8 : 8 + rows, 0:width] = x_ref[...].astype(jnp.float32)
    v = jnp.broadcast_to(b_ref[...], (rows, width))
    for k in range(4):
        v = v + w_ref[k : k + 1, :] * pad[5 + k : 5 + k + rows, 0:width]
    return (v / (1.0 + jnp.exp(-v))).astype(jnp.bfloat16)


def local_kernel(
    x_ref, xb_ref, xc_ref, tx_ref, tb_ref, tc_ref, wx_ref, wb_ref, wc_ref, bx_ref, bb_ref, bc_ref,
    cum_ref, cumt_ref, stept_ref, coef_ref, skip_ref,
    y_ref, fresh_ref, c_out_ref, pad,
):
    rows = x_ref.shape[0]
    b_part = conv_block(pad, xb_ref, tb_ref, wb_ref, bb_ref, NST)
    c_part = conv_block(pad, xc_ref, tc_ref, wc_ref, bc_ref, NST)
    c_out_ref[...] = c_part
    x = conv_block(pad, x_ref, tx_ref, wx_ref, bx_ref, COLS)
    scores = lax.dot_general(c_part, b_part, (((1,), (1,)), ((), ())), preferred_element_type=jnp.float32)
    causal = lax.broadcasted_iota(jnp.int32, (rows, rows), 0) >= lax.broadcasted_iota(jnp.int32, (rows, rows), 1)
    scores = jnp.where(causal, scores, 0.0)
    low = lax.broadcasted_iota(jnp.int32, (rows, 128), 1) < HEAD_DIM
    cum = cum_ref[0]
    coef = coef_ref[0]
    zero = jnp.zeros((rows, 128), jnp.bfloat16)
    carried = []
    for j in range(0, PER_STEP, 2):
        xp = x[:, j * HEAD_DIM : (j + 2) * HEAD_DIM]
        mixes = []
        for h in (j, j + 1):
            decay = jnp.exp(jnp.minimum(cum[:, h : h + 1] - cumt_ref[0, h : h + 1, :], 0.0))
            mixes.append((scores * decay * stept_ref[0, h : h + 1, :]).astype(jnp.bfloat16))
        mix = jnp.concatenate(mixes, axis=1)
        both = jnp.concatenate([jnp.where(low, xp, zero), jnp.where(low, zero, xp)], axis=0)
        xf = xp.astype(jnp.float32)
        sl = slice(j * HEAD_DIM, (j + 2) * HEAD_DIM)
        y_ref[:, sl] = jnp.dot(mix, both, preferred_element_type=jnp.float32) + skip_ref[:, sl] * xf
        carried.append((jnp.where(low, coef[:, j : j + 1], coef[:, j + 1 : j + 2]) * xf).astype(jnp.bfloat16))
    fresh_ref[...] = lax.dot_general(
        b_part, jnp.concatenate(carried, axis=1), (((0,), (0,)), ((), ())), preferred_element_type=jnp.float32
    )


def state_kernel(live_ref, start_ref, y_ref, fresh_ref, c_ref, ecum_ref, elast_ref, y_out_ref, final_ref):
    rows = y_ref.shape[0]
    start = start_ref[...]
    start = jnp.where(live_ref[0] > 0, start, jnp.zeros_like(start))
    low = lax.broadcasted_iota(jnp.int32, (rows, 128), 1) < HEAD_DIM
    ecum = ecum_ref[0]
    ys = jnp.dot(c_ref[...], start, preferred_element_type=jnp.float32)
    for j in range(0, PER_STEP, 2):
        sl = slice(j * HEAD_DIM, (j + 2) * HEAD_DIM)
        factor = jnp.where(low, ecum[:, j : j + 1], ecum[:, j + 1 : j + 2])
        y_out_ref[:, sl] = (y_ref[:, sl] + factor * ys[:, sl]).astype(jnp.bfloat16)
    final_ref[0] = (elast_ref[...] * start.astype(jnp.float32) + fresh_ref[...]).astype(jnp.bfloat16)


def by_step(a):
    return a.reshape(a.shape[0], STEPS, PER_STEP).transpose(1, 0, 2)


LANES = 4
CHUNKS = 8
WIDE = INNER // LANES
CC = WIDE // CHUNKS
PW = 512
TC = WIDE // LANES
DEPTH = 4
EARLY = 2
AHEAD = 1
PACE = 3
TAIL_ROWS = 16
LAG = 4
SETTLE = 4
SETTLE_LIMIT = 60 * 2**20
MESH = pl.DeviceIdType.MESH


def masked_column(row, rows):
    sub = lax.broadcasted_iota(jnp.int32, (rows, 128), 0)
    lane = lax.broadcasted_iota(jnp.int32, (rows, 128), 1)
    return jnp.sum(jnp.where(sub == lane, jnp.broadcast_to(row, (rows, 128)), 0), axis=1, keepdims=True)


def destinations(wanted, n):
    planes = n // LANES
    sub = lax.broadcasted_iota(jnp.int32, (n, 128), 0) // LANES
    lane = lax.broadcasted_iota(jnp.int32, (n, 128), 1)
    hit = wanted == lane
    top = jnp.max(jnp.where(hit, sub, -1), axis=0, keepdims=True)
    low = jnp.min(jnp.where(hit, sub, planes), axis=0, keepdims=True)
    return top, low


def head_terms(dt_ref, dt_bias_ref, a_log_ref, cum_ref, cumt_ref, stept_ref, coef_ref, ecum_ref, elast_ref):
    rows = dt_ref.shape[0]
    step = jax.nn.softplus(dt_ref[...] + dt_bias_ref[...])
    below = (
        lax.broadcasted_iota(jnp.int32, (rows, rows), 0) >= lax.broadcasted_iota(jnp.int32, (rows, rows), 1)
    ).astype(jnp.float32)
    cum = jnp.dot(below, step * (-jnp.exp(a_log_ref[...])), precision=lax.Precision.HIGHEST,
                  preferred_element_type=jnp.float32)
    last = cum[rows - 1 : rows, :]
    cum_ref[...] = cum
    cumt_ref[...] = cum.T
    stept_ref[...] = step.T
    coef_ref[...] = jnp.exp(last - cum) * step
    ecum_ref[...] = jnp.exp(cum)
    elast_ref[...] = jnp.broadcast_to(jnp.exp(last), elast_ref.shape)


def info_kernel(
    groups, n, sizes, owner_ref, slot_ref, spans_ref, request_ref, states_ref, tails_ref,
    dt_ref, dt_bias_ref, a_log_ref,
    table_ref, which_ref, own_out, plane, plane_t, cum_ref, cumt_ref, stept_ref, coef_ref, ecum_ref, elast_ref,
    three, own, own_tail, packed, mine, rows, load_sem, send_sem, recv_sem, spread_s, spread_r, spread_ts, spread_tr,
    out_sem, needs, need_s, need_r,
):
    planes = n // LANES
    grp, me = lax.axis_index("grp"), lax.axis_index("req")
    z, l = lax.div(me, LANES), lax.rem(me, LANES)
    loads = []
    for i in range(states_ref.shape[0]):
        load = pltpu.make_async_copy(states_ref.at[i], three.at[i], load_sem.at[i])
        load.start()
        loads.append(load)
    barrier = pltpu.get_barrier_semaphore()

    def other(k):
        return grp, lax.rem(me + k, n)

    def counterpart(k):
        return lax.rem(grp + k, groups), me

    for k in range(1, n):
        pl.semaphore_signal(barrier, inc=1, device_id=other(k), device_id_type=MESH)
    for k in range(1, groups):
        pl.semaphore_signal(barrier, inc=1, device_id=counterpart(k), device_id_type=MESH)
    request = request_ref[0]
    wanted = jnp.where(spans_ref[request] > 0, owner_ref[request], -1)
    served = jnp.int32(0)
    for r in range(n):
        served = jnp.maximum(served, jnp.where(owner_ref[r] == me, slot_ref[r], 0))
    mine[...] = jnp.full((1, 128), wanted, jnp.int32)
    tail = tails_ref[served].astype(jnp.float32)
    packed[...] = jnp.zeros_like(packed)
    for q in range(-(-tail.shape[1] // WIDE)):
        for p in range(LANES):
            at = q * WIDE + p * TC
            if at < tail.shape[1]:
                packed[p, 3 * q : 3 * q + 3, :] = tail[:, at : at + TC]
    own_tail[...] = packed[...].astype(jnp.bfloat16)
    outs = []

    def put(src, dst):
        copy = pltpu.make_async_copy(src, dst, out_sem.at[len(outs)])
        copy.start()
        outs.append(copy)

    put(own_tail.at[l], plane_t.at[l])
    for load in loads:
        load.wait()

    def take(c):
        for p in range(LANES):
            own[p, c] = three[served, :, p * WIDE + c * CC : p * WIDE + (c + 1) * CC]

    for c in range(EARLY):
        take(c)
        put(own.at[l, c], plane.at[c, l])
    pl.semaphore_wait(barrier, n + groups - 2)
    for k in range(1, n):
        pltpu.make_async_remote_copy(
            src_ref=mine, dst_ref=rows.at[me], send_sem=send_sem, recv_sem=recv_sem,
            device_id=other(k), device_id_type=MESH,
        ).start()

    def spread(src, dst, ss, rs, k):
        return pltpu.make_async_remote_copy(
            src_ref=src, dst_ref=dst, send_sem=ss, recv_sem=rs,
            device_id=(grp, z * LANES + lax.rem(l + k, LANES)), device_id_type=MESH,
        )

    spreads = []
    for k in range(1, LANES):
        to, frm = lax.rem(l + k, LANES), lax.rem(l + LANES - k, LANES)
        sems = (spread_ts.at[k - 1], spread_tr.at[k - 1], k)
        spread(own_tail.at[to], plane_t.at[l], *sems).start()
        spreads.append((spread(own_tail.at[to], plane_t.at[l], *sems), spread(own_tail.at[frm], plane_t.at[frm], *sems)))
    for c in range(EARLY):
        for k in range(1, LANES):
            to, frm = lax.rem(l + k, LANES), lax.rem(l + LANES - k, LANES)
            sems = (spread_s.at[c, k - 1], spread_r.at[c, k - 1], k)
            spread(own.at[to, c], plane.at[c, l], *sems).start()
            spreads.append((spread(own.at[to, c], plane.at[c, l], *sems), spread(own.at[frm, c], plane.at[c, frm], *sems)))
    for c in range(EARLY, CHUNKS):
        take(c)
        for p in range(LANES):
            put(own.at[p, c], own_out.at[p, c])
    head_terms(dt_ref, dt_bias_ref, a_log_ref, cum_ref, cumt_ref, stept_ref, coef_ref, ecum_ref, elast_ref)
    everyone = rows.at[pl.ds(0, n - 1)]
    pltpu.make_async_copy(everyone, everyone, send_sem).wait()
    pltpu.make_async_copy(everyone, everyone, recv_sem).wait()
    rows[pl.ds(me, 1)] = mine[...].reshape(1, 1, 128)

    need = jnp.zeros((1, 1), jnp.int32)
    lane_row = lax.broadcasted_iota(jnp.int32, (1, 128), 1)
    home = lane_row // LANES
    wants = rows[0:n].reshape(n, 128)
    top, low = destinations(wants, n)
    for cut in range(planes - 1):
        up = jnp.sum(((home <= cut) & (top > cut) & (lane_row < n)).astype(jnp.int32), axis=1, keepdims=True)
        down = jnp.sum(((home > cut) & (low <= cut) & (lane_row < n)).astype(jnp.int32), axis=1, keepdims=True)
        need = jnp.maximum(need, jnp.maximum(up, down))
    needs[0] = jnp.broadcast_to(need, (1, 128))
    swaps = []
    for k in range(1, groups):
        swap = pltpu.make_async_remote_copy(
            src_ref=needs.at[0], dst_ref=needs.at[k], send_sem=need_s.at[k], recv_sem=need_r.at[k],
            device_id=counterpart(k), device_id_type=MESH,
        )
        swap.start()
        swaps.append(swap)

    sub = lax.broadcasted_iota(jnp.int32, (n, 128), 0)
    lane = lax.broadcasted_iota(jnp.int32, (n, 128), 1)
    wants_row = jnp.sum(jnp.where(sub == lane, wants, 0), axis=0, keepdims=True)
    col = lax.broadcasted_iota(jnp.int32, (n, 1), 0)
    col_home = col // LANES
    top_col, low_col = masked_column(top, n), masked_column(low, n)

    def up_set(where_home, where_top, cut):
        return (where_home <= cut) & (where_top > cut)

    def down_set(where_home, where_low, cut):
        return (where_home > cut) & (where_low <= cut)

    def rank(inside, key_row, key_col):
        ahead = inside & (key_row < key_col) & (lane_row < n)
        return jnp.sum(ahead.astype(jnp.int32), axis=1, keepdims=True)

    up_row, up_col = (planes - top) * n + lane_row, (planes - top_col) * n + col
    down_row, down_col = (low + 1) * n + lane_row, (low_col + 1) * n + col
    up_in = rank(up_set(home, top, z - 1), up_row, up_col)
    up_out = rank(up_set(home, top, z), up_row, up_col)
    down_in = rank(down_set(home, low, z), down_row, down_col)
    down_out = rank(down_set(home, low, z - 1), down_row, down_col)
    near = lax.rem(col, LANES)
    src_up = jnp.where(col_home == z, near, LANES + up_in)
    src_down = jnp.where(col_home == z, near, LANES + down_in)
    src_fin = jnp.where(col_home == z, near, jnp.where(col_home < z, LANES + up_in, LANES + n + down_in))
    sel_up = jnp.sum(jnp.where(up_set(col_home, top_col, z) & (up_out == lane), src_up, 0), axis=0, keepdims=True)
    sel_down = jnp.sum(jnp.where(down_set(col_home, low_col, z - 1) & (down_out == lane), src_down, 0), axis=0, keepdims=True)
    sel_fin = jnp.sum(jnp.where(wants_row == col, src_fin, 0), axis=0, keepdims=True)
    sel_fin = jnp.where(wants_row < 0, -1, sel_fin)
    table_ref[...] = jnp.zeros_like(table_ref)
    table_ref[0:1, :] = sel_up
    table_ref[1:2, :] = sel_down
    table_ref[2:3, :] = sel_fin
    for swap in swaps:
        swap.wait()
    for k in range(1, groups):
        need = jnp.maximum(need, needs[k][:, 0:1])
    which = jnp.zeros((1, 1), jnp.int32)
    for size in sizes[:-1]:
        which += (need > size).astype(jnp.int32)
    which_ref[...] = which
    for sent, come in spreads:
        sent.wait_send()
        come.wait_recv()
    for copy in outs:
        copy.wait()


def info(
    mesh, sizes, hit_owner, hit_slot, hit_spans, request_of, cache_states, cache_tails, dt_raw, dt_bias, a_log
):
    groups, n = mesh.shape["grp"], mesh.shape["req"]
    smem = pl.BlockSpec(memory_space=pltpu.SMEM)
    vmem = pl.BlockSpec(memory_space=pltpu.VMEM)
    hbm = pl.BlockSpec(memory_space=pl.ANY)
    rows = dt_raw.shape[0]
    bf16 = lambda *shape: jax.ShapeDtypeStruct(shape, jnp.bfloat16)
    f32 = lambda *shape: jax.ShapeDtypeStruct(shape, jnp.float32)
    sem = lambda *shape: [pltpu.SemaphoreType.DMA(shape)] * 2
    return pl.pallas_call(
        functools.partial(info_kernel, groups, n, sizes),
        out_shape=(
            jax.ShapeDtypeStruct((8, 128), jnp.int32),
            jax.ShapeDtypeStruct((1, 1), jnp.int32),
            bf16(LANES, CHUNKS, NST, CC),
            bf16(EARLY, LANES, NST, CC),
            bf16(LANES, TAIL_ROWS, TC),
            f32(rows, HEADS), f32(HEADS, rows), f32(HEADS, rows), f32(rows, HEADS), f32(rows, HEADS), f32(8, HEADS),
        ),
        in_specs=[smem] * 4 + [hbm] + [vmem] * 4,
        out_specs=(vmem, vmem, hbm, hbm, hbm) + (vmem,) * 6,
        scratch_shapes=[
            pltpu.VMEM(cache_states.shape, jnp.bfloat16),
            pltpu.VMEM((LANES, CHUNKS, NST, CC), jnp.bfloat16),
            pltpu.VMEM((LANES, TAIL_ROWS, TC), jnp.bfloat16),
            pltpu.VMEM((LANES, TAIL_ROWS, TC), jnp.float32),
            pltpu.VMEM((1, 128), jnp.int32),
            pltpu.VMEM((n, 1, 128), jnp.int32),
            pltpu.SemaphoreType.DMA((cache_states.shape[0],)),
            pltpu.SemaphoreType.DMA, pltpu.SemaphoreType.DMA,
            *sem(EARLY, LANES - 1), *sem(LANES - 1),
            pltpu.SemaphoreType.DMA((LANES * (CHUNKS - EARLY) + EARLY + 1,)),
            pltpu.VMEM((groups, 1, 128), jnp.int32), *sem(groups),
        ],
        compiler_params=pltpu.CompilerParams(collective_id=0, has_side_effects=True, vmem_limit_bytes=58 * 2**20),
        name="info",
    )(hit_owner, hit_slot, hit_spans, request_of, cache_states, cache_tails, dt_raw, dt_bias, a_log)


def conv(taps, bias, pad, rows):
    v = jnp.broadcast_to(bias, (rows, bias.shape[1]))
    for k in range(4):
        v = v + taps[k : k + 1, :] * pad[5 + k : 5 + k + rows, :]
    return (v / (1.0 + jnp.exp(-v))).astype(jnp.bfloat16)


def route_kernel(
    n, slots, tab, own, plane_in, plane_t_in,
    cum_ref, cumt_ref, stept_ref, coef_ref, ecum_ref, elast_ref, xbc_ref, weight_ref, bias_ref, skip_ref,
    y_out, final_out,
    start, tail_out, xs, pad, head_pad, tail_rows, scores_ref, y_local, fresh, y_stage, f_stage, y_sem, f_sem,
    skips, plane, plane_t, up_recv, up_recv_t, down_recv, down_recv_t,
    up_send, up_send_t, down_send, down_send_t, fin_send, fin_send_t,
    load_sem, spread_s, spread_r, up_s, up_r, up_ts, up_tr,
    down_s, down_r, down_ts, down_tr, fin_s, fin_r, fin_ts, fin_tr,
):
    planes = n // LANES
    steps = CHUNKS * slots
    grp, me = lax.axis_index("grp"), lax.axis_index("req")
    z, l = lax.div(me, LANES), lax.rem(me, LANES)
    first, last = z == 0, z == planes - 1

    def mate(k):
        return z * LANES + lax.rem(l + k, LANES)

    loads = [
        pltpu.make_async_copy(plane_t_in, plane_t, load_sem.at[0]),
        pltpu.make_async_copy(plane_in, plane.at[pl.ds(0, EARLY)], load_sem.at[1]),
    ]
    for c in range(EARLY, CHUNKS):
        loads.append(pltpu.make_async_copy(own.at[l, c], plane.at[c, l], load_sem.at[2 + c - EARLY]))
    for load in loads:
        load.start()
    barrier = pltpu.get_barrier_semaphore()
    for k in range(1, LANES):
        pl.semaphore_signal(barrier, inc=1, device_id=(grp, mate(k)), device_id_type=MESH)

    @pl.when(jnp.logical_not(first))
    def _():
        pl.semaphore_signal(barrier, inc=1, device_id=(grp, me - LANES), device_id_type=MESH)

    @pl.when(jnp.logical_not(last))
    def _():
        pl.semaphore_signal(barrier, inc=1, device_id=(grp, me + LANES), device_id_type=MESH)

    pl.semaphore_wait(barrier, LANES - 1 + jnp.where(first | last, 1, 2))

    def remote(src, dst, ss, rs, to):
        return pltpu.make_async_remote_copy(
            src_ref=src, dst_ref=dst, send_sem=ss, recv_sem=rs, device_id=(grp, to), device_id_type=MESH
        )

    def spread(c, k):
        to = lax.rem(l + k, LANES)
        return remote(own.at[to, c], plane.at[c, l], spread_s.at[c, k - 1], spread_r.at[c, k - 1], mate(k))

    def spread_from(c, k):
        frm = lax.rem(l + LANES - k, LANES)
        return remote(own.at[frm, c], plane.at[c, frm], spread_s.at[c, k - 1], spread_r.at[c, k - 1], mate(k))

    def up(s):
        return remote(up_send.at[s], up_recv.at[s], up_s.at[s], up_r.at[s], me + LANES)

    def up_tail(s):
        return remote(up_send_t.at[s], up_recv_t.at[s], up_ts.at[s], up_tr.at[s], me + LANES)

    def down(s):
        return remote(down_send.at[s], down_recv.at[s], down_s.at[s], down_r.at[s], me - LANES)

    def down_tail(s):
        return remote(down_send_t.at[s], down_recv_t.at[s], down_ts.at[s], down_tr.at[s], me - LANES)

    def fin(c, k):
        to = lax.rem(l + k, LANES)
        return remote(fin_send.at[c, k - 1], start.at[l, c], fin_s.at[c, k - 1], fin_r.at[c, k - 1], mate(k))

    def fin_from(c, k):
        frm = lax.rem(l + LANES - k, LANES)
        return remote(fin_send.at[c, k - 1], start.at[frm, c], fin_s.at[c, k - 1], fin_r.at[c, k - 1], mate(k))

    def fin_tail(k):
        return remote(fin_send_t.at[k - 1], tail_out.at[l], fin_ts.at[k - 1], fin_tr.at[k - 1], mate(k))

    def fin_tail_from(k):
        frm = lax.rem(l + LANES - k, LANES)
        return remote(fin_send_t.at[k - 1], tail_out.at[frm], fin_ts.at[k - 1], fin_tr.at[k - 1], mate(k))

    for c in range(EARLY, min(EARLY + AHEAD, CHUNKS)):
        for k in range(1, LANES):
            spread(c, k).start()
    rows = xbc_ref.shape[0]
    channels = xbc_ref.shape[1]
    pieces = channels // PW
    scans = INNER // PW
    first_b, first_c = INNER, INNER + GROUPS * NST
    low = lax.broadcasted_iota(jnp.int32, (rows, 128), 1) < HEAD_DIM
    low_n = lax.broadcasted_iota(jnp.int32, (NST, 128), 1) < HEAD_DIM

    def columns(i):
        return pl.ds(pl.multiple_of(i * PW, PW), PW)

    def conv_piece(i):
        at = columns(i)
        pad[0:8, :] = jnp.zeros((8, PW), jnp.float32)
        pad[8 : 8 + rows, :] = xbc_ref[:, at].astype(jnp.float32)
        xs[:, at] = conv(weight_ref[:, at], bias_ref[:, at], pad, rows)

    def head_piece(i, _):
        at = columns(i)
        head_pad[0:8, :] = tail_rows[:, at]
        head_pad[8:24, :] = xbc_ref[0:16, at].astype(jnp.float32)
        xs[0:16, at] = conv(weight_ref[:, at], bias_ref[:, at], head_pad, 16)
        return 0

    def with_tail():
        tail_rows[...] = jnp.zeros_like(tail_rows)
        for p in range(LANES):
            got = tail_out[p].astype(jnp.float32)
            for q in range(-(-channels // WIDE)):
                at = q * WIDE + p * TC
                if at < channels:
                    tail_rows[5:8, at : at + TC] = got[3 * q : 3 * q + 3, :]
        lax.fori_loop(scans, pieces, head_piece, 0)

    def score(g):
        causal = lax.broadcasted_iota(jnp.int32, (rows, rows), 0) >= lax.broadcasted_iota(jnp.int32, (rows, rows), 1)
        b = xs[:, pl.ds(pl.multiple_of(first_b + g * NST, NST), NST)]
        c = xs[:, pl.ds(pl.multiple_of(first_c + g * NST, NST), NST)]
        scores = lax.dot_general(c, b, (((1,), (1,)), ((), ())), preferred_element_type=jnp.float32)
        scores_ref[g] = jnp.where(causal, scores, 0.0)

    def turned(ref, head):
        return pltpu.roll(ref[...], lax.rem(128 - head, 128), axis=1)

    def scan_piece(p, c):
        i = p * (scans // LANES) + c
        heads = PW // HEAD_DIM
        at = columns(i)
        x = xs[:, at]
        scores = scores_ref[p]
        cum, coef, skip = turned(cum_ref, heads * i), turned(coef_ref, heads * i), turned(skips, heads * i)
        here = pl.ds(pl.multiple_of(i * heads, heads), heads)
        cumt, stept = cumt_ref[here, :], stept_ref[here, :]
        zero = jnp.zeros((rows, 128), jnp.bfloat16)
        ys, carried = [], []
        for j in range(0, heads, 2):
            xp = x[:, j * HEAD_DIM : (j + 2) * HEAD_DIM]
            mixes = []
            for h in (j, j + 1):
                decay = jnp.exp(jnp.minimum(cum[:, h : h + 1] - cumt[h : h + 1, :], 0.0))
                mixes.append((scores * decay * stept[h : h + 1, :]).astype(jnp.bfloat16))
            mix = jnp.concatenate(mixes, axis=1)
            both = jnp.concatenate([jnp.where(low, xp, zero), jnp.where(low, zero, xp)], axis=0)
            xf = xp.astype(jnp.float32)
            d = jnp.where(low[0:1], skip[0:1, j : j + 1], skip[0:1, j + 1 : j + 2])
            ys.append(jnp.dot(mix, both, preferred_element_type=jnp.float32) + d * xf)
            carried.append((jnp.where(low, coef[:, j : j + 1], coef[:, j + 1 : j + 2]) * xf).astype(jnp.bfloat16))
        per = CC // 128
        for u in range(PW // CC):
            y_local[i * (PW // CC) + u] = jnp.concatenate(ys[u * per : (u + 1) * per], axis=1)
        b = xs[:, pl.ds(pl.multiple_of(first_b + p * NST, NST), NST)]
        new = lax.dot_general(
            b, jnp.concatenate(carried, axis=1), (((0,), (0,)), ((), ())), preferred_element_type=jnp.float32
        )
        for u in range(PW // CC):
            fresh[i * (PW // CC) + u] = new[:, u * CC : (u + 1) * CC]

    def outputs(i):
        at = pl.ds(pl.multiple_of(i * CC, CC), CC)
        return (
            pltpu.make_async_copy(y_stage.at[i], y_out.at[:, at], y_sem.at[i]),
            pltpu.make_async_copy(f_stage.at[i], final_out.at[0, :, at], f_sem.at[i]),
        )

    def last_piece(p, c):
        i = p * CHUNKS + c
        held = start[p, c]
        ys = jnp.dot(xs[:, pl.ds(pl.multiple_of(first_c + p * NST, NST), NST)], held,
                     preferred_element_type=jnp.float32)
        heads = CC // HEAD_DIM
        ecum, elast = turned(ecum_ref, heads * i), turned(elast_ref, heads * i)
        for j in range(0, heads, 2):
            sl = slice(j * HEAD_DIM, (j + 2) * HEAD_DIM)
            factor = jnp.where(low, ecum[:, j : j + 1], ecum[:, j + 1 : j + 2])
            y_stage[i, :, sl] = (y_local[i, :, sl] + factor * ys[:, sl]).astype(jnp.bfloat16)
            kept = jnp.where(low_n[0:1], elast[0:1, j : j + 1], elast[0:1, j + 1 : j + 2])
            f_stage[i, :, sl] = (kept * held[:, sl].astype(jnp.float32) + fresh[i, :, sl]).astype(jnp.bfloat16)
        for copy in outputs(i):
            copy.start()

    def last_chunk(c):
        for k in range(1, LANES):
            fin_from(c, k).wait_recv()

        def one(p, _):
            last_piece(p, c)
            return 0

        lax.fori_loop(0, LANES, one, 0)

    ready = slots + LAG * (planes - 1)
    total = steps + LAG * (planes - 1)
    per_conv = -(-pieces // ready)
    after = ready + 3
    per_scan = -(-scans // (total - after))

    lead = after - ready - 1 + -(-LANES // per_scan)

    def compute(t):
        @pl.when(t < ready)
        def _():
            def one(u, _):
                i = t * per_conv + u

                @pl.when(i < pieces)
                def _():
                    conv_piece(i)

                return 0

            lax.fori_loop(0, per_conv, one, 0)

        @pl.when(t == ready)
        def _():
            for k in range(1, LANES):
                fin_tail_from(k).wait_recv()
            with_tail()

        part = t - ready - 1

        @pl.when((part >= 0) & (part < GROUPS))
        def _():
            score(part)
            lax.fori_loop(part * (scans // GROUPS), (part + 1) * (scans // GROUPS), head_piece, 0)

        @pl.when(t >= after)
        def _():
            def one(u, _):
                i = (t - after) * per_scan + u

                @pl.when(i < scans)
                def _():
                    scan_piece(lax.rem(i, LANES), lax.div(i, LANES))

                return 0

            lax.fori_loop(0, per_scan, one, 0)
            since = t - ready - lead

            @pl.when((since >= 0) & (lax.rem(jnp.maximum(since, 0), slots) == 0))
            def _():
                last_chunk(lax.div(since, slots))

    def fill(dst, at, sel, near, c, far, base, j, inner):
        value = near[c, 0]
        for p in range(1, LANES):
            value = lax.select_n(sel == p, value, near[c, p])
        dst[at] = value

        @pl.when(inner)
        def _():
            def one(i, _):
                dst[at] = lax.select_n(sel == LANES + i, dst[at], far[base + i])
                return 0

            lax.fori_loop(0, j + 1, one, 0)

    def fill_tail(dst, j, sel, far, inner):
        value = plane_t[0]
        for p in range(1, LANES):
            value = lax.select_n(sel == p, value, plane_t[p])
        dst[j] = value

        @pl.when(inner)
        def _():
            def one(i, _):
                dst[j] = lax.select_n(sel == LANES + i, dst[j], far[i])
                return 0

            lax.fori_loop(0, j + 1, one, 0)

    def tick(t, _):
        tp = t - LAG * jnp.minimum(z, planes - 1 - z)

        @pl.when((tp >= 0) & (tp < steps) & (lax.rem(jnp.maximum(tp, 0), slots) == 0))
        def _():
            c = lax.div(tp, slots)

            @pl.when(c >= EARLY)
            def _():
                for k in range(1, LANES):
                    spread_from(c, k).wait_recv()

        more = EARLY + AHEAD + lax.div(t, PACE)

        @pl.when((more < CHUNKS) & (lax.rem(t, PACE) == 0))
        def _():
            for k in range(1, LANES):
                spread(more, k).start()

        def along(s, row, edge_in, edge_out, copy, copy_tail, send, send_t, recv, recv_t):
            @pl.when((s >= 0) & (s < steps))
            def _():
                c, j = lax.div(s, slots), lax.rem(s, slots)
                inner = jnp.logical_not(edge_in)

                @pl.when(inner)
                def _():
                    @pl.when(c == 0)
                    def _():
                        copy_tail(j).wait_recv()

                    copy(s).wait_recv()

                @pl.when(jnp.logical_not(edge_out))
                def _():
                    sel = tab[row, j]

                    @pl.when(c == 0)
                    def _():
                        fill_tail(send_t, j, sel, recv_t, inner)
                        copy_tail(j).start()

                    fill(send, s, sel, plane, c, recv, c * slots, j, inner)

                    @pl.when(s >= DEPTH)
                    def _():
                        copy(s - DEPTH).wait_send()

                    copy(s).start()

        along(t - LAG * z, 0, first, last, up, up_tail, up_send, up_send_t, up_recv, up_recv_t)
        along(t - LAG * (planes - 1 - z), 1, last, first, down, down_tail, down_send, down_send_t, down_recv, down_recv_t)

        tf = t - LAG * jnp.maximum(z, planes - 1 - z)

        @pl.when((tf >= 0) & (tf < steps) & (lax.rem(jnp.maximum(tf, 0), slots) == slots - 1))
        def _():
            c = lax.div(tf, slots)
            sels = [tab[2, mate(k)] for k in range(LANES)]

            def choose(near, far_up, far_down, write, read):
                acc = [jnp.zeros(near(0).shape, jnp.bfloat16)] * LANES
                for p in range(LANES):
                    value = near(p)
                    acc = [lax.select_n(sel == p, a, value) for sel, a in zip(sels, acc)]
                for k in range(LANES):
                    write(k, acc[k])

                def far(get, base):
                    acc = [read(k) for k in range(LANES)]
                    for i in range(slots):
                        value = get(i)
                        acc = [lax.select_n(sel == base + i, a, value) for sel, a in zip(sels, acc)]
                    for k in range(LANES):
                        write(k, acc[k])

                @pl.when(jnp.logical_not(first))
                def _():
                    far(far_up, LANES)

                @pl.when(jnp.logical_not(last))
                def _():
                    far(far_down, LANES + n)

            def rows_of(b, _):
                at = pl.ds(pl.multiple_of(b * 16, 16), 16)

                def write(k, v):
                    if k == 0:
                        start[l, c, at] = v
                    else:
                        fin_send[c, k - 1, at] = v

                def read(k):
                    return start[l, c, at] if k == 0 else fin_send[c, k - 1, at]

                choose(lambda p: plane[c, p, at], lambda i: up_recv[c * slots + i, at],
                       lambda i: down_recv[c * slots + i, at], write, read)
                return 0

            lax.fori_loop(0, NST // 16, rows_of, 0)
            for k in range(1, LANES):
                fin(c, k).start()

            @pl.when(c == 0)
            def _():
                def write(k, v):
                    if k == 0:
                        tail_out[l] = v
                    else:
                        fin_send_t[k - 1] = v

                def read(k):
                    return tail_out[l] if k == 0 else fin_send_t[k - 1]

                choose(lambda p: plane_t[p], lambda i: up_recv_t[i], lambda i: down_recv_t[i], write, read)
                for k in range(1, LANES):
                    fin_tail(k).start()

        compute(t)
        return 0

    skips[...] = jnp.broadcast_to(skip_ref[...], skips.shape)
    for load in loads:
        load.wait()
    lax.fori_loop(0, total, tick, 0)
    for c in range((total - 1 - ready - lead) // slots + 1, CHUNKS):
        last_chunk(c)

    for k in range(1, LANES):
        fin_tail(k).wait_send()
        for c in range(CHUNKS):
            if c >= EARLY:
                spread(c, k).wait_send()
            fin(c, k).wait_send()

    @pl.when(jnp.logical_not(last))
    def _():
        for j in range(slots):
            up_tail(j).wait_send()
        for s in range(max(steps - DEPTH, 0), steps):
            up(s).wait_send()

    @pl.when(jnp.logical_not(first))
    def _():
        for j in range(slots):
            down_tail(j).wait_send()
        for s in range(max(steps - DEPTH, 0), steps):
            down(s).wait_send()

    for i in range(LANES * CHUNKS):
        for copy in outputs(i):
            copy.wait()


def route(n, slots, number, table, own, plane, plane_t, terms, xbc, weight, bias, skip):
    steps = CHUNKS * slots
    rows, channels = xbc.shape
    pieces = LANES * CHUNKS
    f32 = lambda *shape: pltpu.VMEM(shape, jnp.float32)
    big = lambda *lead: pltpu.VMEM(lead + (NST, CC), jnp.bfloat16)
    small = lambda *lead: pltpu.VMEM(lead + (TAIL_ROWS, TC), jnp.bfloat16)
    sem = lambda *shape: [pltpu.SemaphoreType.DMA(shape)] * 2
    vmem = pl.BlockSpec(memory_space=pltpu.VMEM)
    hbm = pl.BlockSpec(memory_space=pl.ANY)
    return pl.pallas_call(
        functools.partial(route_kernel, n, slots),
        out_shape=(
            jax.ShapeDtypeStruct((rows, INNER), jnp.bfloat16),
            jax.ShapeDtypeStruct((1, NST, INNER), jnp.bfloat16),
        ),
        in_specs=[pl.BlockSpec(memory_space=pltpu.SMEM)] + [hbm] * 3 + [vmem] * 10,
        out_specs=(hbm, hbm),
        scratch_shapes=[
            big(LANES, CHUNKS), small(LANES),
            pltpu.VMEM((rows, channels), jnp.bfloat16), f32(8 + rows, PW), f32(24, PW), f32(8, channels),
            f32(GROUPS, rows, rows), f32(pieces, rows, CC), f32(pieces, NST, CC),
            pltpu.VMEM((pieces, rows, CC), jnp.bfloat16), big(pieces), *sem(pieces),
            f32(8, HEADS), big(CHUNKS, LANES), small(LANES),
            big(steps), small(slots), big(steps), small(slots),
            big(steps), small(slots), big(steps), small(slots),
            big(CHUNKS, LANES - 1), small(LANES - 1),
            pltpu.SemaphoreType.DMA((2 + CHUNKS - EARLY,)),
            *sem(CHUNKS, LANES - 1),
            *sem(steps), *sem(slots), *sem(steps), *sem(slots),
            *sem(CHUNKS, LANES - 1), *sem(LANES - 1),
        ],
        compiler_params=pltpu.CompilerParams(
            collective_id=number, has_side_effects=True, vmem_limit_bytes=(34 + 2 * slots) * 2**20
        ),
        name=f"route{slots}",
    )(table, own, plane, plane_t, *terms, xbc, weight, bias, skip)


def settle_kernel(y_ref, f_ref, y_out, f_out, y_held, f_held, in_sem, out_sem):
    pieces = []
    for i in range(SETTLE):
        at = pl.ds(i * (y_ref.shape[0] // SETTLE), y_ref.shape[0] // SETTLE)
        pieces.append((y_ref.at[at], y_held.at[at], y_out.at[at]))
        at = pl.ds(i * (NST // SETTLE), NST // SETTLE)
        pieces.append((f_ref.at[0, at], f_held.at[at], f_out.at[0, at]))
    come = [pltpu.make_async_copy(a, b, in_sem.at[i]) for i, (a, b, _) in enumerate(pieces)]
    go = [pltpu.make_async_copy(b, c, out_sem.at[i]) for i, (_, b, c) in enumerate(pieces)]
    for copy in come:
        copy.start()
    for first, second in zip(come, go):
        first.wait()
        second.start()
    for copy in go:
        copy.wait()


def settle(y, final):
    hbm = pl.BlockSpec(memory_space=pl.ANY)
    return pl.pallas_call(
        settle_kernel,
        out_shape=(jax.ShapeDtypeStruct(y.shape, y.dtype), jax.ShapeDtypeStruct(final.shape, final.dtype)),
        in_specs=[hbm, hbm],
        out_specs=(hbm, hbm),
        scratch_shapes=[
            pltpu.VMEM(y.shape, y.dtype), pltpu.VMEM(final.shape[1:], final.dtype),
            pltpu.SemaphoreType.DMA((2 * SETTLE,)), pltpu.SemaphoreType.DMA((2 * SETTLE,)),
        ],
        compiler_params=pltpu.CompilerParams(vmem_limit_bytes=SETTLE_LIMIT),
        name="settle",
    )(y, final)


def local_routed(
    mesh, xbc, dt_raw, conv_weight, conv_bias, dt_bias, a_log, d_skip, cache_states, cache_tails,
    hit_owner, hit_slot, hit_spans, request_of,
):
    n = mesh.shape["req"]
    sizes = [3, 4, 5, n // 2]
    table, which, own, plane, plane_t, *terms = info(
        mesh, sizes, hit_owner, hit_slot, hit_spans, request_of, cache_states, cache_tails,
        dt_raw, dt_bias[None], a_log[None],
    )
    return settle(*lax.switch(
        which[0, 0],
        [functools.partial(route, n, size, 1 + i) for i, size in enumerate(sizes)],
        table, own, plane, plane_t, terms, xbc, conv_weight, conv_bias[None], d_skip[None],
    ))


def local(
    xbc, dt_raw, conv_weight, conv_bias, dt_bias, a_log, d_skip, cache_states, cache_tails,
    hit_owner, hit_slot, hit_spans, request_of,
):
    count = hit_owner.shape[0]
    rows = xbc.shape[0]
    mine = request_of[0]
    live = (hit_spans[mine] > 0).astype(jnp.int32)
    device = lax.axis_index("req")
    served = jnp.max(jnp.where(hit_owner == device, hit_slot, 0))
    send = lax.dynamic_slice_in_dim(cache_states, served, 1, 0).reshape(count, NST // count, INNER)
    number = jnp.broadcast_to(mine.astype(send.dtype), send.shape[:2] + (128,))
    parts = lax.all_to_all(
        jnp.concatenate([send, number], axis=2), "req", split_axis=0, concat_axis=0, tiled=True
    )
    every_request = parts[:, 0, INNER].astype(jnp.int32)
    own_tail = lax.dynamic_slice_in_dim(cache_tails, served, 1, 0)
    own_tail = jnp.pad(own_tail, ((0, 0), (0, 1), (0, 0)))
    every_tail = lax.all_gather(own_tail, "req", axis=0, tiled=True)[:, :3]
    owners = jnp.sum(
        jnp.where(every_request[:, None] == jnp.arange(count)[None, :], hit_owner[None, :], 0), axis=1
    )
    chosen = pick(parts, owners)
    start = lax.all_to_all(chosen, "req", split_axis=0, concat_axis=0, tiled=True).reshape(NST, INNER)

    tail = lax.dynamic_index_in_dim(every_tail, hit_owner[mine], 0, keepdims=False)
    tail = jnp.where(live > 0, tail, jnp.zeros_like(tail)).astype(jnp.float32)
    tail = jnp.pad(tail, ((5, 0), (0, 0)))
    step = jax.nn.softplus(dt_raw + dt_bias[None, :])
    below = jnp.tril(jnp.ones((rows, rows), jnp.float32))
    cum = jnp.dot(below, step * (-jnp.exp(a_log))[None, :], precision=lax.Precision.HIGHEST)
    last = cum[rows - 1]
    coef = jnp.exp(last[None, :] - cum) * step
    skip = jnp.repeat(d_skip, HEAD_DIM)[None, :]
    elast = jnp.repeat(jnp.exp(last), HEAD_DIM)[None, :]
    cumt = cum.T.reshape(STEPS, PER_STEP, rows)
    stept = step.T.reshape(STEPS, PER_STEP, rows)
    bias = conv_bias[None, :]

    first_b, first_c = INNER // NST, INNER // NST + GROUPS
    per = STEPS_PER_GROUP
    triple = lambda r: [
        pl.BlockSpec((r, COLS), lambda i: (0, i)),
        pl.BlockSpec((r, NST), lambda i: (0, first_b + i // per)),
        pl.BlockSpec((r, NST), lambda i: (0, first_c + i // per)),
    ]
    wide = lambda r: pl.BlockSpec((r, COLS), lambda i: (0, i))
    tall = pl.BlockSpec((1, rows, PER_STEP), lambda i: (i, 0, 0))
    flat = pl.BlockSpec((1, PER_STEP, rows), lambda i: (i, 0, 0))
    group = pl.BlockSpec((rows, NST), lambda i: (0, i // per))
    y_local, fresh, c_part = pl.pallas_call(
        local_kernel,
        grid=(STEPS,),
        out_shape=(
            jax.ShapeDtypeStruct((rows, INNER), jnp.float32),
            jax.ShapeDtypeStruct((NST, INNER), jnp.float32),
            jax.ShapeDtypeStruct((rows, GROUPS * NST), jnp.bfloat16),
        ),
        in_specs=triple(rows) + triple(8) + triple(4) + triple(1) + [tall, flat, flat, tall, wide(1)],
        out_specs=(wide(rows), wide(NST), group),
        scratch_shapes=[pltpu.VMEM((8 + rows, COLS), jnp.float32)],
        compiler_params=pltpu.CompilerParams(vmem_limit_bytes=58 * 2**20),
        cost_estimate=pl.CostEstimate(flops=10**9, bytes_accessed=40 * 10**6, transcendentals=4 * 10**6),
        name="local",
    )(xbc, xbc, xbc, tail, tail, tail, conv_weight, conv_weight, conv_weight, bias, bias, bias,
      by_step(cum), cumt, stept, by_step(coef), skip)

    return pl.pallas_call(
        state_kernel,
        grid=(STEPS,),
        out_shape=(
            jax.ShapeDtypeStruct((rows, INNER), jnp.bfloat16),
            jax.ShapeDtypeStruct((1, NST, INNER), jnp.bfloat16),
        ),
        in_specs=[pl.BlockSpec(memory_space=pltpu.SMEM), wide(NST), wide(rows), wide(NST), group, tall, wide(1)],
        out_specs=(wide(rows), pl.BlockSpec((1, NST, COLS), lambda i: (0, 0, i))),
        compiler_params=pltpu.CompilerParams(vmem_limit_bytes=58 * 2**20),
        name="state",
    )(live[None], start, y_local, fresh, c_part, by_step(jnp.exp(cum)), elast)


def solution(mesh):
    rows = P(("grp", "req"), None)
    slots = P(("grp", "req"), None, None)
    in_specs = (
        rows, rows, P(), P(), P(), P(), P(), slots, slots, P("grp"), P("grp"), P("grp"), P(("grp", "req")),
    )
    body = functools.partial(local_routed, mesh) if mesh.shape["req"] == 16 else local
    return jax.shard_map(body, mesh=mesh, in_specs=in_specs, out_specs=(rows, slots), check_vma=False)
```

```python
import functools

import jax
import jax.numpy as jnp
from jax import lax
from jax.experimental import pallas as pl
from jax.experimental.pallas import tpu as pltpu
from jax.sharding import PartitionSpec as P

HEADS = 128
HEAD_DIM = 64
GROUPS = 4
NST = 128
INNER = 8192
PER_STEP = 16
COLS = PER_STEP * HEAD_DIM
STEPS = HEADS // PER_STEP
STEPS_PER_GROUP = STEPS // GROUPS


def pick_kernel(index_ref, parts_ref, out_ref, sem):
    count = out_ref.shape[0]
    copies = []
    for i in range(count):
        copy = pltpu.make_async_copy(parts_ref.at[index_ref[i], :, pl.ds(0, INNER)], out_ref.at[i], sem.at[i])
        copy.start()
        copies.append(copy)
    for copy in copies:
        copy.wait()


def pick(parts, index):
    count = index.shape[0]
    return pl.pallas_call(
        pick_kernel,
        out_shape=jax.ShapeDtypeStruct((count, parts.shape[1], INNER), parts.dtype),
        in_specs=[pl.BlockSpec(memory_space=pltpu.SMEM), pl.BlockSpec(memory_space=pltpu.VMEM)],
        out_specs=pl.BlockSpec(memory_space=pl.ANY),
        scratch_shapes=[pltpu.SemaphoreType.DMA((count,))],
        compiler_params=pltpu.CompilerParams(vmem_limit_bytes=8 * 2**20),
        name="pick",
    )(index, parts)


def conv_block(pad, x_ref, tail_ref, w_ref, b_ref, width):
    rows = x_ref.shape[0]
    pad[0:8, 0:width] = tail_ref[...]
    pad[8 : 8 + rows, 0:width] = x_ref[...].astype(jnp.float32)
    v = jnp.broadcast_to(b_ref[...], (rows, width))
    for k in range(4):
        v = v + w_ref[k : k + 1, :] * pad[5 + k : 5 + k + rows, 0:width]
    return (v / (1.0 + jnp.exp(-v))).astype(jnp.bfloat16)


def local_kernel(
    x_ref, xb_ref, xc_ref, tx_ref, tb_ref, tc_ref, wx_ref, wb_ref, wc_ref, bx_ref, bb_ref, bc_ref,
    cum_ref, cumt_ref, stept_ref, coef_ref, skip_ref,
    y_ref, fresh_ref, c_out_ref, pad,
):
    rows = x_ref.shape[0]
    b_part = conv_block(pad, xb_ref, tb_ref, wb_ref, bb_ref, NST)
    c_part = conv_block(pad, xc_ref, tc_ref, wc_ref, bc_ref, NST)
    c_out_ref[...] = c_part
    x = conv_block(pad, x_ref, tx_ref, wx_ref, bx_ref, COLS)
    scores = lax.dot_general(c_part, b_part, (((1,), (1,)), ((), ())), preferred_element_type=jnp.float32)
    causal = lax.broadcasted_iota(jnp.int32, (rows, rows), 0) >= lax.broadcasted_iota(jnp.int32, (rows, rows), 1)
    scores = jnp.where(causal, scores, 0.0)
    low = lax.broadcasted_iota(jnp.int32, (rows, 128), 1) < HEAD_DIM
    cum = cum_ref[0]
    coef = coef_ref[0]
    zero = jnp.zeros((rows, 128), jnp.bfloat16)
    carried = []
    for j in range(0, PER_STEP, 2):
        xp = x[:, j * HEAD_DIM : (j + 2) * HEAD_DIM]
        mixes = []
        for h in (j, j + 1):
            decay = jnp.exp(jnp.minimum(cum[:, h : h + 1] - cumt_ref[0, h : h + 1, :], 0.0))
            mixes.append((scores * decay * stept_ref[0, h : h + 1, :]).astype(jnp.bfloat16))
        mix = jnp.concatenate(mixes, axis=1)
        both = jnp.concatenate([jnp.where(low, xp, zero), jnp.where(low, zero, xp)], axis=0)
        xf = xp.astype(jnp.float32)
        sl = slice(j * HEAD_DIM, (j + 2) * HEAD_DIM)
        y_ref[:, sl] = jnp.dot(mix, both, preferred_element_type=jnp.float32) + skip_ref[:, sl] * xf
        carried.append((jnp.where(low, coef[:, j : j + 1], coef[:, j + 1 : j + 2]) * xf).astype(jnp.bfloat16))
    fresh_ref[...] = lax.dot_general(
        b_part, jnp.concatenate(carried, axis=1), (((0,), (0,)), ((), ())), preferred_element_type=jnp.float32
    )


def state_kernel(live_ref, start_ref, y_ref, fresh_ref, c_ref, ecum_ref, elast_ref, y_out_ref, final_ref):
    rows = y_ref.shape[0]
    start = start_ref[...]
    start = jnp.where(live_ref[0] > 0, start, jnp.zeros_like(start))
    low = lax.broadcasted_iota(jnp.int32, (rows, 128), 1) < HEAD_DIM
    ecum = ecum_ref[0]
    ys = jnp.dot(c_ref[...], start, preferred_element_type=jnp.float32)
    for j in range(0, PER_STEP, 2):
        sl = slice(j * HEAD_DIM, (j + 2) * HEAD_DIM)
        factor = jnp.where(low, ecum[:, j : j + 1], ecum[:, j + 1 : j + 2])
        y_out_ref[:, sl] = (y_ref[:, sl] + factor * ys[:, sl]).astype(jnp.bfloat16)
    final_ref[0] = (elast_ref[...] * start.astype(jnp.float32) + fresh_ref[...]).astype(jnp.bfloat16)


def by_step(a):
    return a.reshape(a.shape[0], STEPS, PER_STEP).transpose(1, 0, 2)


LANES = 4
CHUNKS = 8
WIDE = INNER // LANES
CC = WIDE // CHUNKS
PW = 512
TC = WIDE // LANES
DEPTH = 4
EARLY = 2
AHEAD = 1
PACE = 3
TAIL_ROWS = 16
LAG = 4
SETTLE = 4
SETTLE_LIMIT = 60 * 2**20
MESH = pl.DeviceIdType.MESH


def masked_column(row, rows):
    sub = lax.broadcasted_iota(jnp.int32, (rows, 128), 0)
    lane = lax.broadcasted_iota(jnp.int32, (rows, 128), 1)
    return jnp.sum(jnp.where(sub == lane, jnp.broadcast_to(row, (rows, 128)), 0), axis=1, keepdims=True)


def destinations(wanted, n):
    planes = n // LANES
    sub = lax.broadcasted_iota(jnp.int32, (n, 128), 0) // LANES
    lane = lax.broadcasted_iota(jnp.int32, (n, 128), 1)
    hit = wanted == lane
    top = jnp.max(jnp.where(hit, sub, -1), axis=0, keepdims=True)
    low = jnp.min(jnp.where(hit, sub, planes), axis=0, keepdims=True)
    return top, low


def head_terms(dt_ref, dt_bias_ref, a_log_ref, cum_ref, cumt_ref, stept_ref, coef_ref, ecum_ref, elast_ref):
    rows = dt_ref.shape[0]
    step = jax.nn.softplus(dt_ref[...] + dt_bias_ref[...])
    below = (
        lax.broadcasted_iota(jnp.int32, (rows, rows), 0) >= lax.broadcasted_iota(jnp.int32, (rows, rows), 1)
    ).astype(jnp.float32)
    cum = jnp.dot(below, step * (-jnp.exp(a_log_ref[...])), precision=lax.Precision.HIGHEST,
                  preferred_element_type=jnp.float32)
    last = cum[rows - 1 : rows, :]
    cum_ref[...] = cum
    cumt_ref[...] = cum.T
    stept_ref[...] = step.T
    coef_ref[...] = jnp.exp(last - cum) * step
    ecum_ref[...] = jnp.exp(cum)
    elast_ref[...] = jnp.broadcast_to(jnp.exp(last), elast_ref.shape)


def info_kernel(
    groups, n, sizes, owner_ref, slot_ref, spans_ref, request_ref, states_ref, tails_ref,
    dt_ref, dt_bias_ref, a_log_ref,
    table_ref, which_ref, own_out, plane, plane_t, cum_ref, cumt_ref, stept_ref, coef_ref, ecum_ref, elast_ref,
    three, own, own_tail, packed, mine, rows, load_sem, send_sem, recv_sem, spread_s, spread_r, spread_ts, spread_tr,
    out_sem, needs, need_s, need_r,
):
    planes = n // LANES
    grp, me = lax.axis_index("grp"), lax.axis_index("req")
    z, l = lax.div(me, LANES), lax.rem(me, LANES)
    loads = []
    for i in range(states_ref.shape[0]):
        load = pltpu.make_async_copy(states_ref.at[i], three.at[i], load_sem.at[i])
        load.start()
        loads.append(load)
    barrier = pltpu.get_barrier_semaphore()

    def other(k):
        return grp, lax.rem(me + k, n)

    def counterpart(k):
        return lax.rem(grp + k, groups), me

    for k in range(1, n):
        pl.semaphore_signal(barrier, inc=1, device_id=other(k), device_id_type=MESH)
    for k in range(1, groups):
        pl.semaphore_signal(barrier, inc=1, device_id=counterpart(k), device_id_type=MESH)
    request = request_ref[0]
    wanted = jnp.where(spans_ref[request] > 0, owner_ref[request], -1)
    served = jnp.int32(0)
    for r in range(n):
        served = jnp.maximum(served, jnp.where(owner_ref[r] == me, slot_ref[r], 0))
    mine[...] = jnp.full((1, 128), wanted, jnp.int32)
    tail = tails_ref[served].astype(jnp.float32)
    packed[...] = jnp.zeros_like(packed)
    for q in range(-(-tail.shape[1] // WIDE)):
        for p in range(LANES):
            at = q * WIDE + p * TC
            if at < tail.shape[1]:
                packed[p, 3 * q : 3 * q + 3, :] = tail[:, at : at + TC]
    own_tail[...] = packed[...].astype(jnp.bfloat16)
    outs = []

    def put(src, dst):
        copy = pltpu.make_async_copy(src, dst, out_sem.at[len(outs)])
        copy.start()
        outs.append(copy)

    put(own_tail.at[l], plane_t.at[l])
    for load in loads:
        load.wait()

    def take(c):
        for p in range(LANES):
            own[p, c] = three[served, :, p * WIDE + c * CC : p * WIDE + (c + 1) * CC]

    for c in range(EARLY):
        take(c)
        put(own.at[l, c], plane.at[c, l])
    pl.semaphore_wait(barrier, n + groups - 2)
    for k in range(1, n):
        pltpu.make_async_remote_copy(
            src_ref=mine, dst_ref=rows.at[me], send_sem=send_sem, recv_sem=recv_sem,
            device_id=other(k), device_id_type=MESH,
        ).start()

    def spread(src, dst, ss, rs, k):
        return pltpu.make_async_remote_copy(
            src_ref=src, dst_ref=dst, send_sem=ss, recv_sem=rs,
            device_id=(grp, z * LANES + lax.rem(l + k, LANES)), device_id_type=MESH,
        )

    spreads = []
    for k in range(1, LANES):
        to, frm = lax.rem(l + k, LANES), lax.rem(l + LANES - k, LANES)
        sems = (spread_ts.at[k - 1], spread_tr.at[k - 1], k)
        spread(own_tail.at[to], plane_t.at[l], *sems).start()
        spreads.append((spread(own_tail.at[to], plane_t.at[l], *sems), spread(own_tail.at[frm], plane_t.at[frm], *sems)))
    for c in range(EARLY):
        for k in range(1, LANES):
            to, frm = lax.rem(l + k, LANES), lax.rem(l + LANES - k, LANES)
            sems = (spread_s.at[c, k - 1], spread_r.at[c, k - 1], k)
            spread(own.at[to, c], plane.at[c, l], *sems).start()
            spreads.append((spread(own.at[to, c], plane.at[c, l], *sems), spread(own.at[frm, c], plane.at[c, frm], *sems)))
    for c in range(EARLY, CHUNKS):
        take(c)
        for p in range(LANES):
            put(own.at[p, c], own_out.at[p, c])
    head_terms(dt_ref, dt_bias_ref, a_log_ref, cum_ref, cumt_ref, stept_ref, coef_ref, ecum_ref, elast_ref)
    everyone = rows.at[pl.ds(0, n - 1)]
    pltpu.make_async_copy(everyone, everyone, send_sem).wait()
    pltpu.make_async_copy(everyone, everyone, recv_sem).wait()
    rows[pl.ds(me, 1)] = mine[...].reshape(1, 1, 128)

    need = jnp.zeros((1, 1), jnp.int32)
    lane_row = lax.broadcasted_iota(jnp.int32, (1, 128), 1)
    home = lane_row // LANES
    wants = rows[0:n].reshape(n, 128)
    top, low = destinations(wants, n)
    for cut in range(planes - 1):
        up = jnp.sum(((home <= cut) & (top > cut) & (lane_row < n)).astype(jnp.int32), axis=1, keepdims=True)
        down = jnp.sum(((home > cut) & (low <= cut) & (lane_row < n)).astype(jnp.int32), axis=1, keepdims=True)
        need = jnp.maximum(need, jnp.maximum(up, down))
    needs[0] = jnp.broadcast_to(need, (1, 128))
    swaps = []
    for k in range(1, groups):
        swap = pltpu.make_async_remote_copy(
            src_ref=needs.at[0], dst_ref=needs.at[k], send_sem=need_s.at[k], recv_sem=need_r.at[k],
            device_id=counterpart(k), device_id_type=MESH,
        )
        swap.start()
        swaps.append(swap)

    sub = lax.broadcasted_iota(jnp.int32, (n, 128), 0)
    lane = lax.broadcasted_iota(jnp.int32, (n, 128), 1)
    wants_row = jnp.sum(jnp.where(sub == lane, wants, 0), axis=0, keepdims=True)
    col = lax.broadcasted_iota(jnp.int32, (n, 1), 0)
    col_home = col // LANES
    top_col, low_col = masked_column(top, n), masked_column(low, n)

    def up_set(where_home, where_top, cut):
        return (where_home <= cut) & (where_top > cut)

    def down_set(where_home, where_low, cut):
        return (where_home > cut) & (where_low <= cut)

    def rank(inside, key_row, key_col):
        ahead = inside & (key_row < key_col) & (lane_row < n)
        return jnp.sum(ahead.astype(jnp.int32), axis=1, keepdims=True)

    up_row, up_col = (planes - top) * n + lane_row, (planes - top_col) * n + col
    down_row, down_col = (low + 1) * n + lane_row, (low_col + 1) * n + col
    up_in = rank(up_set(home, top, z - 1), up_row, up_col)
    up_out = rank(up_set(home, top, z), up_row, up_col)
    down_in = rank(down_set(home, low, z), down_row, down_col)
    down_out = rank(down_set(home, low, z - 1), down_row, down_col)
    near = lax.rem(col, LANES)
    src_up = jnp.where(col_home == z, near, LANES + up_in)
    src_down = jnp.where(col_home == z, near, LANES + down_in)
    src_fin = jnp.where(col_home == z, near, jnp.where(col_home < z, LANES + up_in, LANES + n + down_in))
    sel_up = jnp.sum(jnp.where(up_set(col_home, top_col, z) & (up_out == lane), src_up, 0), axis=0, keepdims=True)
    sel_down = jnp.sum(jnp.where(down_set(col_home, low_col, z - 1) & (down_out == lane), src_down, 0), axis=0, keepdims=True)
    sel_fin = jnp.sum(jnp.where(wants_row == col, src_fin, 0), axis=0, keepdims=True)
    sel_fin = jnp.where(wants_row < 0, -1, sel_fin)
    table_ref[...] = jnp.zeros_like(table_ref)
    table_ref[0:1, :] = sel_up
    table_ref[1:2, :] = sel_down
    table_ref[2:3, :] = sel_fin
    for swap in swaps:
        swap.wait()
    for k in range(1, groups):
        need = jnp.maximum(need, needs[k][:, 0:1])
    which = jnp.zeros((1, 1), jnp.int32)
    for size in sizes[:-1]:
        which += (need > size).astype(jnp.int32)
    which_ref[...] = which
    for sent, come in spreads:
        sent.wait_send()
        come.wait_recv()
    for copy in outs:
        copy.wait()


def info(
    mesh, sizes, hit_owner, hit_slot, hit_spans, request_of, cache_states, cache_tails, dt_raw, dt_bias, a_log
):
    groups, n = mesh.shape["grp"], mesh.shape["req"]
    smem = pl.BlockSpec(memory_space=pltpu.SMEM)
    vmem = pl.BlockSpec(memory_space=pltpu.VMEM)
    hbm = pl.BlockSpec(memory_space=pl.ANY)
    rows = dt_raw.shape[0]
    bf16 = lambda *shape: jax.ShapeDtypeStruct(shape, jnp.bfloat16)
    f32 = lambda *shape: jax.ShapeDtypeStruct(shape, jnp.float32)
    sem = lambda *shape: [pltpu.SemaphoreType.DMA(shape)] * 2
    return pl.pallas_call(
        functools.partial(info_kernel, groups, n, sizes),
        out_shape=(
            jax.ShapeDtypeStruct((8, 128), jnp.int32),
            jax.ShapeDtypeStruct((1, 1), jnp.int32),
            bf16(LANES, CHUNKS, NST, CC),
            bf16(EARLY, LANES, NST, CC),
            bf16(LANES, TAIL_ROWS, TC),
            f32(rows, HEADS), f32(HEADS, rows), f32(HEADS, rows), f32(rows, HEADS), f32(rows, HEADS), f32(8, HEADS),
        ),
        in_specs=[smem] * 4 + [hbm] + [vmem] * 4,
        out_specs=(vmem, vmem, hbm, hbm, hbm) + (vmem,) * 6,
        scratch_shapes=[
            pltpu.VMEM(cache_states.shape, jnp.bfloat16),
            pltpu.VMEM((LANES, CHUNKS, NST, CC), jnp.bfloat16),
            pltpu.VMEM((LANES, TAIL_ROWS, TC), jnp.bfloat16),
            pltpu.VMEM((LANES, TAIL_ROWS, TC), jnp.float32),
            pltpu.VMEM((1, 128), jnp.int32),
            pltpu.VMEM((n, 1, 128), jnp.int32),
            pltpu.SemaphoreType.DMA((cache_states.shape[0],)),
            pltpu.SemaphoreType.DMA, pltpu.SemaphoreType.DMA,
            *sem(EARLY, LANES - 1), *sem(LANES - 1),
            pltpu.SemaphoreType.DMA((LANES * (CHUNKS - EARLY) + EARLY + 1,)),
            pltpu.VMEM((groups, 1, 128), jnp.int32), *sem(groups),
        ],
        compiler_params=pltpu.CompilerParams(collective_id=0, has_side_effects=True, vmem_limit_bytes=58 * 2**20),
        name="info",
    )(hit_owner, hit_slot, hit_spans, request_of, cache_states, cache_tails, dt_raw, dt_bias, a_log)


def conv(taps, bias, pad, rows):
    v = jnp.broadcast_to(bias, (rows, bias.shape[1]))
    for k in range(4):
        v = v + taps[k : k + 1, :] * pad[5 + k : 5 + k + rows, :]
    return (v / (1.0 + jnp.exp(-v))).astype(jnp.bfloat16)


def route_kernel(
    n, slots, tab, own, plane_in, plane_t_in,
    cum_ref, cumt_ref, stept_ref, coef_ref, ecum_ref, elast_ref, xbc_ref, weight_ref, bias_ref, skip_ref,
    y_out, final_out,
    start, tail_out, xs, pad, head_pad, tail_rows, scores_ref, y_local, fresh, y_stage, f_stage, y_sem, f_sem,
    skips, plane, plane_t, up_recv, up_recv_t, down_recv, down_recv_t,
    up_send, up_send_t, down_send, down_send_t, fin_send, fin_send_t,
    load_sem, spread_s, spread_r, up_s, up_r, up_ts, up_tr,
    down_s, down_r, down_ts, down_tr, fin_s, fin_r, fin_ts, fin_tr,
):
    planes = n // LANES
    steps = CHUNKS * slots
    grp, me = lax.axis_index("grp"), lax.axis_index("req")
    z, l = lax.div(me, LANES), lax.rem(me, LANES)
    first, last = z == 0, z == planes - 1

    def mate(k):
        return z * LANES + lax.rem(l + k, LANES)

    loads = [
        pltpu.make_async_copy(plane_t_in, plane_t, load_sem.at[0]),
        pltpu.make_async_copy(plane_in, plane.at[pl.ds(0, EARLY)], load_sem.at[1]),
    ]
    for c in range(EARLY, CHUNKS):
        loads.append(pltpu.make_async_copy(own.at[l, c], plane.at[c, l], load_sem.at[2 + c - EARLY]))
    for load in loads:
        load.start()
    barrier = pltpu.get_barrier_semaphore()
    for k in range(1, LANES):
        pl.semaphore_signal(barrier, inc=1, device_id=(grp, mate(k)), device_id_type=MESH)

    @pl.when(jnp.logical_not(first))
    def _():
        pl.semaphore_signal(barrier, inc=1, device_id=(grp, me - LANES), device_id_type=MESH)

    @pl.when(jnp.logical_not(last))
    def _():
        pl.semaphore_signal(barrier, inc=1, device_id=(grp, me + LANES), device_id_type=MESH)

    pl.semaphore_wait(barrier, LANES - 1 + jnp.where(first | last, 1, 2))

    def remote(src, dst, ss, rs, to):
        return pltpu.make_async_remote_copy(
            src_ref=src, dst_ref=dst, send_sem=ss, recv_sem=rs, device_id=(grp, to), device_id_type=MESH
        )

    def spread(c, k):
        to = lax.rem(l + k, LANES)
        return remote(own.at[to, c], plane.at[c, l], spread_s.at[c, k - 1], spread_r.at[c, k - 1], mate(k))

    def spread_from(c, k):
        frm = lax.rem(l + LANES - k, LANES)
        return remote(own.at[frm, c], plane.at[c, frm], spread_s.at[c, k - 1], spread_r.at[c, k - 1], mate(k))

    def up(s):
        return remote(up_send.at[s], up_recv.at[s], up_s.at[s], up_r.at[s], me + LANES)

    def up_tail(s):
        return remote(up_send_t.at[s], up_recv_t.at[s], up_ts.at[s], up_tr.at[s], me + LANES)

    def down(s):
        return remote(down_send.at[s], down_recv.at[s], down_s.at[s], down_r.at[s], me - LANES)

    def down_tail(s):
        return remote(down_send_t.at[s], down_recv_t.at[s], down_ts.at[s], down_tr.at[s], me - LANES)

    def fin(c, k):
        to = lax.rem(l + k, LANES)
        return remote(fin_send.at[c, k - 1], start.at[l, c], fin_s.at[c, k - 1], fin_r.at[c, k - 1], mate(k))

    def fin_from(c, k):
        frm = lax.rem(l + LANES - k, LANES)
        return remote(fin_send.at[c, k - 1], start.at[frm, c], fin_s.at[c, k - 1], fin_r.at[c, k - 1], mate(k))

    def fin_tail(k):
        return remote(fin_send_t.at[k - 1], tail_out.at[l], fin_ts.at[k - 1], fin_tr.at[k - 1], mate(k))

    def fin_tail_from(k):
        frm = lax.rem(l + LANES - k, LANES)
        return remote(fin_send_t.at[k - 1], tail_out.at[frm], fin_ts.at[k - 1], fin_tr.at[k - 1], mate(k))

    for c in range(EARLY, min(EARLY + AHEAD, CHUNKS)):
        for k in range(1, LANES):
            spread(c, k).start()
    rows = xbc_ref.shape[0]
    channels = xbc_ref.shape[1]
    pieces = channels // PW
    scans = INNER // PW
    first_b, first_c = INNER, INNER + GROUPS * NST
    low = lax.broadcasted_iota(jnp.int32, (rows, 128), 1) < HEAD_DIM
    low_n = lax.broadcasted_iota(jnp.int32, (NST, 128), 1) < HEAD_DIM

    def columns(i):
        return pl.ds(pl.multiple_of(i * PW, PW), PW)

    def conv_piece(i):
        at = columns(i)
        pad[0:8, :] = jnp.zeros((8, PW), jnp.float32)
        pad[8 : 8 + rows, :] = xbc_ref[:, at].astype(jnp.float32)
        xs[:, at] = conv(weight_ref[:, at], bias_ref[:, at], pad, rows)

    def head_piece(i, _):
        at = columns(i)
        head_pad[0:8, :] = tail_rows[:, at]
        head_pad[8:24, :] = xbc_ref[0:16, at].astype(jnp.float32)
        xs[0:16, at] = conv(weight_ref[:, at], bias_ref[:, at], head_pad, 16)
        return 0

    def with_tail():
        tail_rows[...] = jnp.zeros_like(tail_rows)
        for p in range(LANES):
            got = tail_out[p].astype(jnp.float32)
            for q in range(-(-channels // WIDE)):
                at = q * WIDE + p * TC
                if at < channels:
                    tail_rows[5:8, at : at + TC] = got[3 * q : 3 * q + 3, :]
        lax.fori_loop(scans, pieces, head_piece, 0)

    def score(g):
        causal = lax.broadcasted_iota(jnp.int32, (rows, rows), 0) >= lax.broadcasted_iota(jnp.int32, (rows, rows), 1)
        b = xs[:, pl.ds(pl.multiple_of(first_b + g * NST, NST), NST)]
        c = xs[:, pl.ds(pl.multiple_of(first_c + g * NST, NST), NST)]
        scores = lax.dot_general(c, b, (((1,), (1,)), ((), ())), preferred_element_type=jnp.float32)
        scores_ref[g] = jnp.where(causal, scores, 0.0)

    def turned(ref, head):
        return pltpu.roll(ref[...], lax.rem(128 - head, 128), axis=1)

    def scan_piece(p, c):
        i = p * (scans // LANES) + c
        heads = PW // HEAD_DIM
        at = columns(i)
        x = xs[:, at]
        scores = scores_ref[p]
        cum, coef, skip = turned(cum_ref, heads * i), turned(coef_ref, heads * i), turned(skips, heads * i)
        here = pl.ds(pl.multiple_of(i * heads, heads), heads)
        cumt, stept = cumt_ref[here, :], stept_ref[here, :]
        zero = jnp.zeros((rows, 128), jnp.bfloat16)
        ys, carried = [], []
        for j in range(0, heads, 2):
            xp = x[:, j * HEAD_DIM : (j + 2) * HEAD_DIM]
            mixes = []
            for h in (j, j + 1):
                decay = jnp.exp(jnp.minimum(cum[:, h : h + 1] - cumt[h : h + 1, :], 0.0))
                mixes.append((scores * decay * stept[h : h + 1, :]).astype(jnp.bfloat16))
            mix = jnp.concatenate(mixes, axis=1)
            both = jnp.concatenate([jnp.where(low, xp, zero), jnp.where(low, zero, xp)], axis=0)
            xf = xp.astype(jnp.float32)
            d = jnp.where(low[0:1], skip[0:1, j : j + 1], skip[0:1, j + 1 : j + 2])
            ys.append(jnp.dot(mix, both, preferred_element_type=jnp.float32) + d * xf)
            carried.append((jnp.where(low, coef[:, j : j + 1], coef[:, j + 1 : j + 2]) * xf).astype(jnp.bfloat16))
        per = CC // 128
        for u in range(PW // CC):
            y_local[i * (PW // CC) + u] = jnp.concatenate(ys[u * per : (u + 1) * per], axis=1)
        b = xs[:, pl.ds(pl.multiple_of(first_b + p * NST, NST), NST)]
        new = lax.dot_general(
            b, jnp.concatenate(carried, axis=1), (((0,), (0,)), ((), ())), preferred_element_type=jnp.float32
        )
        for u in range(PW // CC):
            fresh[i * (PW // CC) + u] = new[:, u * CC : (u + 1) * CC]

    def outputs(i):
        at = pl.ds(pl.multiple_of(i * CC, CC), CC)
        return (
            pltpu.make_async_copy(y_stage.at[i], y_out.at[:, at], y_sem.at[i]),
            pltpu.make_async_copy(f_stage.at[i], final_out.at[0, :, at], f_sem.at[i]),
        )

    def last_piece(p, c):
        i = p * CHUNKS + c
        held = start[p, c]
        ys = jnp.dot(xs[:, pl.ds(pl.multiple_of(first_c + p * NST, NST), NST)], held,
                     preferred_element_type=jnp.float32)
        heads = CC // HEAD_DIM
        ecum, elast = turned(ecum_ref, heads * i), turned(elast_ref, heads * i)
        for j in range(0, heads, 2):
            sl = slice(j * HEAD_DIM, (j + 2) * HEAD_DIM)
            factor = jnp.where(low, ecum[:, j : j + 1], ecum[:, j + 1 : j + 2])
            y_stage[i, :, sl] = (y_local[i, :, sl] + factor * ys[:, sl]).astype(jnp.bfloat16)
            kept = jnp.where(low_n[0:1], elast[0:1, j : j + 1], elast[0:1, j + 1 : j + 2])
            f_stage[i, :, sl] = (kept * held[:, sl].astype(jnp.float32) + fresh[i, :, sl]).astype(jnp.bfloat16)
        for copy in outputs(i):
            copy.start()

    def last_chunk(c):
        for k in range(1, LANES):
            fin_from(c, k).wait_recv()

        def one(p, _):
            last_piece(p, c)
            return 0

        lax.fori_loop(0, LANES, one, 0)

    ready = slots + LAG * (planes - 1)
    total = steps + LAG * (planes - 1)
    per_conv = -(-pieces // ready)
    after = ready + 3
    per_scan = -(-scans // (total - after))

    lead = after - ready - 1 + -(-LANES // per_scan)

    def compute(t):
        @pl.when(t < ready)
        def _():
            def one(u, _):
                i = t * per_conv + u

                @pl.when(i < pieces)
                def _():
                    conv_piece(i)

                return 0

            lax.fori_loop(0, per_conv, one, 0)

        @pl.when(t == ready)
        def _():
            for k in range(1, LANES):
                fin_tail_from(k).wait_recv()
            with_tail()

        part = t - ready - 1

        @pl.when((part >= 0) & (part < GROUPS))
        def _():
            score(part)
            lax.fori_loop(part * (scans // GROUPS), (part + 1) * (scans // GROUPS), head_piece, 0)

        @pl.when(t >= after)
        def _():
            def one(u, _):
                i = (t - after) * per_scan + u

                @pl.when(i < scans)
                def _():
                    scan_piece(lax.rem(i, LANES), lax.div(i, LANES))

                return 0

            lax.fori_loop(0, per_scan, one, 0)
            since = t - ready - lead

            @pl.when((since >= 0) & (lax.rem(jnp.maximum(since, 0), slots) == 0))
            def _():
                last_chunk(lax.div(since, slots))

    def fill(dst, at, sel, near, c, far, base, j, inner):
        value = near[c, 0]
        for p in range(1, LANES):
            value = lax.select_n(sel == p, value, near[c, p])
        dst[at] = value

        @pl.when(inner)
        def _():
            def one(i, _):
                dst[at] = lax.select_n(sel == LANES + i, dst[at], far[base + i])
                return 0

            lax.fori_loop(0, j + 1, one, 0)

    def fill_tail(dst, j, sel, far, inner):
        value = plane_t[0]
        for p in range(1, LANES):
            value = lax.select_n(sel == p, value, plane_t[p])
        dst[j] = value

        @pl.when(inner)
        def _():
            def one(i, _):
                dst[j] = lax.select_n(sel == LANES + i, dst[j], far[i])
                return 0

            lax.fori_loop(0, j + 1, one, 0)

    def tick(t, _):
        tp = t - LAG * jnp.minimum(z, planes - 1 - z)

        @pl.when((tp >= 0) & (tp < steps) & (lax.rem(jnp.maximum(tp, 0), slots) == 0))
        def _():
            c = lax.div(tp, slots)

            @pl.when(c >= EARLY)
            def _():
                for k in range(1, LANES):
                    spread_from(c, k).wait_recv()

        more = EARLY + AHEAD + lax.div(t, PACE)

        @pl.when((more < CHUNKS) & (lax.rem(t, PACE) == 0))
        def _():
            for k in range(1, LANES):
                spread(more, k).start()

        def along(s, row, edge_in, edge_out, copy, copy_tail, send, send_t, recv, recv_t):
            @pl.when((s >= 0) & (s < steps))
            def _():
                c, j = lax.div(s, slots), lax.rem(s, slots)
                inner = jnp.logical_not(edge_in)

                @pl.when(inner)
                def _():
                    @pl.when(c == 0)
                    def _():
                        copy_tail(j).wait_recv()

                    copy(s).wait_recv()

                @pl.when(jnp.logical_not(edge_out))
                def _():
                    sel = tab[row, j]

                    @pl.when(c == 0)
                    def _():
                        fill_tail(send_t, j, sel, recv_t, inner)
                        copy_tail(j).start()

                    fill(send, s, sel, plane, c, recv, c * slots, j, inner)

                    @pl.when(s >= DEPTH)
                    def _():
                        copy(s - DEPTH).wait_send()

                    copy(s).start()

        along(t - LAG * z, 0, first, last, up, up_tail, up_send, up_send_t, up_recv, up_recv_t)
        along(t - LAG * (planes - 1 - z), 1, last, first, down, down_tail, down_send, down_send_t, down_recv, down_recv_t)

        tf = t - LAG * jnp.maximum(z, planes - 1 - z)

        @pl.when((tf >= 0) & (tf < steps) & (lax.rem(jnp.maximum(tf, 0), slots) == slots - 1))
        def _():
            c = lax.div(tf, slots)
            sels = [tab[2, mate(k)] for k in range(LANES)]

            def choose(near, far_up, far_down, write, read):
                acc = [jnp.zeros(near(0).shape, jnp.bfloat16)] * LANES
                for p in range(LANES):
                    value = near(p)
                    acc = [lax.select_n(sel == p, a, value) for sel, a in zip(sels, acc)]
                for k in range(LANES):
                    write(k, acc[k])

                def far(get, base):
                    acc = [read(k) for k in range(LANES)]
                    for i in range(slots):
                        value = get(i)
                        acc = [lax.select_n(sel == base + i, a, value) for sel, a in zip(sels, acc)]
                    for k in range(LANES):
                        write(k, acc[k])

                @pl.when(jnp.logical_not(first))
                def _():
                    far(far_up, LANES)

                @pl.when(jnp.logical_not(last))
                def _():
                    far(far_down, LANES + n)

            def rows_of(b, _):
                at = pl.ds(pl.multiple_of(b * 16, 16), 16)

                def write(k, v):
                    if k == 0:
                        start[l, c, at] = v
                    else:
                        fin_send[c, k - 1, at] = v

                def read(k):
                    return start[l, c, at] if k == 0 else fin_send[c, k - 1, at]

                choose(lambda p: plane[c, p, at], lambda i: up_recv[c * slots + i, at],
                       lambda i: down_recv[c * slots + i, at], write, read)
                return 0

            lax.fori_loop(0, NST // 16, rows_of, 0)
            for k in range(1, LANES):
                fin(c, k).start()

            @pl.when(c == 0)
            def _():
                def write(k, v):
                    if k == 0:
                        tail_out[l] = v
                    else:
                        fin_send_t[k - 1] = v

                def read(k):
                    return tail_out[l] if k == 0 else fin_send_t[k - 1]

                choose(lambda p: plane_t[p], lambda i: up_recv_t[i], lambda i: down_recv_t[i], write, read)
                for k in range(1, LANES):
                    fin_tail(k).start()

        compute(t)
        return 0

    skips[...] = jnp.broadcast_to(skip_ref[...], skips.shape)
    for load in loads:
        load.wait()
    lax.fori_loop(0, total, tick, 0)
    for c in range((total - 1 - ready - lead) // slots + 1, CHUNKS):
        last_chunk(c)

    for k in range(1, LANES):
        fin_tail(k).wait_send()
        for c in range(CHUNKS):
            if c >= EARLY:
                spread(c, k).wait_send()
            fin(c, k).wait_send()

    @pl.when(jnp.logical_not(last))
    def _():
        for j in range(slots):
            up_tail(j).wait_send()
        for s in range(max(steps - DEPTH, 0), steps):
            up(s).wait_send()

    @pl.when(jnp.logical_not(first))
    def _():
        for j in range(slots):
            down_tail(j).wait_send()
        for s in range(max(steps - DEPTH, 0), steps):
            down(s).wait_send()

    for i in range(LANES * CHUNKS):
        for copy in outputs(i):
            copy.wait()


def route(n, slots, number, table, own, plane, plane_t, terms, xbc, weight, bias, skip):
    steps = CHUNKS * slots
    rows, channels = xbc.shape
    pieces = LANES * CHUNKS
    f32 = lambda *shape: pltpu.VMEM(shape, jnp.float32)
    big = lambda *lead: pltpu.VMEM(lead + (NST, CC), jnp.bfloat16)
    small = lambda *lead: pltpu.VMEM(lead + (TAIL_ROWS, TC), jnp.bfloat16)
    sem = lambda *shape: [pltpu.SemaphoreType.DMA(shape)] * 2
    vmem = pl.BlockSpec(memory_space=pltpu.VMEM)
    hbm = pl.BlockSpec(memory_space=pl.ANY)
    return pl.pallas_call(
        functools.partial(route_kernel, n, slots),
        out_shape=(
            jax.ShapeDtypeStruct((rows, INNER), jnp.bfloat16),
            jax.ShapeDtypeStruct((1, NST, INNER), jnp.bfloat16),
        ),
        in_specs=[pl.BlockSpec(memory_space=pltpu.SMEM)] + [hbm] * 3 + [vmem] * 10,
        out_specs=(hbm, hbm),
        scratch_shapes=[
            big(LANES, CHUNKS), small(LANES),
            pltpu.VMEM((rows, channels), jnp.bfloat16), f32(8 + rows, PW), f32(24, PW), f32(8, channels),
            f32(GROUPS, rows, rows), f32(pieces, rows, CC), f32(pieces, NST, CC),
            pltpu.VMEM((pieces, rows, CC), jnp.bfloat16), big(pieces), *sem(pieces),
            f32(8, HEADS), big(CHUNKS, LANES), small(LANES),
            big(steps), small(slots), big(steps), small(slots),
            big(steps), small(slots), big(steps), small(slots),
            big(CHUNKS, LANES - 1), small(LANES - 1),
            pltpu.SemaphoreType.DMA((2 + CHUNKS - EARLY,)),
            *sem(CHUNKS, LANES - 1),
            *sem(steps), *sem(slots), *sem(steps), *sem(slots),
            *sem(CHUNKS, LANES - 1), *sem(LANES - 1),
        ],
        compiler_params=pltpu.CompilerParams(
            collective_id=number, has_side_effects=True, vmem_limit_bytes=(34 + 2 * slots) * 2**20
        ),
        name=f"route{slots}",
    )(table, own, plane, plane_t, *terms, xbc, weight, bias, skip)


def settle_kernel(y_ref, f_ref, y_out, f_out, y_held, f_held, in_sem, out_sem):
    pieces = []
    for i in range(SETTLE):
        at = pl.ds(i * (y_ref.shape[0] // SETTLE), y_ref.shape[0] // SETTLE)
        pieces.append((y_ref.at[at], y_held.at[at], y_out.at[at]))
        at = pl.ds(i * (NST // SETTLE), NST // SETTLE)
        pieces.append((f_ref.at[0, at], f_held.at[at], f_out.at[0, at]))
    come = [pltpu.make_async_copy(a, b, in_sem.at[i]) for i, (a, b, _) in enumerate(pieces)]
    go = [pltpu.make_async_copy(b, c, out_sem.at[i]) for i, (_, b, c) in enumerate(pieces)]
    for copy in come:
        copy.start()
    for first, second in zip(come, go):
        first.wait()
        second.start()
    for copy in go:
        copy.wait()


def settle(y, final):
    hbm = pl.BlockSpec(memory_space=pl.ANY)
    return pl.pallas_call(
        settle_kernel,
        out_shape=(jax.ShapeDtypeStruct(y.shape, y.dtype), jax.ShapeDtypeStruct(final.shape, final.dtype)),
        in_specs=[hbm, hbm],
        out_specs=(hbm, hbm),
        scratch_shapes=[
            pltpu.VMEM(y.shape, y.dtype), pltpu.VMEM(final.shape[1:], final.dtype),
            pltpu.SemaphoreType.DMA((2 * SETTLE,)), pltpu.SemaphoreType.DMA((2 * SETTLE,)),
        ],
        compiler_params=pltpu.CompilerParams(vmem_limit_bytes=SETTLE_LIMIT),
        name="settle",
    )(y, final)


def local_routed(
    mesh, xbc, dt_raw, conv_weight, conv_bias, dt_bias, a_log, d_skip, cache_states, cache_tails,
    hit_owner, hit_slot, hit_spans, request_of,
):
    n = mesh.shape["req"]
    sizes = [2, 3, 4, 5, n // 2]
    table, which, own, plane, plane_t, *terms = info(
        mesh, sizes, hit_owner, hit_slot, hit_spans, request_of, cache_states, cache_tails,
        dt_raw, dt_bias[None], a_log[None],
    )
    return settle(*lax.switch(
        which[0, 0],
        [functools.partial(route, n, size, 1 + i) for i, size in enumerate(sizes)],
        table, own, plane, plane_t, terms, xbc, conv_weight, conv_bias[None], d_skip[None],
    ))


def local(
    xbc, dt_raw, conv_weight, conv_bias, dt_bias, a_log, d_skip, cache_states, cache_tails,
    hit_owner, hit_slot, hit_spans, request_of,
):
    count = hit_owner.shape[0]
    rows = xbc.shape[0]
    mine = request_of[0]
    live = (hit_spans[mine] > 0).astype(jnp.int32)
    device = lax.axis_index("req")
    served = jnp.max(jnp.where(hit_owner == device, hit_slot, 0))
    send = lax.dynamic_slice_in_dim(cache_states, served, 1, 0).reshape(count, NST // count, INNER)
    number = jnp.broadcast_to(mine.astype(send.dtype), send.shape[:2] + (128,))
    parts = lax.all_to_all(
        jnp.concatenate([send, number], axis=2), "req", split_axis=0, concat_axis=0, tiled=True
    )
    every_request = parts[:, 0, INNER].astype(jnp.int32)
    own_tail = lax.dynamic_slice_in_dim(cache_tails, served, 1, 0)
    own_tail = jnp.pad(own_tail, ((0, 0), (0, 1), (0, 0)))
    every_tail = lax.all_gather(own_tail, "req", axis=0, tiled=True)[:, :3]
    owners = jnp.sum(
        jnp.where(every_request[:, None] == jnp.arange(count)[None, :], hit_owner[None, :], 0), axis=1
    )
    chosen = pick(parts, owners)
    start = lax.all_to_all(chosen, "req", split_axis=0, concat_axis=0, tiled=True).reshape(NST, INNER)

    tail = lax.dynamic_index_in_dim(every_tail, hit_owner[mine], 0, keepdims=False)
    tail = jnp.where(live > 0, tail, jnp.zeros_like(tail)).astype(jnp.float32)
    tail = jnp.pad(tail, ((5, 0), (0, 0)))
    step = jax.nn.softplus(dt_raw + dt_bias[None, :])
    below = jnp.tril(jnp.ones((rows, rows), jnp.float32))
    cum = jnp.dot(below, step * (-jnp.exp(a_log))[None, :], precision=lax.Precision.HIGHEST)
    last = cum[rows - 1]
    coef = jnp.exp(last[None, :] - cum) * step
    skip = jnp.repeat(d_skip, HEAD_DIM)[None, :]
    elast = jnp.repeat(jnp.exp(last), HEAD_DIM)[None, :]
    cumt = cum.T.reshape(STEPS, PER_STEP, rows)
    stept = step.T.reshape(STEPS, PER_STEP, rows)
    bias = conv_bias[None, :]

    first_b, first_c = INNER // NST, INNER // NST + GROUPS
    per = STEPS_PER_GROUP
    triple = lambda r: [
        pl.BlockSpec((r, COLS), lambda i: (0, i)),
        pl.BlockSpec((r, NST), lambda i: (0, first_b + i // per)),
        pl.BlockSpec((r, NST), lambda i: (0, first_c + i // per)),
    ]
    wide = lambda r: pl.BlockSpec((r, COLS), lambda i: (0, i))
    tall = pl.BlockSpec((1, rows, PER_STEP), lambda i: (i, 0, 0))
    flat = pl.BlockSpec((1, PER_STEP, rows), lambda i: (i, 0, 0))
    group = pl.BlockSpec((rows, NST), lambda i: (0, i // per))
    y_local, fresh, c_part = pl.pallas_call(
        local_kernel,
        grid=(STEPS,),
        out_shape=(
            jax.ShapeDtypeStruct((rows, INNER), jnp.float32),
            jax.ShapeDtypeStruct((NST, INNER), jnp.float32),
            jax.ShapeDtypeStruct((rows, GROUPS * NST), jnp.bfloat16),
        ),
        in_specs=triple(rows) + triple(8) + triple(4) + triple(1) + [tall, flat, flat, tall, wide(1)],
        out_specs=(wide(rows), wide(NST), group),
        scratch_shapes=[pltpu.VMEM((8 + rows, COLS), jnp.float32)],
        compiler_params=pltpu.CompilerParams(vmem_limit_bytes=58 * 2**20),
        cost_estimate=pl.CostEstimate(flops=10**9, bytes_accessed=40 * 10**6, transcendentals=4 * 10**6),
        name="local",
    )(xbc, xbc, xbc, tail, tail, tail, conv_weight, conv_weight, conv_weight, bias, bias, bias,
      by_step(cum), cumt, stept, by_step(coef), skip)

    return pl.pallas_call(
        state_kernel,
        grid=(STEPS,),
        out_shape=(
            jax.ShapeDtypeStruct((rows, INNER), jnp.bfloat16),
            jax.ShapeDtypeStruct((1, NST, INNER), jnp.bfloat16),
        ),
        in_specs=[pl.BlockSpec(memory_space=pltpu.SMEM), wide(NST), wide(rows), wide(NST), group, tall, wide(1)],
        out_specs=(wide(rows), pl.BlockSpec((1, NST, COLS), lambda i: (0, 0, i))),
        compiler_params=pltpu.CompilerParams(vmem_limit_bytes=58 * 2**20),
        name="state",
    )(live[None], start, y_local, fresh, c_part, by_step(jnp.exp(cum)), elast)


def solution(mesh):
    rows = P(("grp", "req"), None)
    slots = P(("grp", "req"), None, None)
    in_specs = (
        rows, rows, P(), P(), P(), P(), P(), slots, slots, P("grp"), P("grp"), P("grp"), P(("grp", "req")),
    )
    body = functools.partial(local_routed, mesh) if mesh.shape["req"] == 16 else local
    return jax.shard_map(body, mesh=mesh, in_specs=in_specs, out_specs=(rows, slots), check_vma=False)
```

```python
import functools

import jax
import jax.numpy as jnp
from jax import lax
from jax.experimental import pallas as pl
from jax.experimental.pallas import tpu as pltpu
from jax.sharding import PartitionSpec as P

HEADS = 128
HEAD_DIM = 64
GROUPS = 4
NST = 128
INNER = 8192
PER_STEP = 16
COLS = PER_STEP * HEAD_DIM
STEPS = HEADS // PER_STEP
STEPS_PER_GROUP = STEPS // GROUPS


def pick_kernel(index_ref, parts_ref, out_ref, sem):
    count = out_ref.shape[0]
    copies = []
    for i in range(count):
        copy = pltpu.make_async_copy(parts_ref.at[index_ref[i], :, pl.ds(0, INNER)], out_ref.at[i], sem.at[i])
        copy.start()
        copies.append(copy)
    for copy in copies:
        copy.wait()


def pick(parts, index):
    count = index.shape[0]
    return pl.pallas_call(
        pick_kernel,
        out_shape=jax.ShapeDtypeStruct((count, parts.shape[1], INNER), parts.dtype),
        in_specs=[pl.BlockSpec(memory_space=pltpu.SMEM), pl.BlockSpec(memory_space=pltpu.VMEM)],
        out_specs=pl.BlockSpec(memory_space=pl.ANY),
        scratch_shapes=[pltpu.SemaphoreType.DMA((count,))],
        compiler_params=pltpu.CompilerParams(vmem_limit_bytes=8 * 2**20),
        name="pick",
    )(index, parts)


def conv_block(pad, x_ref, tail_ref, w_ref, b_ref, width):
    rows = x_ref.shape[0]
    pad[0:8, 0:width] = tail_ref[...]
    pad[8 : 8 + rows, 0:width] = x_ref[...].astype(jnp.float32)
    v = jnp.broadcast_to(b_ref[...], (rows, width))
    for k in range(4):
        v = v + w_ref[k : k + 1, :] * pad[5 + k : 5 + k + rows, 0:width]
    return (v / (1.0 + jnp.exp(-v))).astype(jnp.bfloat16)


def local_kernel(
    x_ref, xb_ref, xc_ref, tx_ref, tb_ref, tc_ref, wx_ref, wb_ref, wc_ref, bx_ref, bb_ref, bc_ref,
    cum_ref, cumt_ref, stept_ref, coef_ref, skip_ref,
    y_ref, fresh_ref, c_out_ref, pad,
):
    rows = x_ref.shape[0]
    b_part = conv_block(pad, xb_ref, tb_ref, wb_ref, bb_ref, NST)
    c_part = conv_block(pad, xc_ref, tc_ref, wc_ref, bc_ref, NST)
    c_out_ref[...] = c_part
    x = conv_block(pad, x_ref, tx_ref, wx_ref, bx_ref, COLS)
    scores = lax.dot_general(c_part, b_part, (((1,), (1,)), ((), ())), preferred_element_type=jnp.float32)
    causal = lax.broadcasted_iota(jnp.int32, (rows, rows), 0) >= lax.broadcasted_iota(jnp.int32, (rows, rows), 1)
    scores = jnp.where(causal, scores, 0.0)
    low = lax.broadcasted_iota(jnp.int32, (rows, 128), 1) < HEAD_DIM
    cum = cum_ref[0]
    coef = coef_ref[0]
    zero = jnp.zeros((rows, 128), jnp.bfloat16)
    carried = []
    for j in range(0, PER_STEP, 2):
        xp = x[:, j * HEAD_DIM : (j + 2) * HEAD_DIM]
        mixes = []
        for h in (j, j + 1):
            decay = jnp.exp(jnp.minimum(cum[:, h : h + 1] - cumt_ref[0, h : h + 1, :], 0.0))
            mixes.append((scores * decay * stept_ref[0, h : h + 1, :]).astype(jnp.bfloat16))
        mix = jnp.concatenate(mixes, axis=1)
        both = jnp.concatenate([jnp.where(low, xp, zero), jnp.where(low, zero, xp)], axis=0)
        xf = xp.astype(jnp.float32)
        sl = slice(j * HEAD_DIM, (j + 2) * HEAD_DIM)
        y_ref[:, sl] = jnp.dot(mix, both, preferred_element_type=jnp.float32) + skip_ref[:, sl] * xf
        carried.append((jnp.where(low, coef[:, j : j + 1], coef[:, j + 1 : j + 2]) * xf).astype(jnp.bfloat16))
    fresh_ref[...] = lax.dot_general(
        b_part, jnp.concatenate(carried, axis=1), (((0,), (0,)), ((), ())), preferred_element_type=jnp.float32
    )


def state_kernel(live_ref, start_ref, y_ref, fresh_ref, c_ref, ecum_ref, elast_ref, y_out_ref, final_ref):
    rows = y_ref.shape[0]
    start = start_ref[...]
    start = jnp.where(live_ref[0] > 0, start, jnp.zeros_like(start))
    low = lax.broadcasted_iota(jnp.int32, (rows, 128), 1) < HEAD_DIM
    ecum = ecum_ref[0]
    ys = jnp.dot(c_ref[...], start, preferred_element_type=jnp.float32)
    for j in range(0, PER_STEP, 2):
        sl = slice(j * HEAD_DIM, (j + 2) * HEAD_DIM)
        factor = jnp.where(low, ecum[:, j : j + 1], ecum[:, j + 1 : j + 2])
        y_out_ref[:, sl] = (y_ref[:, sl] + factor * ys[:, sl]).astype(jnp.bfloat16)
    final_ref[0] = (elast_ref[...] * start.astype(jnp.float32) + fresh_ref[...]).astype(jnp.bfloat16)


def by_step(a):
    return a.reshape(a.shape[0], STEPS, PER_STEP).transpose(1, 0, 2)


LANES = 4
CHUNKS = 8
WIDE = INNER // LANES
CC = WIDE // CHUNKS
PW = 512
TC = WIDE // LANES
DEPTH = 4
EARLY = 2
AHEAD = 1
PACE = 3
TAIL_ROWS = 16
LAG = 4
SETTLE = 4
SETTLE_LIMIT = 60 * 2**20
MESH = pl.DeviceIdType.MESH


def masked_column(row, rows):
    sub = lax.broadcasted_iota(jnp.int32, (rows, 128), 0)
    lane = lax.broadcasted_iota(jnp.int32, (rows, 128), 1)
    return jnp.sum(jnp.where(sub == lane, jnp.broadcast_to(row, (rows, 128)), 0), axis=1, keepdims=True)


def destinations(wanted, n):
    planes = n // LANES
    sub = lax.broadcasted_iota(jnp.int32, (n, 128), 0) // LANES
    lane = lax.broadcasted_iota(jnp.int32, (n, 128), 1)
    hit = wanted == lane
    top = jnp.max(jnp.where(hit, sub, -1), axis=0, keepdims=True)
    low = jnp.min(jnp.where(hit, sub, planes), axis=0, keepdims=True)
    return top, low


def head_terms(dt_ref, dt_bias_ref, a_log_ref, cum_ref, cumt_ref, stept_ref, coef_ref, ecum_ref, elast_ref):
    rows = dt_ref.shape[0]
    step = jax.nn.softplus(dt_ref[...] + dt_bias_ref[...])
    below = (
        lax.broadcasted_iota(jnp.int32, (rows, rows), 0) >= lax.broadcasted_iota(jnp.int32, (rows, rows), 1)
    ).astype(jnp.float32)
    cum = jnp.dot(below, step * (-jnp.exp(a_log_ref[...])), precision=lax.Precision.HIGHEST,
                  preferred_element_type=jnp.float32)
    last = cum[rows - 1 : rows, :]
    cum_ref[...] = cum
    cumt_ref[...] = cum.T
    stept_ref[...] = step.T
    coef_ref[...] = jnp.exp(last - cum) * step
    ecum_ref[...] = jnp.exp(cum)
    elast_ref[...] = jnp.broadcast_to(jnp.exp(last), elast_ref.shape)


def info_kernel(
    groups, n, sizes, owner_ref, slot_ref, spans_ref, request_ref, states_ref, tails_ref,
    dt_ref, dt_bias_ref, a_log_ref,
    table_ref, which_ref, own_out, plane, plane_t, cum_ref, cumt_ref, stept_ref, coef_ref, ecum_ref, elast_ref,
    three, own, own_tail, packed, mine, rows, load_sem, send_sem, recv_sem, spread_s, spread_r, spread_ts, spread_tr,
    out_sem, needs, need_s, need_r,
):
    planes = n // LANES
    grp, me = lax.axis_index("grp"), lax.axis_index("req")
    z, l = lax.div(me, LANES), lax.rem(me, LANES)
    loads = []
    for i in range(states_ref.shape[0]):
        load = pltpu.make_async_copy(states_ref.at[i], three.at[i], load_sem.at[i])
        load.start()
        loads.append(load)
    barrier = pltpu.get_barrier_semaphore()

    def other(k):
        return grp, lax.rem(me + k, n)

    def counterpart(k):
        return lax.rem(grp + k, groups), me

    for k in range(1, n):
        pl.semaphore_signal(barrier, inc=1, device_id=other(k), device_id_type=MESH)
    for k in range(1, groups):
        pl.semaphore_signal(barrier, inc=1, device_id=counterpart(k), device_id_type=MESH)
    request = request_ref[0]
    wanted = jnp.where(spans_ref[request] > 0, owner_ref[request], -1)
    served = jnp.int32(0)
    for r in range(n):
        served = jnp.maximum(served, jnp.where(owner_ref[r] == me, slot_ref[r], 0))
    mine[...] = jnp.full((1, 128), wanted, jnp.int32)
    tail = tails_ref[served].astype(jnp.float32)
    packed[...] = jnp.zeros_like(packed)
    for q in range(-(-tail.shape[1] // WIDE)):
        for p in range(LANES):
            at = q * WIDE + p * TC
            if at < tail.shape[1]:
                packed[p, 3 * q : 3 * q + 3, :] = tail[:, at : at + TC]
    own_tail[...] = packed[...].astype(jnp.bfloat16)
    outs = []

    def put(src, dst):
        copy = pltpu.make_async_copy(src, dst, out_sem.at[len(outs)])
        copy.start()
        outs.append(copy)

    put(own_tail.at[l], plane_t.at[l])
    for load in loads:
        load.wait()

    def take(c):
        for p in range(LANES):
            own[p, c] = three[served, :, p * WIDE + c * CC : p * WIDE + (c + 1) * CC]

    for c in range(EARLY):
        take(c)
        put(own.at[l, c], plane.at[c, l])
    pl.semaphore_wait(barrier, n + groups - 2)
    for k in range(1, n):
        pltpu.make_async_remote_copy(
            src_ref=mine, dst_ref=rows.at[me], send_sem=send_sem, recv_sem=recv_sem,
            device_id=other(k), device_id_type=MESH,
        ).start()

    def spread(src, dst, ss, rs, k):
        return pltpu.make_async_remote_copy(
            src_ref=src, dst_ref=dst, send_sem=ss, recv_sem=rs,
            device_id=(grp, z * LANES + lax.rem(l + k, LANES)), device_id_type=MESH,
        )

    spreads = []
    for k in range(1, LANES):
        to, frm = lax.rem(l + k, LANES), lax.rem(l + LANES - k, LANES)
        sems = (spread_ts.at[k - 1], spread_tr.at[k - 1], k)
        spread(own_tail.at[to], plane_t.at[l], *sems).start()
        spreads.append((spread(own_tail.at[to], plane_t.at[l], *sems), spread(own_tail.at[frm], plane_t.at[frm], *sems)))
    for c in range(EARLY):
        for k in range(1, LANES):
            to, frm = lax.rem(l + k, LANES), lax.rem(l + LANES - k, LANES)
            sems = (spread_s.at[c, k - 1], spread_r.at[c, k - 1], k)
            spread(own.at[to, c], plane.at[c, l], *sems).start()
            spreads.append((spread(own.at[to, c], plane.at[c, l], *sems), spread(own.at[frm, c], plane.at[c, frm], *sems)))
    for c in range(EARLY, CHUNKS):
        take(c)
        for p in range(LANES):
            put(own.at[p, c], own_out.at[p, c])
    head_terms(dt_ref, dt_bias_ref, a_log_ref, cum_ref, cumt_ref, stept_ref, coef_ref, ecum_ref, elast_ref)
    everyone = rows.at[pl.ds(0, n - 1)]
    pltpu.make_async_copy(everyone, everyone, send_sem).wait()
    pltpu.make_async_copy(everyone, everyone, recv_sem).wait()
    rows[pl.ds(me, 1)] = mine[...].reshape(1, 1, 128)

    need = jnp.zeros((1, 1), jnp.int32)
    lane_row = lax.broadcasted_iota(jnp.int32, (1, 128), 1)
    home = lane_row // LANES
    wants = rows[0:n].reshape(n, 128)
    top, low = destinations(wants, n)
    for cut in range(planes - 1):
        up = jnp.sum(((home <= cut) & (top > cut) & (lane_row < n)).astype(jnp.int32), axis=1, keepdims=True)
        down = jnp.sum(((home > cut) & (low <= cut) & (lane_row < n)).astype(jnp.int32), axis=1, keepdims=True)
        need = jnp.maximum(need, jnp.maximum(up, down))
    needs[0] = jnp.broadcast_to(need, (1, 128))
    swaps = []
    for k in range(1, groups):
        swap = pltpu.make_async_remote_copy(
            src_ref=needs.at[0], dst_ref=needs.at[k], send_sem=need_s.at[k], recv_sem=need_r.at[k],
            device_id=counterpart(k), device_id_type=MESH,
        )
        swap.start()
        swaps.append(swap)

    sub = lax.broadcasted_iota(jnp.int32, (n, 128), 0)
    lane = lax.broadcasted_iota(jnp.int32, (n, 128), 1)
    wants_row = jnp.sum(jnp.where(sub == lane, wants, 0), axis=0, keepdims=True)
    col = lax.broadcasted_iota(jnp.int32, (n, 1), 0)
    col_home = col // LANES
    top_col, low_col = masked_column(top, n), masked_column(low, n)

    def up_set(where_home, where_top, cut):
        return (where_home <= cut) & (where_top > cut)

    def down_set(where_home, where_low, cut):
        return (where_home > cut) & (where_low <= cut)

    def rank(inside, key_row, key_col):
        ahead = inside & (key_row < key_col) & (lane_row < n)
        return jnp.sum(ahead.astype(jnp.int32), axis=1, keepdims=True)

    up_row, up_col = (planes - top) * n + lane_row, (planes - top_col) * n + col
    down_row, down_col = (low + 1) * n + lane_row, (low_col + 1) * n + col
    up_in = rank(up_set(home, top, z - 1), up_row, up_col)
    up_out = rank(up_set(home, top, z), up_row, up_col)
    down_in = rank(down_set(home, low, z), down_row, down_col)
    down_out = rank(down_set(home, low, z - 1), down_row, down_col)
    near = lax.rem(col, LANES)
    src_up = jnp.where(col_home == z, near, LANES + up_in)
    src_down = jnp.where(col_home == z, near, LANES + down_in)
    src_fin = jnp.where(col_home == z, near, jnp.where(col_home < z, LANES + up_in, LANES + n + down_in))
    sel_up = jnp.sum(jnp.where(up_set(col_home, top_col, z) & (up_out == lane), src_up, 0), axis=0, keepdims=True)
    sel_down = jnp.sum(jnp.where(down_set(col_home, low_col, z - 1) & (down_out == lane), src_down, 0), axis=0, keepdims=True)
    sel_fin = jnp.sum(jnp.where(wants_row == col, src_fin, 0), axis=0, keepdims=True)
    sel_fin = jnp.where(wants_row < 0, -1, sel_fin)
    table_ref[...] = jnp.zeros_like(table_ref)
    table_ref[0:1, :] = sel_up
    table_ref[1:2, :] = sel_down
    table_ref[2:3, :] = sel_fin
    for swap in swaps:
        swap.wait()
    for k in range(1, groups):
        need = jnp.maximum(need, needs[k][:, 0:1])
    which = jnp.zeros((1, 1), jnp.int32)
    for size in sizes[:-1]:
        which += (need > size).astype(jnp.int32)
    which_ref[...] = which
    for sent, come in spreads:
        sent.wait_send()
        come.wait_recv()
    for copy in outs:
        copy.wait()


def info(
    mesh, sizes, hit_owner, hit_slot, hit_spans, request_of, cache_states, cache_tails, dt_raw, dt_bias, a_log
):
    groups, n = mesh.shape["grp"], mesh.shape["req"]
    smem = pl.BlockSpec(memory_space=pltpu.SMEM)
    vmem = pl.BlockSpec(memory_space=pltpu.VMEM)
    hbm = pl.BlockSpec(memory_space=pl.ANY)
    rows = dt_raw.shape[0]
    bf16 = lambda *shape: jax.ShapeDtypeStruct(shape, jnp.bfloat16)
    f32 = lambda *shape: jax.ShapeDtypeStruct(shape, jnp.float32)
    sem = lambda *shape: [pltpu.SemaphoreType.DMA(shape)] * 2
    return pl.pallas_call(
        functools.partial(info_kernel, groups, n, sizes),
        out_shape=(
            jax.ShapeDtypeStruct((8, 128), jnp.int32),
            jax.ShapeDtypeStruct((1, 1), jnp.int32),
            bf16(LANES, CHUNKS, NST, CC),
            bf16(EARLY, LANES, NST, CC),
            bf16(LANES, TAIL_ROWS, TC),
            f32(rows, HEADS), f32(HEADS, rows), f32(HEADS, rows), f32(rows, HEADS), f32(rows, HEADS), f32(8, HEADS),
        ),
        in_specs=[smem] * 4 + [hbm] + [vmem] * 4,
        out_specs=(vmem, vmem, hbm, hbm, hbm) + (vmem,) * 6,
        scratch_shapes=[
            pltpu.VMEM(cache_states.shape, jnp.bfloat16),
            pltpu.VMEM((LANES, CHUNKS, NST, CC), jnp.bfloat16),
            pltpu.VMEM((LANES, TAIL_ROWS, TC), jnp.bfloat16),
            pltpu.VMEM((LANES, TAIL_ROWS, TC), jnp.float32),
            pltpu.VMEM((1, 128), jnp.int32),
            pltpu.VMEM((n, 1, 128), jnp.int32),
            pltpu.SemaphoreType.DMA((cache_states.shape[0],)),
            pltpu.SemaphoreType.DMA, pltpu.SemaphoreType.DMA,
            *sem(EARLY, LANES - 1), *sem(LANES - 1),
            pltpu.SemaphoreType.DMA((LANES * (CHUNKS - EARLY) + EARLY + 1,)),
            pltpu.VMEM((groups, 1, 128), jnp.int32), *sem(groups),
        ],
        compiler_params=pltpu.CompilerParams(collective_id=0, has_side_effects=True, vmem_limit_bytes=58 * 2**20),
        name="info",
    )(hit_owner, hit_slot, hit_spans, request_of, cache_states, cache_tails, dt_raw, dt_bias, a_log)


def conv(taps, bias, pad, rows):
    v = jnp.broadcast_to(bias, (rows, bias.shape[1]))
    for k in range(4):
        v = v + taps[k : k + 1, :] * pad[5 + k : 5 + k + rows, :]
    return (v / (1.0 + jnp.exp(-v))).astype(jnp.bfloat16)


def route_kernel(
    n, slots, tab, own, plane_in, plane_t_in,
    cum_ref, cumt_ref, stept_ref, coef_ref, ecum_ref, elast_ref, xbc_ref, weight_ref, bias_ref, skip_ref,
    y_out, final_out,
    start, tail_out, xs, pad, head_pad, tail_rows, scores_ref, y_local, fresh, y_stage, f_stage, y_sem, f_sem,
    skips, plane, plane_t, up_recv, up_recv_t, down_recv, down_recv_t,
    up_send, up_send_t, down_send, down_send_t, fin_send, fin_send_t,
    load_sem, spread_s, spread_r, up_s, up_r, up_ts, up_tr,
    down_s, down_r, down_ts, down_tr, fin_s, fin_r, fin_ts, fin_tr,
):
    planes = n // LANES
    steps = CHUNKS * slots
    grp, me = lax.axis_index("grp"), lax.axis_index("req")
    z, l = lax.div(me, LANES), lax.rem(me, LANES)
    first, last = z == 0, z == planes - 1

    def mate(k):
        return z * LANES + lax.rem(l + k, LANES)

    loads = [
        pltpu.make_async_copy(plane_t_in, plane_t, load_sem.at[0]),
        pltpu.make_async_copy(plane_in, plane.at[pl.ds(0, EARLY)], load_sem.at[1]),
    ]
    for c in range(EARLY, CHUNKS):
        loads.append(pltpu.make_async_copy(own.at[l, c], plane.at[c, l], load_sem.at[2 + c - EARLY]))
    for load in loads:
        load.start()
    barrier = pltpu.get_barrier_semaphore()
    for k in range(1, LANES):
        pl.semaphore_signal(barrier, inc=1, device_id=(grp, mate(k)), device_id_type=MESH)

    @pl.when(jnp.logical_not(first))
    def _():
        pl.semaphore_signal(barrier, inc=1, device_id=(grp, me - LANES), device_id_type=MESH)

    @pl.when(jnp.logical_not(last))
    def _():
        pl.semaphore_signal(barrier, inc=1, device_id=(grp, me + LANES), device_id_type=MESH)

    pl.semaphore_wait(barrier, LANES - 1 + jnp.where(first | last, 1, 2))

    def remote(src, dst, ss, rs, to):
        return pltpu.make_async_remote_copy(
            src_ref=src, dst_ref=dst, send_sem=ss, recv_sem=rs, device_id=(grp, to), device_id_type=MESH
        )

    def spread(c, k):
        to = lax.rem(l + k, LANES)
        return remote(own.at[to, c], plane.at[c, l], spread_s.at[c, k - 1], spread_r.at[c, k - 1], mate(k))

    def spread_from(c, k):
        frm = lax.rem(l + LANES - k, LANES)
        return remote(own.at[frm, c], plane.at[c, frm], spread_s.at[c, k - 1], spread_r.at[c, k - 1], mate(k))

    def up(s):
        return remote(up_send.at[s], up_recv.at[s], up_s.at[s], up_r.at[s], me + LANES)

    def up_tail(s):
        return remote(up_send_t.at[s], up_recv_t.at[s], up_ts.at[s], up_tr.at[s], me + LANES)

    def down(s):
        return remote(down_send.at[s], down_recv.at[s], down_s.at[s], down_r.at[s], me - LANES)

    def down_tail(s):
        return remote(down_send_t.at[s], down_recv_t.at[s], down_ts.at[s], down_tr.at[s], me - LANES)

    def fin(c, k):
        to = lax.rem(l + k, LANES)
        return remote(fin_send.at[c, k - 1], start.at[l, c], fin_s.at[c, k - 1], fin_r.at[c, k - 1], mate(k))

    def fin_from(c, k):
        frm = lax.rem(l + LANES - k, LANES)
        return remote(fin_send.at[c, k - 1], start.at[frm, c], fin_s.at[c, k - 1], fin_r.at[c, k - 1], mate(k))

    def fin_tail(k):
        return remote(fin_send_t.at[k - 1], tail_out.at[l], fin_ts.at[k - 1], fin_tr.at[k - 1], mate(k))

    def fin_tail_from(k):
        frm = lax.rem(l + LANES - k, LANES)
        return remote(fin_send_t.at[k - 1], tail_out.at[frm], fin_ts.at[k - 1], fin_tr.at[k - 1], mate(k))

    for c in range(EARLY, min(EARLY + AHEAD, CHUNKS)):
        for k in range(1, LANES):
            spread(c, k).start()
    rows = xbc_ref.shape[0]
    channels = xbc_ref.shape[1]
    pieces = channels // PW
    scans = INNER // PW
    first_b, first_c = INNER, INNER + GROUPS * NST
    low = lax.broadcasted_iota(jnp.int32, (rows, 128), 1) < HEAD_DIM
    low_n = lax.broadcasted_iota(jnp.int32, (NST, 128), 1) < HEAD_DIM

    def columns(i):
        return pl.ds(pl.multiple_of(i * PW, PW), PW)

    def conv_piece(i):
        at = columns(i)
        pad[0:8, :] = jnp.zeros((8, PW), jnp.float32)
        pad[8 : 8 + rows, :] = xbc_ref[:, at].astype(jnp.float32)
        xs[:, at] = conv(weight_ref[:, at], bias_ref[:, at], pad, rows)

    def head_piece(i, _):
        at = columns(i)
        head_pad[0:8, :] = tail_rows[:, at]
        head_pad[8:24, :] = xbc_ref[0:16, at].astype(jnp.float32)
        xs[0:16, at] = conv(weight_ref[:, at], bias_ref[:, at], head_pad, 16)
        return 0

    def with_tail():
        tail_rows[...] = jnp.zeros_like(tail_rows)
        for p in range(LANES):
            got = tail_out[p].astype(jnp.float32)
            for q in range(-(-channels // WIDE)):
                at = q * WIDE + p * TC
                if at < channels:
                    tail_rows[5:8, at : at + TC] = got[3 * q : 3 * q + 3, :]
        lax.fori_loop(scans, pieces, head_piece, 0)

    def score(g):
        causal = lax.broadcasted_iota(jnp.int32, (rows, rows), 0) >= lax.broadcasted_iota(jnp.int32, (rows, rows), 1)
        b = xs[:, pl.ds(pl.multiple_of(first_b + g * NST, NST), NST)]
        c = xs[:, pl.ds(pl.multiple_of(first_c + g * NST, NST), NST)]
        scores = lax.dot_general(c, b, (((1,), (1,)), ((), ())), preferred_element_type=jnp.float32)
        scores_ref[g] = jnp.where(causal, scores, 0.0)

    def turned(ref, head):
        return pltpu.roll(ref[...], lax.rem(128 - head, 128), axis=1)

    def scan_piece(p, c):
        i = p * (scans // LANES) + c
        heads = PW // HEAD_DIM
        at = columns(i)
        x = xs[:, at]
        scores = scores_ref[p]
        cum, coef, skip = turned(cum_ref, heads * i), turned(coef_ref, heads * i), turned(skips, heads * i)
        here = pl.ds(pl.multiple_of(i * heads, heads), heads)
        cumt, stept = cumt_ref[here, :], stept_ref[here, :]
        zero = jnp.zeros((rows, 128), jnp.bfloat16)
        ys, carried = [], []
        for j in range(0, heads, 2):
            xp = x[:, j * HEAD_DIM : (j + 2) * HEAD_DIM]
            mixes = []
            for h in (j, j + 1):
                decay = jnp.exp(jnp.minimum(cum[:, h : h + 1] - cumt[h : h + 1, :], 0.0))
                mixes.append((scores * decay * stept[h : h + 1, :]).astype(jnp.bfloat16))
            mix = jnp.concatenate(mixes, axis=1)
            both = jnp.concatenate([jnp.where(low, xp, zero), jnp.where(low, zero, xp)], axis=0)
            xf = xp.astype(jnp.float32)
            d = jnp.where(low[0:1], skip[0:1, j : j + 1], skip[0:1, j + 1 : j + 2])
            ys.append(jnp.dot(mix, both, preferred_element_type=jnp.float32) + d * xf)
            carried.append((jnp.where(low, coef[:, j : j + 1], coef[:, j + 1 : j + 2]) * xf).astype(jnp.bfloat16))
        per = CC // 128
        for u in range(PW // CC):
            y_local[i * (PW // CC) + u] = jnp.concatenate(ys[u * per : (u + 1) * per], axis=1)
        b = xs[:, pl.ds(pl.multiple_of(first_b + p * NST, NST), NST)]
        new = lax.dot_general(
            b, jnp.concatenate(carried, axis=1), (((0,), (0,)), ((), ())), preferred_element_type=jnp.float32
        )
        for u in range(PW // CC):
            fresh[i * (PW // CC) + u] = new[:, u * CC : (u + 1) * CC]

    def outputs(i):
        at = pl.ds(pl.multiple_of(i * CC, CC), CC)
        return (
            pltpu.make_async_copy(y_stage.at[i], y_out.at[:, at], y_sem.at[i]),
            pltpu.make_async_copy(f_stage.at[i], final_out.at[0, :, at], f_sem.at[i]),
        )

    def last_piece(p, c):
        i = p * CHUNKS + c
        held = start[p, c]
        ys = jnp.dot(xs[:, pl.ds(pl.multiple_of(first_c + p * NST, NST), NST)], held,
                     preferred_element_type=jnp.float32)
        heads = CC // HEAD_DIM
        ecum, elast = turned(ecum_ref, heads * i), turned(elast_ref, heads * i)
        for j in range(0, heads, 2):
            sl = slice(j * HEAD_DIM, (j + 2) * HEAD_DIM)
            factor = jnp.where(low, ecum[:, j : j + 1], ecum[:, j + 1 : j + 2])
            y_stage[i, :, sl] = (y_local[i, :, sl] + factor * ys[:, sl]).astype(jnp.bfloat16)
            kept = jnp.where(low_n[0:1], elast[0:1, j : j + 1], elast[0:1, j + 1 : j + 2])
            f_stage[i, :, sl] = (kept * held[:, sl].astype(jnp.float32) + fresh[i, :, sl]).astype(jnp.bfloat16)
        for copy in outputs(i):
            copy.start()

    def last_chunk(c):
        for k in range(1, LANES):
            fin_from(c, k).wait_recv()

        def one(p, _):
            last_piece(p, c)
            return 0

        lax.fori_loop(0, LANES, one, 0)

    ready = slots + LAG * (planes - 1)
    total = steps + LAG * (planes - 1)
    per_conv = -(-pieces // ready)
    after = ready + 3
    per_scan = -(-scans // (total - after))

    lead = after - ready - 1 + -(-LANES // per_scan)

    def compute(t):
        @pl.when(t < ready)
        def _():
            def one(u, _):
                i = t * per_conv + u

                @pl.when(i < pieces)
                def _():
                    conv_piece(i)

                return 0

            lax.fori_loop(0, per_conv, one, 0)

        @pl.when(t == ready)
        def _():
            for k in range(1, LANES):
                fin_tail_from(k).wait_recv()
            with_tail()

        part = t - ready - 1

        @pl.when((part >= 0) & (part < GROUPS))
        def _():
            score(part)
            lax.fori_loop(part * (scans // GROUPS), (part + 1) * (scans // GROUPS), head_piece, 0)

        @pl.when(t >= after)
        def _():
            def one(u, _):
                i = (t - after) * per_scan + u

                @pl.when(i < scans)
                def _():
                    scan_piece(lax.rem(i, LANES), lax.div(i, LANES))

                return 0

            lax.fori_loop(0, per_scan, one, 0)
            since = t - ready - lead

            @pl.when((since >= 0) & (lax.rem(jnp.maximum(since, 0), slots) == 0))
            def _():
                last_chunk(lax.div(since, slots))

    def fill(dst, at, sel, near, c, far, base, j, inner):
        value = near[c, 0]
        for p in range(1, LANES):
            value = lax.select_n(sel == p, value, near[c, p])
        dst[at] = value

        @pl.when(inner)
        def _():
            def one(i, _):
                dst[at] = lax.select_n(sel == LANES + i, dst[at], far[base + i])
                return 0

            lax.fori_loop(0, j + 1, one, 0)

    def fill_tail(dst, j, sel, far, inner):
        value = plane_t[0]
        for p in range(1, LANES):
            value = lax.select_n(sel == p, value, plane_t[p])
        dst[j] = value

        @pl.when(inner)
        def _():
            def one(i, _):
                dst[j] = lax.select_n(sel == LANES + i, dst[j], far[i])
                return 0

            lax.fori_loop(0, j + 1, one, 0)

    def tick(t, _):
        tp = t - LAG * jnp.minimum(z, planes - 1 - z)

        @pl.when((tp >= 0) & (tp < steps) & (lax.rem(jnp.maximum(tp, 0), slots) == 0))
        def _():
            c = lax.div(tp, slots)

            @pl.when(c >= EARLY)
            def _():
                for k in range(1, LANES):
                    spread_from(c, k).wait_recv()

        more = EARLY + AHEAD + lax.div(t, PACE)

        @pl.when((more < CHUNKS) & (lax.rem(t, PACE) == 0))
        def _():
            for k in range(1, LANES):
                spread(more, k).start()

        def along(s, row, edge_in, edge_out, copy, copy_tail, send, send_t, recv, recv_t):
            @pl.when((s >= 0) & (s < steps))
            def _():
                c, j = lax.div(s, slots), lax.rem(s, slots)
                inner = jnp.logical_not(edge_in)

                @pl.when(inner)
                def _():
                    @pl.when(c == 0)
                    def _():
                        copy_tail(j).wait_recv()

                    copy(s).wait_recv()

                @pl.when(jnp.logical_not(edge_out))
                def _():
                    sel = tab[row, j]

                    @pl.when(c == 0)
                    def _():
                        fill_tail(send_t, j, sel, recv_t, inner)
                        copy_tail(j).start()

                    fill(send, s, sel, plane, c, recv, c * slots, j, inner)

                    @pl.when(s >= DEPTH)
                    def _():
                        copy(s - DEPTH).wait_send()

                    copy(s).start()

        along(t - LAG * z, 0, first, last, up, up_tail, up_send, up_send_t, up_recv, up_recv_t)
        along(t - LAG * (planes - 1 - z), 1, last, first, down, down_tail, down_send, down_send_t, down_recv, down_recv_t)

        tf = t - LAG * jnp.maximum(z, planes - 1 - z)

        @pl.when((tf >= 0) & (tf < steps) & (lax.rem(jnp.maximum(tf, 0), slots) == slots - 1))
        def _():
            c = lax.div(tf, slots)
            sels = [tab[2, mate(k)] for k in range(LANES)]

            def choose(near, far_up, far_down, write, read):
                acc = [jnp.zeros(near(0).shape, jnp.bfloat16)] * LANES
                for p in range(LANES):
                    value = near(p)
                    acc = [lax.select_n(sel == p, a, value) for sel, a in zip(sels, acc)]
                for k in range(LANES):
                    write(k, acc[k])

                def far(get, base):
                    acc = [read(k) for k in range(LANES)]
                    for i in range(slots):
                        value = get(i)
                        acc = [lax.select_n(sel == base + i, a, value) for sel, a in zip(sels, acc)]
                    for k in range(LANES):
                        write(k, acc[k])

                @pl.when(jnp.logical_not(first))
                def _():
                    far(far_up, LANES)

                @pl.when(jnp.logical_not(last))
                def _():
                    far(far_down, LANES + n)

            def rows_of(b, _):
                at = pl.ds(pl.multiple_of(b * 16, 16), 16)

                def write(k, v):
                    if k == 0:
                        start[l, c, at] = v
                    else:
                        fin_send[c, k - 1, at] = v

                def read(k):
                    return start[l, c, at] if k == 0 else fin_send[c, k - 1, at]

                choose(lambda p: plane[c, p, at], lambda i: up_recv[c * slots + i, at],
                       lambda i: down_recv[c * slots + i, at], write, read)
                return 0

            lax.fori_loop(0, NST // 16, rows_of, 0)
            for k in (2, 1, 3):
                fin(c, k).start()

            @pl.when(c == 0)
            def _():
                def write(k, v):
                    if k == 0:
                        tail_out[l] = v
                    else:
                        fin_send_t[k - 1] = v

                def read(k):
                    return tail_out[l] if k == 0 else fin_send_t[k - 1]

                choose(lambda p: plane_t[p], lambda i: up_recv_t[i], lambda i: down_recv_t[i], write, read)
                for k in range(1, LANES):
                    fin_tail(k).start()

        compute(t)
        return 0

    skips[...] = jnp.broadcast_to(skip_ref[...], skips.shape)
    for load in loads:
        load.wait()
    lax.fori_loop(0, total, tick, 0)
    for c in range((total - 1 - ready - lead) // slots + 1, CHUNKS):
        last_chunk(c)

    for k in range(1, LANES):
        fin_tail(k).wait_send()
        for c in range(CHUNKS):
            if c >= EARLY:
                spread(c, k).wait_send()
            fin(c, k).wait_send()

    @pl.when(jnp.logical_not(last))
    def _():
        for j in range(slots):
            up_tail(j).wait_send()
        for s in range(max(steps - DEPTH, 0), steps):
            up(s).wait_send()

    @pl.when(jnp.logical_not(first))
    def _():
        for j in range(slots):
            down_tail(j).wait_send()
        for s in range(max(steps - DEPTH, 0), steps):
            down(s).wait_send()

    for i in range(LANES * CHUNKS):
        for copy in outputs(i):
            copy.wait()


def route(n, slots, number, table, own, plane, plane_t, terms, xbc, weight, bias, skip):
    steps = CHUNKS * slots
    rows, channels = xbc.shape
    pieces = LANES * CHUNKS
    f32 = lambda *shape: pltpu.VMEM(shape, jnp.float32)
    big = lambda *lead: pltpu.VMEM(lead + (NST, CC), jnp.bfloat16)
    small = lambda *lead: pltpu.VMEM(lead + (TAIL_ROWS, TC), jnp.bfloat16)
    sem = lambda *shape: [pltpu.SemaphoreType.DMA(shape)] * 2
    vmem = pl.BlockSpec(memory_space=pltpu.VMEM)
    hbm = pl.BlockSpec(memory_space=pl.ANY)
    return pl.pallas_call(
        functools.partial(route_kernel, n, slots),
        out_shape=(
            jax.ShapeDtypeStruct((rows, INNER), jnp.bfloat16),
            jax.ShapeDtypeStruct((1, NST, INNER), jnp.bfloat16),
        ),
        in_specs=[pl.BlockSpec(memory_space=pltpu.SMEM)] + [hbm] * 3 + [vmem] * 10,
        out_specs=(hbm, hbm),
        scratch_shapes=[
            big(LANES, CHUNKS), small(LANES),
            pltpu.VMEM((rows, channels), jnp.bfloat16), f32(8 + rows, PW), f32(24, PW), f32(8, channels),
            f32(GROUPS, rows, rows), f32(pieces, rows, CC), f32(pieces, NST, CC),
            pltpu.VMEM((pieces, rows, CC), jnp.bfloat16), big(pieces), *sem(pieces),
            f32(8, HEADS), big(CHUNKS, LANES), small(LANES),
            big(steps), small(slots), big(steps), small(slots),
            big(steps), small(slots), big(steps), small(slots),
            big(CHUNKS, LANES - 1), small(LANES - 1),
            pltpu.SemaphoreType.DMA((2 + CHUNKS - EARLY,)),
            *sem(CHUNKS, LANES - 1),
            *sem(steps), *sem(slots), *sem(steps), *sem(slots),
            *sem(CHUNKS, LANES - 1), *sem(LANES - 1),
        ],
        compiler_params=pltpu.CompilerParams(
            collective_id=number, has_side_effects=True, vmem_limit_bytes=(34 + 2 * slots) * 2**20
        ),
        name=f"route{slots}",
    )(table, own, plane, plane_t, *terms, xbc, weight, bias, skip)


def settle_kernel(y_ref, f_ref, y_out, f_out, y_held, f_held, in_sem, out_sem):
    pieces = []
    for i in range(SETTLE):
        at = pl.ds(i * (y_ref.shape[0] // SETTLE), y_ref.shape[0] // SETTLE)
        pieces.append((y_ref.at[at], y_held.at[at], y_out.at[at]))
        at = pl.ds(i * (NST // SETTLE), NST // SETTLE)
        pieces.append((f_ref.at[0, at], f_held.at[at], f_out.at[0, at]))
    come = [pltpu.make_async_copy(a, b, in_sem.at[i]) for i, (a, b, _) in enumerate(pieces)]
    go = [pltpu.make_async_copy(b, c, out_sem.at[i]) for i, (_, b, c) in enumerate(pieces)]
    for copy in come:
        copy.start()
    for first, second in zip(come, go):
        first.wait()
        second.start()
    for copy in go:
        copy.wait()


def settle(y, final):
    hbm = pl.BlockSpec(memory_space=pl.ANY)
    return pl.pallas_call(
        settle_kernel,
        out_shape=(jax.ShapeDtypeStruct(y.shape, y.dtype), jax.ShapeDtypeStruct(final.shape, final.dtype)),
        in_specs=[hbm, hbm],
        out_specs=(hbm, hbm),
        scratch_shapes=[
            pltpu.VMEM(y.shape, y.dtype), pltpu.VMEM(final.shape[1:], final.dtype),
            pltpu.SemaphoreType.DMA((2 * SETTLE,)), pltpu.SemaphoreType.DMA((2 * SETTLE,)),
        ],
        compiler_params=pltpu.CompilerParams(vmem_limit_bytes=SETTLE_LIMIT),
        name="settle",
    )(y, final)


def local_routed(
    mesh, xbc, dt_raw, conv_weight, conv_bias, dt_bias, a_log, d_skip, cache_states, cache_tails,
    hit_owner, hit_slot, hit_spans, request_of,
):
    n = mesh.shape["req"]
    sizes = [3, 4, 5, n // 2]
    table, which, own, plane, plane_t, *terms = info(
        mesh, sizes, hit_owner, hit_slot, hit_spans, request_of, cache_states, cache_tails,
        dt_raw, dt_bias[None], a_log[None],
    )
    return settle(*lax.switch(
        which[0, 0],
        [functools.partial(route, n, size, 1 + i) for i, size in enumerate(sizes)],
        table, own, plane, plane_t, terms, xbc, conv_weight, conv_bias[None], d_skip[None],
    ))


def local(
    xbc, dt_raw, conv_weight, conv_bias, dt_bias, a_log, d_skip, cache_states, cache_tails,
    hit_owner, hit_slot, hit_spans, request_of,
):
    count = hit_owner.shape[0]
    rows = xbc.shape[0]
    mine = request_of[0]
    live = (hit_spans[mine] > 0).astype(jnp.int32)
    device = lax.axis_index("req")
    served = jnp.max(jnp.where(hit_owner == device, hit_slot, 0))
    send = lax.dynamic_slice_in_dim(cache_states, served, 1, 0).reshape(count, NST // count, INNER)
    number = jnp.broadcast_to(mine.astype(send.dtype), send.shape[:2] + (128,))
    parts = lax.all_to_all(
        jnp.concatenate([send, number], axis=2), "req", split_axis=0, concat_axis=0, tiled=True
    )
    every_request = parts[:, 0, INNER].astype(jnp.int32)
    own_tail = lax.dynamic_slice_in_dim(cache_tails, served, 1, 0)
    own_tail = jnp.pad(own_tail, ((0, 0), (0, 1), (0, 0)))
    every_tail = lax.all_gather(own_tail, "req", axis=0, tiled=True)[:, :3]
    owners = jnp.sum(
        jnp.where(every_request[:, None] == jnp.arange(count)[None, :], hit_owner[None, :], 0), axis=1
    )
    chosen = pick(parts, owners)
    start = lax.all_to_all(chosen, "req", split_axis=0, concat_axis=0, tiled=True).reshape(NST, INNER)

    tail = lax.dynamic_index_in_dim(every_tail, hit_owner[mine], 0, keepdims=False)
    tail = jnp.where(live > 0, tail, jnp.zeros_like(tail)).astype(jnp.float32)
    tail = jnp.pad(tail, ((5, 0), (0, 0)))
    step = jax.nn.softplus(dt_raw + dt_bias[None, :])
    below = jnp.tril(jnp.ones((rows, rows), jnp.float32))
    cum = jnp.dot(below, step * (-jnp.exp(a_log))[None, :], precision=lax.Precision.HIGHEST)
    last = cum[rows - 1]
    coef = jnp.exp(last[None, :] - cum) * step
    skip = jnp.repeat(d_skip, HEAD_DIM)[None, :]
    elast = jnp.repeat(jnp.exp(last), HEAD_DIM)[None, :]
    cumt = cum.T.reshape(STEPS, PER_STEP, rows)
    stept = step.T.reshape(STEPS, PER_STEP, rows)
    bias = conv_bias[None, :]

    first_b, first_c = INNER // NST, INNER // NST + GROUPS
    per = STEPS_PER_GROUP
    triple = lambda r: [
        pl.BlockSpec((r, COLS), lambda i: (0, i)),
        pl.BlockSpec((r, NST), lambda i: (0, first_b + i // per)),
        pl.BlockSpec((r, NST), lambda i: (0, first_c + i // per)),
    ]
    wide = lambda r: pl.BlockSpec((r, COLS), lambda i: (0, i))
    tall = pl.BlockSpec((1, rows, PER_STEP), lambda i: (i, 0, 0))
    flat = pl.BlockSpec((1, PER_STEP, rows), lambda i: (i, 0, 0))
    group = pl.BlockSpec((rows, NST), lambda i: (0, i // per))
    y_local, fresh, c_part = pl.pallas_call(
        local_kernel,
        grid=(STEPS,),
        out_shape=(
            jax.ShapeDtypeStruct((rows, INNER), jnp.float32),
            jax.ShapeDtypeStruct((NST, INNER), jnp.float32),
            jax.ShapeDtypeStruct((rows, GROUPS * NST), jnp.bfloat16),
        ),
        in_specs=triple(rows) + triple(8) + triple(4) + triple(1) + [tall, flat, flat, tall, wide(1)],
        out_specs=(wide(rows), wide(NST), group),
        scratch_shapes=[pltpu.VMEM((8 + rows, COLS), jnp.float32)],
        compiler_params=pltpu.CompilerParams(vmem_limit_bytes=58 * 2**20),
        cost_estimate=pl.CostEstimate(flops=10**9, bytes_accessed=40 * 10**6, transcendentals=4 * 10**6),
        name="local",
    )(xbc, xbc, xbc, tail, tail, tail, conv_weight, conv_weight, conv_weight, bias, bias, bias,
      by_step(cum), cumt, stept, by_step(coef), skip)

    return pl.pallas_call(
        state_kernel,
        grid=(STEPS,),
        out_shape=(
            jax.ShapeDtypeStruct((rows, INNER), jnp.bfloat16),
            jax.ShapeDtypeStruct((1, NST, INNER), jnp.bfloat16),
        ),
        in_specs=[pl.BlockSpec(memory_space=pltpu.SMEM), wide(NST), wide(rows), wide(NST), group, tall, wide(1)],
        out_specs=(wide(rows), pl.BlockSpec((1, NST, COLS), lambda i: (0, 0, i))),
        compiler_params=pltpu.CompilerParams(vmem_limit_bytes=58 * 2**20),
        name="state",
    )(live[None], start, y_local, fresh, c_part, by_step(jnp.exp(cum)), elast)


def solution(mesh):
    rows = P(("grp", "req"), None)
    slots = P(("grp", "req"), None, None)
    in_specs = (
        rows, rows, P(), P(), P(), P(), P(), slots, slots, P("grp"), P("grp"), P("grp"), P(("grp", "req")),
    )
    body = functools.partial(local_routed, mesh) if mesh.shape["req"] == 16 else local
    return jax.shard_map(body, mesh=mesh, in_specs=in_specs, out_specs=(rows, slots), check_vma=False)
```
